32 devices in a mesh: tm: 2 (over x), ulysses: 4 (over z), dp: 4 (over y, core).
Axes of the slice: x: 2, y: 2, z: 4, core: 2. Of those that a mesh axis runs over, the one named last changes fastest.
Arguments:
- queries: bfloat16 [4, 1536, 1536], P('dp', ('tm', 'ulysses')), may hold values from -16 to 16
- keys: bfloat16 [4, 1536, 1536], P('dp', ('tm', 'ulysses')), may hold values from -16 to 16
- values: bfloat16 [4, 1536, 1536], P('dp', ('tm', 'ulysses')), may hold values from -6 to 6
- attn_out: bfloat16 [4, 1536, 1536], P('dp', ('tm', 'ulysses')), may hold values from -4 to 4
- out_grad: bfloat16 [4, 1536, 1536], P('dp', ('tm', 'ulysses')), may hold values from -6 to 6
- out_gain: float32 [1536], replicated, may hold values from 0.5 to 2
Outputs:
- query_grad: bfloat16 [4, 1536, 1536], P('dp', ('tm', 'ulysses'))
- key_grad: bfloat16 [4, 1536, 1536], P('dp', ('tm', 'ulysses'))
- value_grad: bfloat16 [4, 1536, 1536], P('dp', ('tm', 'ulysses'))
- gain_grad: float32 [1536], replicated
The draws below stay inside these ranges and needn't reach their ends.
All inputs are finite; a program needn't handle non-finite values.
Results may differ from the reference program's by a relative error of at most 0.0058.
Values may be sent and summed in bfloat16 or wider, within the bound.
No kernel may reach another device: no remote copies, remote signals or barrier semaphores. Data moves between devices by JAX's collectives and lax.ppermute only.
A program may use at most 128 MiB of HBM per device.

```python
import math
import jax
import jax.numpy as jnp
from jax import lax

HEADS = 12
HD = 128
TILE = 384
SLAB = 768
TOKENS = 1536
CLIPS = 4


def drawn_rows(key):
    key = jax.random.fold_in(key, 101)
    second = jax.random.fold_in(key, 1)
    anchor = jax.random.uniform(second, (CLIPS, TOKENS, HEADS * HD), jnp.float32, -4.0, 4.0)
    return anchor


def draw_queries(key, part):
    anchor = drawn_rows(key)
    key = jax.random.fold_in(key, 1)
    result = jnp.clip(jax.random.normal(key, anchor.shape, jnp.float32), -6.0, 6.0)
    return result.astype(jnp.bfloat16)


def draw_keys(key, part):
    anchor = drawn_rows(key)
    key = jax.random.fold_in(key, 2)
    result = jnp.clip(jax.random.normal(key, anchor.shape, jnp.float32), -6.0, 6.0)
    return result.astype(jnp.bfloat16)


def grad_rows(key):
    key = jax.random.fold_in(key, 202)
    first = jax.random.fold_in(key, 0)
    shape = (CLIPS, TOKENS, HEADS * HD)
    drawn = jnp.clip(jax.random.normal(first, shape, jnp.float32), -6.0, 6.0)
    return drawn


def draw_out_grad(key, part):
    result = grad_rows(key)
    return result.astype(jnp.bfloat16)


def draw_attn_out(key, part):
    shared_key = key
    key = jax.random.fold_in(key, 4)
    shape = (CLIPS, TOKENS, HEADS * HD)
    noise = jnp.clip(jax.random.normal(key, shape, jnp.float32), -6.0, 6.0)
    carried = grad_rows(shared_key)
    slab_index = (jnp.arange(TOKENS, dtype=jnp.int32) // SLAB).astype(jnp.float32)
    ramp = 0.05 + 0.1 * slab_index / max(TOKENS // SLAB - 1, 1)
    return (0.4 * noise + ramp[None, :, None] * carried).astype(jnp.bfloat16)


def shard_levels(rng, extent, shards, least, largest):
    def one(position, blocks):
        draws = jax.random.uniform(jax.random.fold_in(jax.random.fold_in(rng, 6), position), (blocks,), jnp.float32, least / len(shards), largest / len(shards))
        return jnp.repeat(jnp.exp(draws), extent[position] // blocks).reshape((-1,) + (1,) * (len(extent) - position - 1))

    gain = one(*shards[0])
    for cut in shards[1:]:
        gain = gain * one(*cut)
    return gain


def gaussian(rng, extent, scale, most, cuts=(), kind=jnp.bfloat16):
    values = scale * jax.random.normal(rng, extent, jnp.float32)
    if cuts:
        values = values * shard_levels(rng, extent, cuts, -0.22, 0.18)
    return jnp.clip(values, -most, most).astype(kind)


def setup_inputs(seed: int = 0) -> dict:
    streams_of = jax.random.split(jax.random.key(seed), 7)
    queries = draw_queries(jax.random.fold_in(streams_of[6], 71), 0)
    keys = draw_keys(jax.random.fold_in(streams_of[6], 71), 0)
    values = gaussian(streams_of[2], (CLIPS, TOKENS, HEADS * HD), 1.0, 6.0, ((0, 4), (1, 8)))
    attn_out = draw_attn_out(jax.random.fold_in(streams_of[6], 71), 0)
    out_grad = draw_out_grad(jax.random.fold_in(streams_of[6], 71), 0)
    out_gain = jnp.clip(jnp.exp(jax.random.uniform(streams_of[5], (HEADS * HD,), jnp.float32, math.log(0.5), math.log(2.0))), 0.5, 2.0)
    return {"queries": queries, "keys": keys, "values": values, "attn_out": attn_out, "out_grad": out_grad, "out_gain": out_gain}


def window_grads(query_slab, grad_slab, dots_slab, key_window, value_window, keep_mask):
    inv_root = 1.0 / (HD ** 0.5)
    scores = jnp.einsum("qhd,khd->hqk", query_slab.astype(jnp.float32), key_window.astype(jnp.float32)) * inv_root
    scores = jnp.where(keep_mask[None], scores, -jnp.inf)
    row_max = jnp.max(scores, axis=2, keepdims=True)
    sum_exp = jnp.sum(jnp.exp(scores - row_max), axis=2, keepdims=True)
    log_total = row_max + jnp.log(sum_exp)
    weights = jnp.exp(scores - log_total)
    grad_weights = jnp.einsum("qhd,khd->hqk", grad_slab.astype(jnp.float32), value_window.astype(jnp.float32))
    grad_scores = (weights * (grad_weights - jnp.transpose(dots_slab)[:, :, None]) * inv_root).astype(jnp.bfloat16)
    grad_scores = lax.optimization_barrier(grad_scores).astype(jnp.float32)
    weights_low = lax.optimization_barrier(weights.astype(jnp.bfloat16)).astype(jnp.float32)
    grad_query = jnp.einsum("hqk,khd->qhd", grad_scores, key_window.astype(jnp.float32))
    grad_key = jnp.einsum("hqk,qhd->khd", grad_scores, query_slab.astype(jnp.float32))
    grad_value = jnp.einsum("hqk,qhd->khd", weights_low, grad_slab.astype(jnp.float32))
    return grad_query, grad_key, grad_value


def clip_grads(operands):
    queries, keys, values, grad_out, row_dots = operands
    tiles = queries.shape[0]
    pad_zero = jnp.zeros((1,) + keys.shape[1:], keys.dtype)
    key_pad = jnp.concatenate([pad_zero, keys, pad_zero], axis=0)
    value_pad = jnp.concatenate([pad_zero, values, pad_zero], axis=0)
    column = jnp.arange(SLAB, dtype=jnp.int32) // TILE
    near = jnp.abs(column[:, None] - jnp.tile(column, 3)[None, :]) <= 1
    source = jnp.repeat(jnp.arange(3, dtype=jnp.int32), SLAB)

    def advance(carry, index):
        key_acc, value_acc = carry
        key_window = lax.dynamic_slice_in_dim(key_pad, index, 3, 0).reshape(3 * SLAB, HEADS, HD)
        value_window = lax.dynamic_slice_in_dim(value_pad, index, 3, 0).reshape(3 * SLAB, HEADS, HD)
        slab_index = index - 1 + source
        keep_mask = near & ((slab_index >= 0) & (slab_index < tiles))[None, :]
        grad_query, grad_key, grad_value = window_grads(
            lax.dynamic_index_in_dim(queries, index, 0, keepdims=False),
            lax.dynamic_index_in_dim(grad_out, index, 0, keepdims=False),
            lax.dynamic_index_in_dim(row_dots, index, 0, keepdims=False),
            key_window, value_window, keep_mask)
        current = lax.dynamic_slice_in_dim(key_acc, index, 3, 0)
        key_acc = lax.dynamic_update_slice_in_dim(key_acc, current + grad_key.reshape(3, SLAB, HEADS, HD), index, 0)
        current = lax.dynamic_slice_in_dim(value_acc, index, 3, 0)
        value_acc = lax.dynamic_update_slice_in_dim(value_acc, current + grad_value.reshape(3, SLAB, HEADS, HD), index, 0)
        return (key_acc, value_acc), grad_query.astype(jnp.bfloat16)

    start = jnp.zeros((tiles + 2, SLAB, HEADS, HD), jnp.float32)
    (key_acc, value_acc), query_grad = lax.scan(advance, (start, start), jnp.arange(tiles, dtype=jnp.int32))
    return query_grad, key_acc[1:-1].astype(jnp.bfloat16), value_acc[1:-1].astype(jnp.bfloat16)


def reference(queries, keys, values, attn_out, out_grad, out_gain):
    grad_out = (out_grad.astype(jnp.float32) * out_gain).astype(jnp.bfloat16)
    grad_wide = lax.optimization_barrier(grad_out).astype(jnp.float32)
    row_dots = jnp.sum((grad_wide * attn_out.astype(jnp.float32)).reshape(CLIPS, TOKENS, HEADS, HD), axis=3)
    gain_grad = jnp.sum(out_grad.astype(jnp.float32) * attn_out.astype(jnp.float32), axis=(0, 1)) / (CLIPS * TOKENS)
    shape = (CLIPS, TOKENS // SLAB, SLAB, HEADS, HD)
    grads = lax.map(clip_grads, (queries.reshape(shape), keys.reshape(shape), values.reshape(shape),
                                 grad_out.reshape(shape), row_dots.reshape(shape[:4])))
    flat = (CLIPS, TOKENS, HEADS * HD)
    return grads[0].reshape(flat), grads[1].reshape(flat), grads[2].reshape(flat), gain_grad
```

```python
import functools
import math

import jax
import jax.numpy as jnp
from jax import lax
from jax.experimental import pallas as pl
from jax.experimental.pallas import tpu as pltpu
from jax.sharding import PartitionSpec as P

HD = 128
LANES = 128
TILE_ROWS = 16
QUERY_BLOCK = 256
KEY_BLOCK = 256
VMEM_LIMIT = 48 * 1024 * 1024
SCALE = 1.0 / math.sqrt(HD)
SCALE_LOG2 = SCALE / math.log(2.0)


def params():
    return pltpu.CompilerParams(vmem_limit_bytes=VMEM_LIMIT)


def head_columns(head):
    return slice(head * HD, (head + 1) * HD)


def pack_pairs_kernel(first_ref, second_ref, out_ref):
    rows, width = first_ref.shape
    for head in range(width // HD):
        start = 2 * head * rows
        out_ref[0, start : start + rows] = first_ref[:, head_columns(head)]
        out_ref[0, start + rows : start + 2 * rows] = second_ref[:, head_columns(head)]


def pack_pairs(first, second, parts):
    rows, channels = first.shape
    width = channels // parts
    depth = 2 * rows * (width // HD)
    piece = pl.BlockSpec((rows, width), lambda part: (0, part))
    return pl.pallas_call(
        pack_pairs_kernel,
        grid=(parts,),
        in_specs=[piece, piece],
        out_specs=pl.BlockSpec((1, depth, HD), lambda part: (part, 0, 0)),
        out_shape=jax.ShapeDtypeStruct((parts, depth, HD), first.dtype),
        compiler_params=params(),
        cost_estimate=pl.CostEstimate(flops=0, bytes_accessed=8 * rows * channels, transcendentals=0),
    )(first, second)


def dot_groups(rows):
    return -(-rows // LANES)


def dots_rows(rows, heads):
    group = -(-2 * heads // TILE_ROWS) * TILE_ROWS
    return group, group * dot_groups(rows)


def pack_queries_kernel(query_ref, out_grad_ref, attn_ref, gain_ref, out_ref, gain_part_ref):
    rows, width = query_ref.shape
    heads = width // HD
    out_grad = out_grad_ref[...].astype(jnp.float32)
    attn = attn_ref[...].astype(jnp.float32)
    grad = (out_grad * gain_ref[...]).astype(jnp.bfloat16)
    gain_part_ref[...] = jnp.sum(out_grad * attn, axis=0, keepdims=True)
    product = grad.astype(jnp.float32) * attn
    group, _ = dots_rows(rows, heads)
    base = 2 * heads * rows
    dots = []
    for head in range(heads):
        start = 2 * head * rows
        out_ref[0, start : start + rows] = query_ref[:, head_columns(head)]
        out_ref[0, start + rows : start + 2 * rows] = grad[:, head_columns(head)]
        dots.append(jnp.sum(jnp.transpose(product[:, head_columns(head)]), axis=0, keepdims=True))
    for index in range(dot_groups(rows)):
        first, last = index * LANES, min(rows, (index + 1) * LANES)
        terms = []
        for head in range(heads):
            value = dots[head][:, first:last]
            if last - first < LANES:
                value = jnp.concatenate([value, jnp.zeros((1, LANES - last + first), jnp.float32)], axis=1)
            high = value.astype(jnp.bfloat16).astype(jnp.float32)
            terms += [high, value - high]
        terms.append(jnp.zeros((group - 2 * heads, LANES), jnp.float32))
        out_ref[0, base + index * group : base + (index + 1) * group] = jnp.concatenate(terms, axis=0).astype(
            jnp.bfloat16
        )


def pack_queries(queries, out_grad, attn_out, out_gain, parts):
    rows, channels = queries.shape
    width = channels // parts
    heads = width // HD
    depth = 2 * rows * heads + dots_rows(rows, heads)[1]
    piece = pl.BlockSpec((rows, width), lambda part: (0, part))
    line = pl.BlockSpec((1, width), lambda part: (0, part))
    return pl.pallas_call(
        pack_queries_kernel,
        grid=(parts,),
        in_specs=[piece, piece, piece, line],
        out_specs=[pl.BlockSpec((1, depth, HD), lambda part: (part, 0, 0)), line],
        out_shape=[
            jax.ShapeDtypeStruct((parts, depth, HD), jnp.bfloat16),
            jax.ShapeDtypeStruct((1, channels), jnp.float32),
        ],
        compiler_params=params(),
        cost_estimate=pl.CostEstimate(
            flops=8 * rows * channels, bytes_accessed=10 * rows * channels, transcendentals=0
        ),
    )(queries, out_grad, attn_out, out_gain.reshape(1, channels))


def attention_kernel(sources, masked, head, *refs):
    flags_ref = None
    if masked:
        flags_ref, refs = refs[0], refs[1:]
    query_ref, grad_ref, dots_ref = refs[:3]
    key_refs = refs[3 : 3 + 2 * sources : 2]
    value_refs = refs[4 : 4 + 2 * sources : 2]
    outs = refs[3 + 2 * sources :]
    query_grad_ref, own_ref = outs[0], outs[1]
    side_refs = outs[2 : 1 + sources]
    score_ref, key_acc, value_acc = outs[1 + sources :]
    parts, rows, _ = query_ref.shape
    slab = parts * rows
    queries = query_ref[...].reshape(slab, HD)
    grads = grad_ref[...].reshape(slab, HD)
    groups = dot_groups(rows)
    group = dots_ref.shape[1] // groups
    pieces = []
    for part in range(parts):
        for index in range(groups):
            count = min(LANES, rows - index * LANES)
            pair = dots_ref[part, index * group : (index + 1) * group].astype(jnp.float32)
            line = 2 * head
            pieces.append((pair[line : line + 1] + pair[line + 1 : line + 2])[:, :count])
    dots = jnp.concatenate(pieces, axis=1)
    keys = [ref[...].reshape(slab, HD) for ref in key_refs]
    values = [ref[...].reshape(slab, HD) for ref in value_refs]
    blocks = [(source, first) for source in range(sources) for first in range(0, slab, KEY_BLOCK)]
    query_grads = []
    for query_first in range(0, slab, QUERY_BLOCK):
        span = slice(query_first, query_first + QUERY_BLOCK)
        query_block, grad_block = queries[span], grads[span]
        query_flip, grad_flip = jnp.transpose(query_block), jnp.transpose(grad_block)
        dots_block = dots[:, span]
        top = None
        for source, first in blocks:
            scores = jnp.dot(
                keys[source][first : first + KEY_BLOCK], query_flip, preferred_element_type=jnp.float32
            )
            if masked and source > 0:
                scores = jnp.where(flags_ref[source - 1] > 0, scores, -jnp.inf)
            place = source * slab + first
            score_ref[place : place + KEY_BLOCK] = scores
            part_top = jnp.max(scores.reshape(-1, 8, QUERY_BLOCK), axis=0)
            top = part_top if top is None else jnp.maximum(top, part_top)
        top = jnp.max(top, axis=0, keepdims=True) * SCALE_LOG2
        total = None
        for source, first in blocks:
            place = source * slab + first
            powers = jnp.exp2(score_ref[place : place + KEY_BLOCK] * SCALE_LOG2 - top)
            score_ref[place : place + KEY_BLOCK] = powers
            part_total = jnp.sum(powers.reshape(-1, 8, QUERY_BLOCK), axis=0)
            total = part_total if total is None else total + part_total
        inverse = 1.0 / jnp.sum(total, axis=0, keepdims=True)
        query_acc = None
        for source, first in blocks:
            place = source * slab + first
            stretch = slice(first, first + KEY_BLOCK)
            weights = score_ref[place : place + KEY_BLOCK] * inverse
            grad_weights = jnp.dot(values[source][stretch], grad_flip, preferred_element_type=jnp.float32)
            grad_scores = (weights * (grad_weights - dots_block)).astype(jnp.bfloat16)
            value_part = jnp.dot(weights.astype(jnp.bfloat16), grad_block, preferred_element_type=jnp.float32)
            key_part = jnp.dot(grad_scores, query_block, preferred_element_type=jnp.float32)
            query_part = lax.dot_general(
                grad_scores,
                keys[source][stretch],
                (((0,), (0,)), ((), ())),
                preferred_element_type=jnp.float32,
            )
            query_acc = query_part if query_acc is None else query_acc + query_part
            if query_first == 0:
                key_acc[place : place + KEY_BLOCK] = key_part
                value_acc[place : place + KEY_BLOCK] = value_part
            else:
                key_acc[place : place + KEY_BLOCK] += key_part
                value_acc[place : place + KEY_BLOCK] += value_part
        query_grads.append((query_acc * SCALE).astype(jnp.bfloat16))
    query_grad_ref[...] = jnp.concatenate(query_grads, axis=0).reshape(parts, rows, HD)
    for source in range(sources):
        out_ref = own_ref if source == 0 else side_refs[source - 1]
        span = slice(source * slab, (source + 1) * slab)
        out_ref[:, :rows] = (key_acc[span] * SCALE).astype(out_ref.dtype).reshape(parts, rows, HD)
        out_ref[:, rows:] = value_acc[span].astype(out_ref.dtype).reshape(parts, rows, HD)


def attention(head, heads, packed_queries, packed_pairs, flags):
    parts, depth, _ = packed_pairs[0].shape
    sources = len(packed_pairs)
    masked = flags is not None
    packed_depth = packed_queries.shape[1]
    dots_depth = packed_depth - depth
    rows = depth // (2 * heads)
    slab = parts * rows

    def block(index):
        return pl.BlockSpec((parts, rows, HD), lambda step: (0, index, 0))

    in_specs = [block(2 * head), block(2 * head + 1)]
    in_specs.append(pl.BlockSpec((parts, dots_depth, HD), lambda step: (0, depth // dots_depth, 0)))
    operands = [packed_queries, packed_queries, packed_queries]
    for pairs in packed_pairs:
        in_specs += [block(2 * head), block(2 * head + 1)]
        operands += [pairs, pairs]
    if masked:
        in_specs = [pl.BlockSpec(memory_space=pltpu.SMEM)] + in_specs
        operands = [flags] + operands
    whole = pl.BlockSpec((parts, rows, HD), lambda step: (0, 0, 0))
    double = pl.BlockSpec((parts, 2 * rows, HD), lambda step: (0, 0, 0))
    shape = (parts, 2 * rows, HD)
    pairs_of = slab * sources * slab
    return pl.pallas_call(
        functools.partial(attention_kernel, sources, masked, head),
        grid=(1,),
        in_specs=in_specs,
        out_specs=[whole] + [double] * sources,
        out_shape=[
            jax.ShapeDtypeStruct((parts, rows, HD), jnp.bfloat16),
            jax.ShapeDtypeStruct(shape, jnp.float32),
        ]
        + [jax.ShapeDtypeStruct(shape, jnp.bfloat16)] * (sources - 1),
        scratch_shapes=[
            pltpu.VMEM((sources * slab, QUERY_BLOCK), jnp.float32),
            pltpu.VMEM((sources * slab, HD), jnp.float32),
            pltpu.VMEM((sources * slab, HD), jnp.float32),
        ],
        compiler_params=params(),
        cost_estimate=pl.CostEstimate(
            flops=10 * pairs_of * HD, bytes_accessed=slab * HD * 2 * (4 + 6 * sources), transcendentals=pairs_of
        ),
    )(*operands)


def exchange(value):
    return lax.all_to_all(value, "ulysses", split_axis=0, concat_axis=0, tiled=True)


def neighbours(size):
    if size == 1:
        return []
    if size == 2:
        swap = [(0, 1), (1, 0)]
        return [(swap, swap)]
    up = [(index, index + 1) for index in range(size - 1)]
    down = [(index + 1, index) for index in range(size - 1)]
    return [(up, down), (down, up)]


def unpack(received, heads):
    parts, depth, _ = received.shape
    rows = depth // heads
    laid = received.reshape(parts, heads, rows, HD)
    return jnp.transpose(laid, (2, 0, 1, 3)).reshape(1, rows, parts * heads * HD)


def local(queries, keys, values, attn_out, out_grad, out_gain):
    parts = lax.axis_size("ulysses")
    span = lax.axis_size("tm")
    rows, channels = queries.shape[1:]
    heads = channels // (parts * HD)
    sides = neighbours(span)
    pairs_sent = pack_pairs(keys[0], values[0], parts)
    queries_sent, gain_part = pack_queries(queries[0], out_grad[0], attn_out[0], out_gain, parts)
    pairs = exchange(pairs_sent)
    packed_queries = exchange(queries_sent)
    side_pairs = [lax.ppermute(pairs, "tm", there) for there, _ in sides]
    gain_all = lax.all_gather(gain_part, ("tm", "ulysses", "dp"), axis=0, tiled=True)
    token_count = rows * span * parts * lax.axis_size("dp")
    gain_grad = jnp.sum(gain_all, axis=0) / token_count
    flags = None
    if len(sides) > 1:
        position = lax.axis_index("tm")
        flags = jnp.stack([position > 0, position < span - 1]).astype(jnp.int32)
    query_grads, pair_grads = [], []
    for head in range(heads):
        query_grad, own, *others = attention(head, heads, packed_queries, [pairs] + side_pairs, flags)
        query_grads.append(query_grad)
        total = own
        for other, (_, back) in zip(others, sides):
            total = total + lax.ppermute(other, "tm", back).astype(jnp.float32)
        pair_grads.append(total.astype(jnp.bfloat16))
    token_query = unpack(exchange(jnp.concatenate(query_grads, axis=1)), heads)
    received = exchange(jnp.concatenate(pair_grads, axis=1)).reshape(parts, heads, 2, rows, HD)
    token_key = unpack(received[:, :, 0].reshape(parts, heads * rows, HD), heads)
    token_value = unpack(received[:, :, 1].reshape(parts, heads * rows, HD), heads)
    return (token_query, token_key, token_value, gain_grad)


def solution(mesh):
    split = P("dp", ("tm", "ulysses"), None)
    return jax.shard_map(
        local,
        mesh=mesh,
        in_specs=(split,) * 5 + (P(),),
        out_specs=(split,) * 3 + (P(),),
        check_vma=False,
    )
```

```python
import functools
import math

import jax
import jax.numpy as jnp
from jax import lax
from jax.experimental import pallas as pl
from jax.experimental.pallas import tpu as pltpu
from jax.sharding import PartitionSpec as P

HD = 128
LANES = 128
TILE_ROWS = 16
QUERY_BLOCK = 256
KEY_BLOCK = 256
VMEM_LIMIT = 48 * 1024 * 1024
SCALE = 1.0 / math.sqrt(HD)
SCALE_LOG2 = SCALE / math.log(2.0)


def params():
    return pltpu.CompilerParams(vmem_limit_bytes=VMEM_LIMIT)


def partner(distance):
    return lax.axis_index("ulysses") ^ distance


def column_of(distance, heads, head):
    return pl.multiple_of((partner(distance) * heads + head) * HD, HD)


def run_copies(pairs, semaphores):
    copies = [
        pltpu.make_async_copy(source, target, semaphores.at[index]) for index, (source, target) in enumerate(pairs)
    ]
    for copy in copies:
        copy.start()
    for copy in copies:
        copy.wait()


def pack_pairs_kernel(parts, key_ref, value_ref, *refs):
    pieces, semaphores = refs[:parts], refs[parts]
    rows, channels = key_ref.shape
    heads = channels // (parts * HD)
    pairs = []
    for distance in range(parts):
        for head in range(heads):
            columns = pl.ds(column_of(distance, heads, head), HD)
            for half, ref in enumerate((key_ref, value_ref)):
                start = (2 * head + half) * rows
                pairs.append((ref.at[:, columns], pieces[distance].at[start : start + rows]))
    run_copies(pairs, semaphores)


def pack_pairs(keys, values, parts):
    rows, channels = keys.shape
    heads = channels // (parts * HD)
    whole = pl.BlockSpec(memory_space=pl.ANY)
    return pl.pallas_call(
        functools.partial(pack_pairs_kernel, parts),
        in_specs=[whole, whole],
        out_specs=[whole] * parts,
        out_shape=[jax.ShapeDtypeStruct((2 * heads * rows, HD), keys.dtype)] * parts,
        scratch_shapes=[pltpu.SemaphoreType.DMA((2 * heads * parts,))],
        compiler_params=params(),
        cost_estimate=pl.CostEstimate(flops=0, bytes_accessed=8 * rows * channels, transcendentals=0),
    )(keys, values)


def dot_groups(rows):
    return -(-rows // LANES)


def dots_depth(rows):
    return -(-2 * dot_groups(rows) // TILE_ROWS) * TILE_ROWS


def pack_queries_kernel(parts, groups, query_ref, out_grad_ref, attn_ref, gain_ref, *refs):
    gain_part_ref = refs[-1]
    rows, channels = query_ref.shape
    heads = channels // (parts * HD)
    depth = 2 * rows + dots_depth(rows)
    for number, group in enumerate(groups):
        for distance in range(parts):
            piece = refs[number * parts + distance]
            for place, head in enumerate(group):
                columns = pl.ds(column_of(distance, heads, head), HD)
                out_grad = out_grad_ref[:, columns].astype(jnp.float32)
                attn = attn_ref[:, columns].astype(jnp.float32)
                grad = (out_grad * gain_ref[:, columns]).astype(jnp.bfloat16)
                gain_part_ref[:, columns] = jnp.sum(out_grad * attn, axis=0, keepdims=True)
                base = place * depth
                piece[base : base + rows] = query_ref[:, columns]
                piece[base + rows : base + 2 * rows] = grad
                dots = jnp.sum(jnp.transpose(grad.astype(jnp.float32) * attn), axis=0, keepdims=True)
                terms = []
                for first in range(0, rows, LANES):
                    value = dots[:, first : first + LANES]
                    if value.shape[1] < LANES:
                        rest = jnp.zeros((1, LANES - value.shape[1]), jnp.float32)
                        value = jnp.concatenate([value, rest], axis=1)
                    high = value.astype(jnp.bfloat16).astype(jnp.float32)
                    terms += [high, value - high]
                terms.append(jnp.zeros((dots_depth(rows) - len(terms), LANES), jnp.float32))
                piece[base + 2 * rows : base + depth] = jnp.concatenate(terms, axis=0).astype(jnp.bfloat16)


def pack_queries(queries, out_grad, attn_out, out_gain, parts, groups):
    rows, channels = queries.shape
    depth = 2 * rows + dots_depth(rows)
    out_shape = [
        jax.ShapeDtypeStruct((depth * len(group), HD), jnp.bfloat16) for group in groups for _ in range(parts)
    ]
    *pieces, gain_part = pl.pallas_call(
        functools.partial(pack_queries_kernel, parts, groups),
        out_shape=out_shape + [jax.ShapeDtypeStruct((1, channels), jnp.float32)],
        compiler_params=params(),
        cost_estimate=pl.CostEstimate(
            flops=8 * rows * channels, bytes_accessed=10 * rows * channels, transcendentals=0
        ),
    )(queries, out_grad, attn_out, out_gain.reshape(1, channels))
    return [pieces[number * parts : (number + 1) * parts] for number in range(len(groups))], gain_part


def attention_kernel(parts, sources, masked, rows, *refs):
    flags_ref = None
    if masked:
        flags_ref, refs = refs[0], refs[1:]
    query_refs, refs = refs[:parts], refs[parts:]
    pair_refs, refs = refs[: parts * sources], refs[parts * sources :]
    query_grad_refs, own_ref = refs[:parts], refs[parts]
    side_refs = refs[parts + 1 : parts + sources]
    score_ref, key_acc, value_acc = refs[parts + sources :]
    slab = parts * rows
    queries = jnp.concatenate([ref[:rows] for ref in query_refs], axis=0)
    grads = jnp.concatenate([ref[rows : 2 * rows] for ref in query_refs], axis=0)
    lines = []
    for ref in query_refs:
        terms = ref[2 * rows : 2 * rows + dots_depth(rows)].astype(jnp.float32)
        for index in range(dot_groups(rows)):
            count = min(LANES, rows - index * LANES)
            lines.append((terms[2 * index : 2 * index + 1] + terms[2 * index + 1 : 2 * index + 2])[:, :count])
    dots = jnp.concatenate(lines, axis=1)
    keys, values = [], []
    for source in range(sources):
        held = pair_refs[source * parts : (source + 1) * parts]
        keys.append(jnp.concatenate([ref[:rows] for ref in held], axis=0))
        values.append(jnp.concatenate([ref[rows:] for ref in held], axis=0))
    blocks = [(source, first) for source in range(sources) for first in range(0, slab, KEY_BLOCK)]
    query_grads = []
    for query_first in range(0, slab, QUERY_BLOCK):
        span = slice(query_first, query_first + QUERY_BLOCK)
        query_block, grad_block = queries[span], grads[span]
        query_flip, grad_flip = jnp.transpose(query_block), jnp.transpose(grad_block)
        dots_block = dots[:, span]
        top = None
        for source, first in blocks:
            scores = jnp.dot(
                keys[source][first : first + KEY_BLOCK], query_flip, preferred_element_type=jnp.float32
            )
            if masked and source > 0:
                scores = jnp.where(flags_ref[source - 1] > 0, scores, -jnp.inf)
            place = source * slab + first
            score_ref[place : place + KEY_BLOCK] = scores
            part_top = jnp.max(scores.reshape(-1, 8, QUERY_BLOCK), axis=0)
            top = part_top if top is None else jnp.maximum(top, part_top)
        top = jnp.max(top, axis=0, keepdims=True) * SCALE_LOG2
        total = None
        for source, first in blocks:
            place = source * slab + first
            powers = jnp.exp2(score_ref[place : place + KEY_BLOCK] * SCALE_LOG2 - top)
            score_ref[place : place + KEY_BLOCK] = powers
            part_total = jnp.sum(powers.reshape(-1, 8, QUERY_BLOCK), axis=0)
            total = part_total if total is None else total + part_total
        inverse = 1.0 / jnp.sum(total, axis=0, keepdims=True)
        query_acc = None
        for source, first in blocks:
            place = source * slab + first
            stretch = slice(first, first + KEY_BLOCK)
            weights = score_ref[place : place + KEY_BLOCK] * inverse
            grad_weights = jnp.dot(values[source][stretch], grad_flip, preferred_element_type=jnp.float32)
            grad_scores = (weights * (grad_weights - dots_block)).astype(jnp.bfloat16)
            value_part = jnp.dot(weights.astype(jnp.bfloat16), grad_block, preferred_element_type=jnp.float32)
            key_part = jnp.dot(grad_scores, query_block, preferred_element_type=jnp.float32)
            query_part = lax.dot_general(
                grad_scores,
                keys[source][stretch],
                (((0,), (0,)), ((), ())),
                preferred_element_type=jnp.float32,
            )
            query_acc = query_part if query_acc is None else query_acc + query_part
            if query_first == 0:
                key_acc[place : place + KEY_BLOCK] = key_part
                value_acc[place : place + KEY_BLOCK] = value_part
            else:
                key_acc[place : place + KEY_BLOCK] += key_part
                value_acc[place : place + KEY_BLOCK] += value_part
        query_grads.append((query_acc * SCALE).astype(jnp.bfloat16))
    query_grad = jnp.concatenate(query_grads, axis=0)
    for part in range(parts):
        query_grad_refs[part][...] = query_grad[part * rows : (part + 1) * rows]
    for source in range(sources):
        out_ref = own_ref if source == 0 else side_refs[source - 1]
        for part in range(parts):
            span = slice(source * slab + part * rows, source * slab + (part + 1) * rows)
            start = 2 * part * rows
            out_ref[start : start + rows] = (key_acc[span] * SCALE).astype(out_ref.dtype)
            out_ref[start + rows : start + 2 * rows] = value_acc[span].astype(out_ref.dtype)


def attention(head, place, query_pieces, pair_pieces, rows, flags):
    parts = len(query_pieces)
    sources = len(pair_pieces)
    masked = flags is not None
    slab = parts * rows
    query_depth = 2 * rows + dots_depth(rows)

    def block(depth, index):
        return pl.BlockSpec((depth, HD), lambda step: (index, 0))

    in_specs = [block(query_depth, place)] * parts + [block(2 * rows, head)] * (parts * sources)
    operands = list(query_pieces) + [piece for held in pair_pieces for piece in held]
    if masked:
        in_specs = [pl.BlockSpec(memory_space=pltpu.SMEM)] + in_specs
        operands = [flags] + operands
    pairs_of = slab * sources * slab
    outs = pl.pallas_call(
        functools.partial(attention_kernel, parts, sources, masked, rows),
        grid=(1,),
        in_specs=in_specs,
        out_specs=[block(rows, 0)] * parts + [block(2 * slab, 0)] * sources,
        out_shape=[jax.ShapeDtypeStruct((rows, HD), jnp.bfloat16)] * parts
        + [jax.ShapeDtypeStruct((2 * slab, HD), jnp.float32)]
        + [jax.ShapeDtypeStruct((2 * slab, HD), jnp.bfloat16)] * (sources - 1),
        scratch_shapes=[
            pltpu.VMEM((sources * slab, QUERY_BLOCK), jnp.float32),
            pltpu.VMEM((sources * slab, HD), jnp.float32),
            pltpu.VMEM((sources * slab, HD), jnp.float32),
        ],
        compiler_params=params(),
        cost_estimate=pl.CostEstimate(
            flops=10 * pairs_of * HD, bytes_accessed=slab * HD * 2 * (4 + 6 * sources), transcendentals=pairs_of
        ),
    )(*operands)
    return outs[:parts], outs[parts], outs[parts + 1 :]


def close_kernel(parts, rows, sides, lead, *refs):
    leads, refs = refs[: parts * lead], refs[parts * lead :]
    own_ref, side_refs, pieces = refs[0], refs[1 : 1 + sides], refs[1 + sides :]
    for part in range(parts):
        base = 0
        if lead:
            pieces[part][:rows] = leads[part][...]
            base = rows
        span = slice(2 * part * rows, 2 * (part + 1) * rows)
        total = own_ref[span]
        for ref in side_refs:
            total = total + ref[span].astype(jnp.float32)
        pieces[part][base : base + 2 * rows] = total.astype(jnp.bfloat16)


def close(query_grads, own, sides):
    lead = int(query_grads is not None)
    leads = list(query_grads) if lead else []
    parts = len(leads) if lead else lax.axis_size("ulysses")
    rows = own.shape[0] // (2 * parts)
    depth = (2 + lead) * rows
    return pl.pallas_call(
        functools.partial(close_kernel, parts, rows, len(sides), lead),
        out_shape=[jax.ShapeDtypeStruct((depth, HD), jnp.bfloat16)] * parts,
        compiler_params=params(),
        cost_estimate=pl.CostEstimate(
            flops=own.size * (1 + len(sides)), bytes_accessed=own.size * 8, transcendentals=0
        ),
    )(*leads, own, *sides)


def unpack_kernel(parts, rows, heads, stages, *refs):
    count = parts * len(stages)
    pieces, outs, semaphores = refs[:count], refs[count:-1], refs[-1]
    pairs = []
    for number, blocks in enumerate(stages):
        for distance in range(parts):
            piece = pieces[number * parts + distance]
            for index, (output, head) in enumerate(blocks):
                columns = pl.ds(column_of(distance, heads, head), HD)
                pairs.append((piece.at[index * rows : (index + 1) * rows], outs[output].at[:, columns]))
    run_copies(pairs, semaphores)


def unpack(stages, pieces, rows, heads):
    parts = len(pieces[0])
    whole = pl.BlockSpec(memory_space=pl.ANY)
    channels = parts * heads * HD
    return pl.pallas_call(
        functools.partial(unpack_kernel, parts, rows, heads, stages),
        in_specs=[whole] * (parts * len(stages)),
        out_specs=[whole] * 3,
        out_shape=[jax.ShapeDtypeStruct((rows, channels), jnp.bfloat16)] * 3,
        scratch_shapes=[pltpu.SemaphoreType.DMA((3 * heads * parts,))],
        compiler_params=params(),
        cost_estimate=pl.CostEstimate(flops=0, bytes_accessed=12 * rows * channels, transcendentals=0),
    )(*[piece for stage in pieces for piece in stage])


def swap(value, axis, distance):
    return lax.ppermute(value, axis, [(index, index ^ distance) for index in range(lax.axis_size(axis))])


def swap_pieces(pieces):
    return [pieces[0]] + [swap(piece, "ulysses", distance) for distance, piece in enumerate(pieces) if distance]


def total_of(value, axes):
    for axis in axes:
        size = lax.axis_size(axis)
        if size & (size - 1):
            value = lax.psum(value, axis)
            continue
        distance = 1
        while distance < size:
            value = value + swap(value, axis, distance)
            distance *= 2
    return value


def after(values, *earlier):
    return lax.optimization_barrier((list(values), earlier))[0]


def neighbours(size):
    if size == 1:
        return []
    if size == 2:
        swapped = [(0, 1), (1, 0)]
        return [(swapped, swapped)]
    up = [(index, index + 1) for index in range(size - 1)]
    down = [(index + 1, index) for index in range(size - 1)]
    return [(up, down), (down, up)]


def local(queries, keys, values, attn_out, out_grad, out_gain):
    parts = lax.axis_size("ulysses")
    span = lax.axis_size("tm")
    rows, channels = queries.shape[1:]
    heads = channels // (parts * HD)
    sides = neighbours(span)
    groups = [[head] for head in range(heads)]
    pairs = swap_pieces(pack_pairs(keys[0], values[0], parts))
    side_pairs = [[lax.ppermute(piece, "tm", there) for piece in pairs] for there, _ in sides]
    sent, gain_part = pack_queries(queries[0], out_grad[0], attn_out[0], out_gain, parts, groups)
    token_count = rows * span * parts * lax.axis_size("dp")
    gain_grad = total_of(gain_part.reshape(-1, LANES), ("tm", "dp", "ulysses")).reshape(channels) / token_count
    flags = None
    if len(sides) > 1:
        position = lax.axis_index("tm")
        flags = jnp.stack([position > 0, position < span - 1]).astype(jnp.int32)
    gates = [pairs[1 % parts], pairs[2 % parts]]
    held = []
    for number in range(len(groups)):
        held.append(swap_pieces(after(sent[number], gates[number])))
        gates.append(held[-1][2 % parts])
    stages, pieces = [], []
    own = others = None
    for head in range(heads):
        query_grads, next_own, next_others = attention(head, 0, held[head], [pairs] + side_pairs, rows, flags)
        if head == 0:
            stages.append([(0, 0)])
            pieces.append(swap_pieces(query_grads))
        else:
            stages.append([(0, head), (1, head - 1), (2, head - 1)])
            pieces.append(swap_pieces(close(query_grads, own, others)))
        own = next_own
        others = [lax.ppermute(other, "tm", back) for other, (_, back) in zip(next_others, sides)]
    stages.append([(1, heads - 1), (2, heads - 1)])
    pieces.append(swap_pieces(close(None, own, others)))
    grads = unpack(stages, pieces, rows, heads)
    return tuple(grad[None] for grad in grads) + (gain_grad,)


def solution(mesh):
    split = P("dp", ("tm", "ulysses"), None)
    return jax.shard_map(
        local,
        mesh=mesh,
        in_specs=(split,) * 5 + (P(),),
        out_specs=(split,) * 3 + (P(),),
        check_vma=False,
    )
```

```python
import functools
import math

import jax
import jax.numpy as jnp
from jax import lax
from jax.experimental import pallas as pl
from jax.experimental.pallas import tpu as pltpu
from jax.sharding import PartitionSpec as P

HD = 128
LANES = 128
TILE_ROWS = 16
KEY_BLOCK = 256
QUERY_BLOCK = 256
VMEM_LIMIT = 48 * 1024 * 1024
SCALE = 1.0 / math.sqrt(HD)
SCALE_LOG2 = SCALE / math.log(2.0)
COST = pl.CostEstimate(flops=1, bytes_accessed=1, transcendentals=0)


def params():
    return pltpu.CompilerParams(vmem_limit_bytes=VMEM_LIMIT)


def partner(distance):
    return lax.axis_index("ulysses") ^ distance


def column_of(distance, heads, head):
    return pl.multiple_of((partner(distance) * heads + head) * HD, HD)


def run_copies(pairs, semaphores):
    copies = [
        pltpu.make_async_copy(source, target, semaphores.at[index]) for index, (source, target) in enumerate(pairs)
    ]
    for copy in copies:
        copy.start()
    for copy in copies:
        copy.wait()


def pack_kernel(parts, *refs):
    sources, pieces, semaphores = refs[: -parts - 1], refs[-parts - 1 : -1], refs[-1]
    rows, channels = sources[0].shape
    heads = channels // (parts * HD)
    pairs = []
    for distance in range(parts):
        for half, ref in enumerate(sources):
            for head in range(heads):
                columns = pl.ds(column_of(distance, heads, head), HD)
                start = (half * heads + head) * rows
                pairs.append((ref.at[:, columns], pieces[distance].at[start : start + rows]))
    run_copies(pairs, semaphores)


def pack(sources, parts):
    rows, channels = sources[0].shape
    heads = channels // (parts * HD)
    depth = len(sources) * heads * rows
    whole = pl.BlockSpec(memory_space=pl.ANY)
    return pl.pallas_call(
        functools.partial(pack_kernel, parts),
        in_specs=[whole] * len(sources),
        out_specs=[whole] * parts,
        out_shape=[jax.ShapeDtypeStruct((depth, HD), sources[0].dtype)] * parts,
        scratch_shapes=[pltpu.SemaphoreType.DMA((len(sources) * heads * parts,))],
        compiler_params=params(),
        cost_estimate=COST,
    )(*sources)


def dot_groups(rows):
    return -(-rows // LANES)


def dots_depth(rows, heads):
    return -(-2 * heads * dot_groups(rows) // TILE_ROWS) * TILE_ROWS


def pack_grads_kernel(parts, out_grad_ref, attn_ref, gain_ref, *refs):
    pieces, gain_part_ref = refs[:-1], refs[-1]
    rows, channels = out_grad_ref.shape
    heads = channels // (parts * HD)
    for distance, piece in enumerate(pieces):
        terms = []
        for head in range(heads):
            columns = pl.ds(column_of(distance, heads, head), HD)
            out_grad = out_grad_ref[:, columns].astype(jnp.float32)
            attn = attn_ref[:, columns].astype(jnp.float32)
            grad = (out_grad * gain_ref[:, columns]).astype(jnp.bfloat16)
            gain_part_ref[:, columns] = jnp.sum(out_grad * attn, axis=0, keepdims=True)
            piece[head * rows : (head + 1) * rows] = grad
            dots = jnp.sum(jnp.transpose(grad.astype(jnp.float32) * attn), axis=0, keepdims=True)
            for first in range(0, rows, LANES):
                value = dots[:, first : first + LANES]
                if value.shape[1] < LANES:
                    rest = jnp.zeros((1, LANES - value.shape[1]), jnp.float32)
                    value = jnp.concatenate([value, rest], axis=1)
                high = value.astype(jnp.bfloat16).astype(jnp.float32)
                terms += [high, value - high]
        rest = dots_depth(rows, heads) - len(terms)
        if rest:
            terms.append(jnp.zeros((rest, LANES), jnp.float32))
        piece[heads * rows :] = jnp.concatenate(terms, axis=0).astype(jnp.bfloat16)


def pack_grads(out_grad, attn_out, out_gain, parts):
    rows, channels = out_grad.shape
    heads = channels // (parts * HD)
    depth = heads * rows + dots_depth(rows, heads)
    outs = pl.pallas_call(
        functools.partial(pack_grads_kernel, parts),
        out_shape=[jax.ShapeDtypeStruct((depth, HD), jnp.bfloat16)] * parts
        + [jax.ShapeDtypeStruct((1, channels), jnp.float32)],
        compiler_params=params(),
        cost_estimate=COST,
    )(out_grad, attn_out, out_gain.reshape(1, channels))
    return outs[:parts], outs[parts]


def rows_of(refs, first, count):
    return jnp.concatenate([ref[first : first + count] for ref in refs], axis=0)


def totals_kernel(parts, sources, heads, rows, *refs):
    held, refs = refs[:parts], refs[parts:]
    sides, refs = refs[: parts * (sources - 1)], refs[parts * (sources - 1) :]
    outs, score_ref = refs[:sources], refs[sources]
    slab = parts * rows
    for head in range(heads):
        keys = rows_of(held, head * rows, rows)
        for source in range(sources):
            if source == 0:
                queries = rows_of(held, (heads + head) * rows, rows)
            else:
                queries = rows_of(sides[(source - 1) * parts : source * parts], head * rows, rows)
            flip = jnp.transpose(queries)
            top = None
            for first in range(0, slab, KEY_BLOCK):
                scores = jnp.dot(keys[first : first + KEY_BLOCK], flip, preferred_element_type=jnp.float32)
                score_ref[first : first + KEY_BLOCK] = scores
                part_top = jnp.max(scores.reshape(-1, 8, slab), axis=0)
                top = part_top if top is None else jnp.maximum(top, part_top)
            top = jnp.max(top, axis=0, keepdims=True) * SCALE_LOG2
            total = None
            for first in range(0, slab, KEY_BLOCK):
                powers = jnp.exp2(score_ref[first : first + KEY_BLOCK] * SCALE_LOG2 - top)
                part_total = jnp.sum(powers.reshape(-1, 8, slab), axis=0)
                total = part_total if total is None else total + part_total
            total = jnp.sum(total, axis=0, keepdims=True)
            outs[source][head : head + 1] = top + jnp.log(total) * (1.0 / math.log(2.0))


def partial_totals(pairs, side_queries, heads, rows):
    parts = len(pairs)
    sources = 1 + len(side_queries)
    slab = parts * rows
    return pl.pallas_call(
        functools.partial(totals_kernel, parts, sources, heads, rows),
        out_shape=[jax.ShapeDtypeStruct((heads, slab), jnp.float32)] * sources,
        scratch_shapes=[pltpu.VMEM((slab, slab), jnp.float32)],
        compiler_params=params(),
        cost_estimate=pl.CostEstimate(
            flops=2 * heads * sources * slab * slab * HD,
            bytes_accessed=heads * sources * slab * HD * 4,
            transcendentals=heads * sources * slab * slab,
        ),
    )(*pairs, *[piece for held in side_queries for piece in held])


def join_totals(values):
    top = functools.reduce(jnp.maximum, values)
    return top + jnp.log2(functools.reduce(jnp.add, [jnp.exp2(value - top) for value in values]))


def attention_kernel(parts, sources, head, rows, before, *refs):
    slab = parts * rows

    def take(count):
        nonlocal refs
        taken, refs = refs[:count], refs[count:]
        return taken

    key_refs, value_refs = take(parts), take(parts)
    query_refs, grad_refs, dots_refs = take(parts * sources), take(parts * sources), take(parts * sources)
    total_refs = take(sources)
    before_refs = take(sources) if before else ()
    piece_refs, query_grad_refs = take(parts), take(sources)
    weight_ref, score_ref = refs
    if before:
        closed = before_refs[0][...]
        for ref in before_refs[1:]:
            closed = closed + ref[...].astype(jnp.float32)
        closed = closed.astype(jnp.bfloat16)
        for part in range(parts):
            piece_refs[part][2 * rows :] = closed[part * rows : (part + 1) * rows]
    keys, values = rows_of(key_refs, 0, rows), rows_of(value_refs, 0, rows)
    queries, grads = rows_of(query_refs, 0, rows), rows_of(grad_refs, 0, rows)
    query_flip, grad_flip = jnp.transpose(queries), jnp.transpose(grads)
    lines = []
    for ref in dots_refs:
        terms = ref[...].astype(jnp.float32)
        for index in range(dot_groups(rows)):
            line = 2 * (head * dot_groups(rows) + index)
            count = min(LANES, rows - index * LANES)
            lines.append((terms[line : line + 1] + terms[line + 1 : line + 2])[:, :count])
    dots = jnp.concatenate(lines, axis=1)
    totals = jnp.concatenate([ref[head : head + 1] for ref in total_refs], axis=1)
    width = sources * slab
    for first in range(0, slab, KEY_BLOCK):
        stretch = slice(first, first + KEY_BLOCK)
        for start in range(0, width, QUERY_BLOCK):
            span = slice(start, start + QUERY_BLOCK)
            scores = jnp.dot(keys[stretch], query_flip[:, span], preferred_element_type=jnp.float32)
            weights = jnp.exp2(scores * SCALE_LOG2 - totals[:, span])
            grad_weights = jnp.dot(values[stretch], grad_flip[:, span], preferred_element_type=jnp.float32)
            weight_ref[stretch, span] = weights.astype(jnp.bfloat16)
            score_ref[stretch, span] = (weights * (grad_weights - dots[:, span])).astype(jnp.bfloat16)
        value_grad = jnp.dot(weight_ref[stretch], grads, preferred_element_type=jnp.float32)
        key_grad = jnp.dot(score_ref[stretch], queries, preferred_element_type=jnp.float32) * SCALE
        key_grad, value_grad = key_grad.astype(jnp.bfloat16), value_grad.astype(jnp.bfloat16)
        for part in range(parts):
            low, high = max(first, part * rows), min(first + KEY_BLOCK, (part + 1) * rows)
            if low < high:
                place = low - part * rows
                piece_refs[part][place : place + high - low] = key_grad[low - first : high - first]
                piece_refs[part][rows + place : rows + place + high - low] = value_grad[low - first : high - first]
    for source in range(sources):
        query_grad = lax.dot_general(
            score_ref[:, source * slab : (source + 1) * slab],
            keys,
            (((0,), (0,)), ((), ())),
            preferred_element_type=jnp.float32,
        )
        query_grad_refs[source][...] = (query_grad * SCALE).astype(query_grad_refs[source].dtype)


def attention(head, heads, rows, pairs, values, queries, grads, totals, before):
    parts = len(pairs)
    sources = len(queries)
    slab = parts * rows
    dots = dots_depth(rows, heads)

    def block(depth, index):
        return pl.BlockSpec((depth, HD), lambda step: (index, 0))

    flat_queries = [piece for held in queries for piece in held]
    flat_grads = [piece for held in grads for piece in held]
    operands = list(pairs) + list(values) + flat_queries + flat_grads + flat_grads + list(totals) + list(before)
    in_specs = [block(rows, head)] * (2 * parts)
    in_specs += [block(rows, heads + head)] * parts + [block(rows, head)] * (parts * (sources - 1))
    in_specs += [block(rows, head)] * (parts * sources) + [block(dots, heads * rows // dots)] * (parts * sources)
    in_specs += [pl.BlockSpec((heads, slab), lambda step: (0, 0))] * sources + [block(slab, 0)] * len(before)
    depth = (3 if before else 2) * rows
    outs = pl.pallas_call(
        functools.partial(attention_kernel, parts, sources, head, rows, bool(before)),
        grid=(1,),
        in_specs=in_specs,
        out_specs=[block(depth, 0)] * parts + [block(slab, 0)] * sources,
        out_shape=[jax.ShapeDtypeStruct((depth, HD), jnp.bfloat16)] * parts
        + [jax.ShapeDtypeStruct((slab, HD), jnp.float32)]
        + [jax.ShapeDtypeStruct((slab, HD), jnp.bfloat16)] * (sources - 1),
        scratch_shapes=[pltpu.VMEM((slab, sources * slab), jnp.bfloat16)] * 2,
        compiler_params=params(),
        cost_estimate=pl.CostEstimate(
            flops=10 * slab * sources * slab * HD,
            bytes_accessed=32 * slab * HD,
            transcendentals=slab * sources * slab,
        ),
    )(*operands)
    return outs[:parts], outs[parts:]


def close_kernel(parts, *refs):
    own_ref, side_refs, pieces = refs[0], refs[1:-parts], refs[-parts:]
    rows = pieces[0].shape[0]
    for part in range(parts):
        span = slice(part * rows, (part + 1) * rows)
        total = own_ref[span]
        for ref in side_refs:
            total = total + ref[span].astype(jnp.float32)
        pieces[part][...] = total.astype(jnp.bfloat16)


def close(query_grads, parts):
    rows = query_grads[0].shape[0] // parts
    return pl.pallas_call(
        functools.partial(close_kernel, parts),
        out_shape=[jax.ShapeDtypeStruct((rows, HD), jnp.bfloat16)] * parts,
        compiler_params=params(),
        cost_estimate=COST,
    )(*query_grads)


def unpack_kernel(parts, rows, heads, stages, *refs):
    count = parts * len(stages)
    pieces, outs, semaphores = refs[:count], refs[count:-1], refs[-1]
    pairs = []
    for number, blocks in enumerate(stages):
        for distance in range(parts):
            piece = pieces[number * parts + distance]
            for index, (output, head) in enumerate(blocks):
                columns = pl.ds(column_of(distance, heads, head), HD)
                pairs.append((piece.at[index * rows : (index + 1) * rows], outs[output].at[:, columns]))
    run_copies(pairs, semaphores)


def unpack(stages, pieces, rows, heads):
    parts = len(pieces[0])
    whole = pl.BlockSpec(memory_space=pl.ANY)
    channels = parts * heads * HD
    return pl.pallas_call(
        functools.partial(unpack_kernel, parts, rows, heads, stages),
        in_specs=[whole] * (parts * len(stages)),
        out_specs=[whole] * 3,
        out_shape=[jax.ShapeDtypeStruct((rows, channels), jnp.bfloat16)] * 3,
        scratch_shapes=[pltpu.SemaphoreType.DMA((3 * heads * parts,))],
        compiler_params=params(),
        cost_estimate=COST,
    )(*[piece for stage in pieces for piece in stage])


def swap(value, axis, distance):
    return lax.ppermute(value, axis, [(index, index ^ distance) for index in range(lax.axis_size(axis))])


def swap_pieces(pieces):
    return [pieces[0]] + [swap(piece, "ulysses", distance) for distance, piece in enumerate(pieces) if distance]


def total_of(value, axes):
    for axis in axes:
        size = lax.axis_size(axis)
        if size & (size - 1):
            value = lax.psum(value, axis)
            continue
        distance = 1
        while distance < size:
            value = value + swap(value, axis, distance)
            distance *= 2
    return value


def after(values, *earlier):
    return lax.optimization_barrier((list(values), earlier))[0]


def neighbours(size):
    if size == 1:
        return []
    if size == 2:
        swapped = [(0, 1), (1, 0)]
        return [(swapped, swapped)]
    up = [(index, index + 1) for index in range(size - 1)]
    down = [(index + 1, index) for index in range(size - 1)]
    return [(up, down), (down, up)]


def exchange_totals(partial, sides):
    if not sides:
        return partial
    if len(sides) == 1:
        other = lax.ppermute(jnp.concatenate(partial), "tm", sides[0][0])
        heads = partial[0].shape[0]
        return [join_totals([partial[0], other[heads:]]), join_totals([partial[1], other[:heads]])]
    position = lax.axis_index("tm")
    present = [position < lax.axis_size("tm") - 1, position > 0]
    values = [partial[0]]
    for value, (_, back), flag in zip(partial[1:], sides, present):
        values.append(jnp.where(flag, lax.ppermute(value, "tm", back), -jnp.inf))
    own = join_totals(values)
    return [own] + [lax.ppermute(own, "tm", there) for there, _ in sides]


def local(queries, keys, values, attn_out, out_grad, out_gain):
    parts = lax.axis_size("ulysses")
    span = lax.axis_size("tm")
    rows, channels = queries.shape[1:]
    heads = channels // (parts * HD)
    sides = neighbours(span)
    with jax.named_scope("keys_queries"):
        pairs = swap_pieces(pack([keys[0], queries[0]], parts))
    with jax.named_scope("halo_queries"):
        side_queries = [[lax.ppermute(piece[heads * rows :], "tm", there) for piece in pairs] for there, _ in sides]
    with jax.named_scope("grads"):
        sent, gain_part = pack_grads(out_grad[0], attn_out[0], out_gain, parts)
        held_grads = swap_pieces(after(sent, pairs))
    with jax.named_scope("halo_grads"):
        side_grads = [[lax.ppermute(piece, "tm", there) for piece in held_grads] for there, _ in sides]
    with jax.named_scope("values"):
        held_values = swap_pieces(after(pack([values[0]], parts), held_grads))
    token_count = rows * span * parts * lax.axis_size("dp")
    with jax.named_scope("gain"):
        gain_total = total_of(gain_part.reshape(-1, LANES), ("tm", "dp", "ulysses"))
        gain_grad = gain_total.reshape(channels) / token_count
    with jax.named_scope("totals"):
        part_totals = partial_totals(pairs, side_queries, heads, rows)
        totals = exchange_totals(after(part_totals, held_grads), sides)
    held_values = after(held_values, gain_total)
    stages, pieces = [], []
    before = ()
    for head in range(heads):
        with jax.named_scope("attention_%d" % head):
            leaving, query_grads = attention(
                head,
                heads,
                rows,
                pairs,
                held_values,
                [pairs] + side_queries,
                [held_grads] + side_grads,
                totals,
                before,
            )
        stages.append([(1, head), (2, head)] + ([(0, head - 1)] if head else []))
        if head:
            leaving, query_grads = lax.optimization_barrier((leaving, query_grads, pieces[-1][1:]))[:2]
        with jax.named_scope("halo_query_grads_%d" % head):
            before = list(query_grads[:1]) + [
                lax.ppermute(other, "tm", back) for other, (_, back) in zip(query_grads[1:], sides)
            ]
        with jax.named_scope("returns_%d" % head):
            pieces.append(swap_pieces(leaving))
    with jax.named_scope("returns_last"):
        stages.append([(0, heads - 1)])
        pieces.append(swap_pieces(close(before, parts)))
    result = unpack(stages, pieces, rows, heads)
    return tuple(grad[None] for grad in result) + (gain_grad,)


def solution(mesh):
    split = P("dp", ("tm", "ulysses"), None)
    return jax.shard_map(
        local,
        mesh=mesh,
        in_specs=(split,) * 5 + (P(),),
        out_specs=(split,) * 3 + (P(),),
        check_vma=False,
    )
```

```python
import functools
import math

import jax
import jax.numpy as jnp
from jax import lax
from jax.experimental import pallas as pl
from jax.experimental.pallas import tpu as pltpu
from jax.sharding import PartitionSpec as P

HD = 128
LANES = 128
TILE_ROWS = 16
KEY_BLOCK = 256
QUERY_BLOCK = 256
VMEM_LIMIT = 48 * 1024 * 1024
SCALE = 1.0 / math.sqrt(HD)
SCALE_LOG2 = SCALE / math.log(2.0)
COST = pl.CostEstimate(flops=1, bytes_accessed=1, transcendentals=0)


def params():
    return pltpu.CompilerParams(vmem_limit_bytes=VMEM_LIMIT)


def partner(distance):
    return lax.axis_index("ulysses") ^ distance


def column_of(distance, heads, head):
    return pl.multiple_of((partner(distance) * heads + head) * HD, HD)


def run_copies(pairs, semaphores):
    copies = [
        pltpu.make_async_copy(source, target, semaphores.at[index]) for index, (source, target) in enumerate(pairs)
    ]
    for copy in copies:
        copy.start()
    for copy in copies:
        copy.wait()


def pack_kernel(parts, chosen, *refs):
    sources, pieces, semaphores = refs[: -parts - 1], refs[-parts - 1 : -1], refs[-1]
    rows, channels = sources[0].shape
    heads = channels // (parts * HD)
    pairs = []
    for distance in range(parts):
        for half, ref in enumerate(sources):
            for place, head in enumerate(chosen):
                columns = pl.ds(column_of(distance, heads, head), HD)
                start = (half * len(chosen) + place) * rows
                pairs.append((ref.at[:, columns], pieces[distance].at[start : start + rows]))
    run_copies(pairs, semaphores)


def pack(sources, parts, chosen):
    rows = sources[0].shape[0]
    depth = len(sources) * len(chosen) * rows
    whole = pl.BlockSpec(memory_space=pl.ANY)
    return pl.pallas_call(
        functools.partial(pack_kernel, parts, chosen),
        in_specs=[whole] * len(sources),
        out_specs=[whole] * parts,
        out_shape=[jax.ShapeDtypeStruct((depth, HD), sources[0].dtype)] * parts,
        scratch_shapes=[pltpu.SemaphoreType.DMA((len(sources) * len(chosen) * parts,))],
        compiler_params=params(),
        cost_estimate=COST,
    )(*sources)


def gather_kernel(ranges, *refs):
    arrays, out_ref, semaphores = refs[:-2], refs[-2], refs[-1]
    pairs = []
    place = 0
    for number, first, count in ranges:
        pairs.append((arrays[number].at[first : first + count], out_ref.at[place : place + count]))
        place += count
    run_copies(pairs, semaphores)


def gather_rows(arrays, ranges):
    whole = pl.BlockSpec(memory_space=pl.ANY)
    depth = sum(count for _, _, count in ranges)
    return pl.pallas_call(
        functools.partial(gather_kernel, ranges),
        in_specs=[whole] * len(arrays),
        out_specs=whole,
        out_shape=jax.ShapeDtypeStruct((depth, HD), arrays[0].dtype),
        scratch_shapes=[pltpu.SemaphoreType.DMA((len(ranges),))],
        compiler_params=params(),
        cost_estimate=COST,
    )(*arrays)


def dot_groups(rows):
    return -(-rows // LANES)


def dots_depth(rows, heads):
    return -(-2 * heads * dot_groups(rows) // TILE_ROWS) * TILE_ROWS


def pack_grads_kernel(parts, out_grad_ref, attn_ref, value_ref, gain_ref, *refs):
    leads, rests, gain_part_ref = refs[:parts], refs[parts:-1], refs[-1]
    rows, channels = out_grad_ref.shape
    heads = channels // (parts * HD)
    for distance in range(parts):
        terms = []
        for head in range(heads):
            columns = pl.ds(column_of(distance, heads, head), HD)
            out_grad = out_grad_ref[:, columns].astype(jnp.float32)
            attn = attn_ref[:, columns].astype(jnp.float32)
            grad = (out_grad * gain_ref[:, columns]).astype(jnp.bfloat16)
            gain_part_ref[:, columns] = jnp.sum(out_grad * attn, axis=0, keepdims=True)
            if head:
                rests[distance][(head - 1) * rows : head * rows] = grad
            else:
                leads[distance][:rows] = grad
                leads[distance][rows : 2 * rows] = value_ref[:, columns]
            dots = jnp.sum(jnp.transpose(grad.astype(jnp.float32) * attn), axis=0, keepdims=True)
            for first in range(0, rows, LANES):
                value = dots[:, first : first + LANES]
                if value.shape[1] < LANES:
                    rest = jnp.zeros((1, LANES - value.shape[1]), jnp.float32)
                    value = jnp.concatenate([value, rest], axis=1)
                high = value.astype(jnp.bfloat16).astype(jnp.float32)
                terms += [high, value - high]
        rest = dots_depth(rows, heads) - len(terms)
        if rest:
            terms.append(jnp.zeros((rest, LANES), jnp.float32))
        leads[distance][2 * rows :] = jnp.concatenate(terms, axis=0).astype(jnp.bfloat16)


def pack_grads(out_grad, attn_out, values, out_gain, parts):
    rows, channels = out_grad.shape
    heads = channels // (parts * HD)
    lead = jax.ShapeDtypeStruct((2 * rows + dots_depth(rows, heads), HD), jnp.bfloat16)
    rest = jax.ShapeDtypeStruct(((heads - 1) * rows, HD), jnp.bfloat16)
    outs = pl.pallas_call(
        functools.partial(pack_grads_kernel, parts),
        out_shape=[lead] * parts + [rest] * parts + [jax.ShapeDtypeStruct((1, channels), jnp.float32)],
        compiler_params=params(),
        cost_estimate=COST,
    )(out_grad, attn_out, values, out_gain.reshape(1, channels))
    return outs[:parts], outs[parts : 2 * parts], outs[2 * parts]


def stacked(refs):
    return jnp.concatenate([ref[...] for ref in refs], axis=0)


def block_specs(depth, places):
    def block(index):
        return pl.BlockSpec((depth, HD), lambda step: (index, 0))

    return [block(index) for _, index in places], [array for array, _ in places]


def totals_kernel(parts, sources, heads, *refs):
    key_refs, refs = refs[: parts * heads], refs[parts * heads :]
    query_refs, refs = refs[: parts * heads * sources], refs[parts * heads * sources :]
    outs, score_ref = refs[:sources], refs[sources]
    slab = score_ref.shape[0]
    for head in range(heads):
        keys = stacked(key_refs[head * parts : (head + 1) * parts])
        for source in range(sources):
            start = (source * heads + head) * parts
            flip = jnp.transpose(stacked(query_refs[start : start + parts]))
            top = None
            for first in range(0, slab, KEY_BLOCK):
                scores = jnp.dot(keys[first : first + KEY_BLOCK], flip, preferred_element_type=jnp.float32)
                score_ref[first : first + KEY_BLOCK] = scores
                part_top = jnp.max(scores.reshape(-1, 8, slab), axis=0)
                top = part_top if top is None else jnp.maximum(top, part_top)
            top = jnp.max(top, axis=0, keepdims=True) * SCALE_LOG2
            total = None
            for first in range(0, slab, KEY_BLOCK):
                powers = jnp.exp2(score_ref[first : first + KEY_BLOCK] * SCALE_LOG2 - top)
                part_total = jnp.sum(powers.reshape(-1, 8, slab), axis=0)
                total = part_total if total is None else total + part_total
            total = jnp.sum(total, axis=0, keepdims=True)
            outs[source][head : head + 1] = top + jnp.log(total) * (1.0 / math.log(2.0))


def partial_totals(keys, queries, rows):
    heads, parts, sources = len(keys), len(keys[0]), len(queries)
    slab = parts * rows
    places = [place for head in keys for place in head]
    places += [place for source in queries for head in source for place in head]
    in_specs, operands = block_specs(rows, places)
    line = pl.BlockSpec((heads, slab), lambda step: (0, 0))
    return pl.pallas_call(
        functools.partial(totals_kernel, parts, sources, heads),
        grid=(1,),
        in_specs=in_specs,
        out_specs=[line] * sources,
        out_shape=[jax.ShapeDtypeStruct((heads, slab), jnp.float32)] * sources,
        scratch_shapes=[pltpu.VMEM((slab, slab), jnp.float32)],
        compiler_params=params(),
        cost_estimate=pl.CostEstimate(
            flops=2 * heads * sources * slab * slab * HD,
            bytes_accessed=heads * sources * slab * HD * 4,
            transcendentals=heads * sources * slab * slab,
        ),
    )(*operands)


def join_totals(values):
    top = functools.reduce(jnp.maximum, values)
    return top + jnp.log2(functools.reduce(jnp.add, [jnp.exp2(value - top) for value in values]))


def attention_kernel(parts, sources, head, rows, before, *refs):
    slab = parts * rows

    def take(count):
        nonlocal refs
        taken, refs = refs[:count], refs[count:]
        return taken

    key_refs, value_refs = take(parts), take(parts)
    query_refs, grad_refs, dots_refs = take(parts * sources), take(parts * sources), take(parts * sources)
    total_refs = take(sources)
    before_refs = take(sources) if before else ()
    piece_refs, query_grad_refs = take(parts), take(sources)
    weight_ref, score_ref = refs
    if before:
        closed = before_refs[0][...]
        for ref in before_refs[1:]:
            closed = closed + ref[...].astype(jnp.float32)
        closed = closed.astype(jnp.bfloat16)
        for part in range(parts):
            piece_refs[part][2 * rows :] = closed[part * rows : (part + 1) * rows]
    keys, values, queries, grads = stacked(key_refs), stacked(value_refs), stacked(query_refs), stacked(grad_refs)
    query_flip, grad_flip = jnp.transpose(queries), jnp.transpose(grads)
    lines = []
    for ref in dots_refs:
        terms = ref[...].astype(jnp.float32)
        for index in range(dot_groups(rows)):
            line = 2 * (head * dot_groups(rows) + index)
            count = min(LANES, rows - index * LANES)
            lines.append((terms[line : line + 1] + terms[line + 1 : line + 2])[:, :count])
    dots = jnp.concatenate(lines, axis=1)
    totals = jnp.concatenate([ref[head : head + 1] for ref in total_refs], axis=1)
    width = sources * slab
    for first in range(0, slab, KEY_BLOCK):
        stretch = slice(first, first + KEY_BLOCK)
        for start in range(0, width, QUERY_BLOCK):
            span = slice(start, start + QUERY_BLOCK)
            scores = jnp.dot(keys[stretch], query_flip[:, span], preferred_element_type=jnp.float32)
            weights = jnp.exp2(scores * SCALE_LOG2 - totals[:, span])
            grad_weights = jnp.dot(values[stretch], grad_flip[:, span], preferred_element_type=jnp.float32)
            weight_ref[stretch, span] = weights.astype(jnp.bfloat16)
            score_ref[stretch, span] = (weights * (grad_weights - dots[:, span])).astype(jnp.bfloat16)
        value_grad = jnp.dot(weight_ref[stretch], grads, preferred_element_type=jnp.float32)
        key_grad = jnp.dot(score_ref[stretch], queries, preferred_element_type=jnp.float32) * SCALE
        key_grad, value_grad = key_grad.astype(jnp.bfloat16), value_grad.astype(jnp.bfloat16)
        for part in range(parts):
            low, high = max(first, part * rows), min(first + KEY_BLOCK, (part + 1) * rows)
            if low < high:
                place = low - part * rows
                piece_refs[part][place : place + high - low] = key_grad[low - first : high - first]
                piece_refs[part][rows + place : rows + place + high - low] = value_grad[low - first : high - first]
    for source in range(sources):
        query_grad = lax.dot_general(
            score_ref[:, source * slab : (source + 1) * slab],
            keys,
            (((0,), (0,)), ((), ())),
            preferred_element_type=jnp.float32,
        )
        query_grad_refs[source][...] = (query_grad * SCALE).astype(query_grad_refs[source].dtype)


def attention(head, heads, rows, keys, values, queries, grads, dots, totals, before):
    parts = len(keys)
    sources = len(totals)
    slab = parts * rows
    in_specs, operands = block_specs(rows, keys + values + queries + grads)
    dot_specs, dot_arrays = block_specs(dots_depth(rows, heads), dots)
    before_specs, before_arrays = block_specs(slab, [(array, 0) for array in before])
    line = pl.BlockSpec((heads, slab), lambda step: (0, 0))
    depth = (3 if before else 2) * rows
    out_specs, _ = block_specs(depth, [(None, 0)] * parts)
    query_specs, _ = block_specs(slab, [(None, 0)] * sources)
    outs = pl.pallas_call(
        functools.partial(attention_kernel, parts, sources, head, rows, bool(before)),
        grid=(1,),
        in_specs=in_specs + dot_specs + [line] * sources + before_specs,
        out_specs=out_specs + query_specs,
        out_shape=[jax.ShapeDtypeStruct((depth, HD), jnp.bfloat16)] * parts
        + [jax.ShapeDtypeStruct((slab, HD), jnp.float32)]
        + [jax.ShapeDtypeStruct((slab, HD), jnp.bfloat16)] * (sources - 1),
        scratch_shapes=[pltpu.VMEM((slab, sources * slab), jnp.bfloat16)] * 2,
        compiler_params=params(),
        cost_estimate=pl.CostEstimate(
            flops=10 * slab * sources * slab * HD,
            bytes_accessed=32 * slab * HD,
            transcendentals=slab * sources * slab,
        ),
    )(*operands, *dot_arrays, *totals, *before_arrays)
    return outs[:parts], outs[parts:]


def close_kernel(parts, *refs):
    own_ref, side_refs, pieces = refs[0], refs[1:-parts], refs[-parts:]
    rows = pieces[0].shape[0]
    for part in range(parts):
        span = slice(part * rows, (part + 1) * rows)
        total = own_ref[span]
        for ref in side_refs:
            total = total + ref[span].astype(jnp.float32)
        pieces[part][...] = total.astype(jnp.bfloat16)


def close(query_grads, parts):
    rows = query_grads[0].shape[0] // parts
    return pl.pallas_call(
        functools.partial(close_kernel, parts),
        out_shape=[jax.ShapeDtypeStruct((rows, HD), jnp.bfloat16)] * parts,
        compiler_params=params(),
        cost_estimate=COST,
    )(*query_grads)


def unpack_kernel(parts, rows, heads, stages, *refs):
    count = parts * len(stages)
    pieces, outs, semaphores = refs[:count], refs[count:-1], refs[-1]
    pairs = []
    for number, blocks in enumerate(stages):
        for distance in range(parts):
            piece = pieces[number * parts + distance]
            for index, (output, head) in enumerate(blocks):
                columns = pl.ds(column_of(distance, heads, head), HD)
                pairs.append((piece.at[index * rows : (index + 1) * rows], outs[output].at[:, columns]))
    run_copies(pairs, semaphores)


def unpack(stages, pieces, rows, heads):
    parts = len(pieces[0])
    whole = pl.BlockSpec(memory_space=pl.ANY)
    channels = parts * heads * HD
    return pl.pallas_call(
        functools.partial(unpack_kernel, parts, rows, heads, stages),
        in_specs=[whole] * (parts * len(stages)),
        out_specs=[whole] * 3,
        out_shape=[jax.ShapeDtypeStruct((rows, channels), jnp.bfloat16)] * 3,
        scratch_shapes=[pltpu.SemaphoreType.DMA((3 * heads * parts,))],
        compiler_params=params(),
        cost_estimate=COST,
    )(*[piece for stage in pieces for piece in stage])


def swap(value, axis, distance):
    return lax.ppermute(value, axis, [(index, index ^ distance) for index in range(lax.axis_size(axis))])


def swap_pieces(pieces):
    return [pieces[0]] + [swap(piece, "ulysses", distance) for distance, piece in enumerate(pieces) if distance]


def sum_steps(axes):
    steps = []
    for axis in axes:
        size = lax.axis_size(axis)
        if size & (size - 1):
            steps.append(functools.partial(lax.psum, axis_name=axis))
            continue
        distance = 1
        while distance < size:
            steps.append(lambda value, axis=axis, distance=distance: value + swap(value, axis, distance))
            distance *= 2
    return steps


def after(values, *earlier):
    return lax.optimization_barrier((list(values), earlier))[0]


def neighbours(size):
    if size == 1:
        return []
    if size == 2:
        swapped = [(0, 1), (1, 0)]
        return [(swapped, swapped)]
    up = [(index, index + 1) for index in range(size - 1)]
    down = [(index + 1, index) for index in range(size - 1)]
    return [(up, down), (down, up)]


def exchange_totals(partial, sides):
    if not sides:
        return partial
    if len(sides) == 1:
        other = lax.ppermute(jnp.concatenate(partial), "tm", sides[0][0])
        heads = partial[0].shape[0]
        return [join_totals([partial[0], other[heads:]]), join_totals([partial[1], other[:heads]])]
    position = lax.axis_index("tm")
    present = [position < lax.axis_size("tm") - 1, position > 0]
    values = [partial[0]]
    for value, (_, back), flag in zip(partial[1:], sides, present):
        values.append(jnp.where(flag, lax.ppermute(value, "tm", back), -jnp.inf))
    own = join_totals(values)
    return [own] + [lax.ppermute(own, "tm", there) for there, _ in sides]


def local(queries, keys, values, attn_out, out_grad, out_gain):
    parts = lax.axis_size("ulysses")
    span = lax.axis_size("tm")
    rows, channels = queries.shape[1:]
    heads = channels // (parts * HD)
    rest = list(range(1, heads))
    dots = dots_depth(rows, heads)
    every = list(range(parts))
    sides = neighbours(span)

    def forward(array):
        return [lax.ppermute(array, "tm", there) for there, _ in sides]

    with jax.named_scope("keys_queries"):
        packed = pack([keys[0], queries[0]], parts, list(range(heads)))
        pairs = swap_pieces(packed)
    with jax.named_scope("grads"):
        out_grad = after([out_grad], packed[0])[0]
        sent_lead, sent_rest, gain_part = pack_grads(out_grad[0], attn_out[0], values[0], out_gain, parts)
    token_count = rows * span * parts * lax.axis_size("dp")
    gain = gain_part.reshape(-1, LANES)
    steps = sum_steps(("tm", "dp", "ulysses"))

    def advance(value, count=1):
        with jax.named_scope("gain"):
            for step in steps[:count]:
                value = step(value)
        del steps[:count]
        return value

    gain = advance(gain, max(1, len(steps) - 4))
    with jax.named_scope("halo_queries"):
        width = heads * rows
        first_side = forward(pairs[0][width:])
        late = after(pairs[1:], gain, first_side)
        late_side = forward(gather_rows(late, [(number, width, width) for number in range(parts - 1)]))
    with jax.named_scope("first_grads"):
        lead = swap_pieces(after(sent_lead, late))
    with jax.named_scope("halo_first_grads"):
        ranges = [(part, 0, rows) for part in every] + [(part, 2 * rows, dots) for part in every]
        lead_side = forward(gather_rows(lead, ranges))
    with jax.named_scope("totals"):
        key_places = [[(piece, head) for piece in pairs] for head in range(heads)]
        query_places = [[[(piece, heads + head) for piece in pairs] for head in range(heads)]]
        for first, others in zip(first_side, late_side):
            query_places.append(
                [
                    [(first, head)] + [(others, (part - 1) * heads + head) for part in every[1:]]
                    for head in range(heads)
                ]
            )
        part_totals = partial_totals(key_places, query_places, rows)
        totals = exchange_totals(part_totals, sides)
    gain = advance(after([gain], late)[0], 2)
    with jax.named_scope("rest_grads"):
        rest_grads = swap_pieces(after(sent_rest, lead, gain))
    with jax.named_scope("halo_rest_grads"):
        ranges = [(part, place * rows, rows) for place in range(heads - 1) for part in every]
        rest_side = forward(gather_rows(rest_grads, ranges))
    with jax.named_scope("rest_values"):
        rest_values = swap_pieces(after(pack([values[0]], parts, rest), rest_grads, part_totals))
    dot_places = [(piece, 2 * rows // dots) for piece in lead]
    dot_places += [(array, parts * rows // dots + part) for array in lead_side for part in every]
    stages, pieces, open_grads = [], [], []
    gate = rest_values[1:]
    for head in range(heads):
        if head == 0:
            value_places = [(piece, 1) for piece in lead]
            grad_places = [(piece, 0) for piece in lead] + [(array, part) for array in lead_side for part in every]
        else:
            value_places = [(piece, head - 1) for piece in rest_values]
            grad_places = [(piece, head - 1) for piece in rest_grads]
            grad_places += [(array, (head - 1) * parts + part) for array in rest_side for part in every]
        final = head == heads - 1
        before = open_grads if head else ()
        with jax.named_scope("attention_%d" % head):
            leaving, query_grads = attention(
                head,
                heads,
                rows,
                key_places[head],
                value_places,
                [place for source in query_places for place in source[head]],
                grad_places,
                dot_places,
                totals,
                before,
            )
        stages.append([(1, head), (2, head)] + ([(0, head - 1)] if before else []))
        leaving, query_grads = lax.optimization_barrier((leaving, query_grads, gate))[:2]
        with jax.named_scope("halo_query_grads_%d" % head):
            back_grads = [lax.ppermute(other, "tm", back) for other, (_, back) in zip(query_grads[1:], sides)]
            open_grads = list(query_grads[:1]) + back_grads
        with jax.named_scope("returns_%d" % head):
            pieces.append(swap_pieces(leaving))
        gate = pieces[-1][1:]
        if not final:
            ready = after([gain], gate)[0]
            if head:
                gate = gate + [gain]
            gain = advance(ready)
    with jax.named_scope("returns_last"):
        stages.append([(0, heads - 1)])
        pieces.append(swap_pieces(close(open_grads, parts)))
    result = unpack(stages, pieces, rows, heads)
    gain = advance(gain, len(steps)).reshape(channels) / token_count
    return tuple(grad[None] for grad in result) + (gain,)


def solution(mesh):
    split = P("dp", ("tm", "ulysses"), None)
    return jax.shard_map(
        local,
        mesh=mesh,
        in_specs=(split,) * 5 + (P(),),
        out_specs=(split,) * 3 + (P(),),
        check_vma=False,
    )
```

```python
import functools
import math

import jax
import jax.numpy as jnp
from jax import lax
from jax.experimental import pallas as pl
from jax.experimental.pallas import tpu as pltpu
from jax.sharding import PartitionSpec as P

HD = 128
LANES = 128
TILE_ROWS = 16
KEY_BLOCK = 256
QUERY_BLOCK = 256
VMEM_LIMIT = 48 * 1024 * 1024
SCALE = 1.0 / math.sqrt(HD)
SCALE_LOG2 = SCALE / math.log(2.0)
COST = pl.CostEstimate(flops=1, bytes_accessed=1, transcendentals=0)


def params():
    return pltpu.CompilerParams(vmem_limit_bytes=VMEM_LIMIT)


def partner(distance):
    return lax.axis_index("ulysses") ^ distance


def column_of(distance, heads, head):
    return pl.multiple_of((partner(distance) * heads + head) * HD, HD)


def run_copies(pairs, semaphores):
    copies = [
        pltpu.make_async_copy(source, target, semaphores.at[index]) for index, (source, target) in enumerate(pairs)
    ]
    for copy in copies:
        copy.start()
    for copy in copies:
        copy.wait()


def pack_kernel(parts, chosen, *refs):
    sources, pieces, semaphores = refs[: -parts - 1], refs[-parts - 1 : -1], refs[-1]
    rows, channels = sources[0].shape
    heads = channels // (parts * HD)
    pairs = []
    for distance in range(parts):
        for half, ref in enumerate(sources):
            for place, head in enumerate(chosen):
                columns = pl.ds(column_of(distance, heads, head), HD)
                start = (half * len(chosen) + place) * rows
                pairs.append((ref.at[:, columns], pieces[distance].at[start : start + rows]))
    run_copies(pairs, semaphores)


def pack(sources, parts, chosen):
    rows = sources[0].shape[0]
    depth = len(sources) * len(chosen) * rows
    whole = pl.BlockSpec(memory_space=pl.ANY)
    return pl.pallas_call(
        functools.partial(pack_kernel, parts, chosen),
        in_specs=[whole] * len(sources),
        out_specs=[whole] * parts,
        out_shape=[jax.ShapeDtypeStruct((depth, HD), sources[0].dtype)] * parts,
        scratch_shapes=[pltpu.SemaphoreType.DMA((len(sources) * len(chosen) * parts,))],
        compiler_params=params(),
        cost_estimate=COST,
    )(*sources)


def gather_kernel(ranges, *refs):
    arrays, out_ref, semaphores = refs[:-2], refs[-2], refs[-1]
    pairs = []
    place = 0
    for number, first, count in ranges:
        pairs.append((arrays[number].at[first : first + count], out_ref.at[place : place + count]))
        place += count
    run_copies(pairs, semaphores)


def gather_rows(arrays, ranges):
    whole = pl.BlockSpec(memory_space=pl.ANY)
    depth = sum(count for _, _, count in ranges)
    return pl.pallas_call(
        functools.partial(gather_kernel, ranges),
        in_specs=[whole] * len(arrays),
        out_specs=whole,
        out_shape=jax.ShapeDtypeStruct((depth, HD), arrays[0].dtype),
        scratch_shapes=[pltpu.SemaphoreType.DMA((len(ranges),))],
        compiler_params=params(),
        cost_estimate=COST,
    )(*arrays)


def dot_groups(rows):
    return -(-rows // LANES)


def dots_depth(rows, heads):
    return -(-2 * heads * dot_groups(rows) // TILE_ROWS) * TILE_ROWS


def pack_grads_kernel(parts, out_grad_ref, attn_ref, value_ref, gain_ref, *refs):
    leads, rests, gain_part_ref = refs[:parts], refs[parts:-1], refs[-1]
    rows, channels = out_grad_ref.shape
    heads = channels // (parts * HD)
    for distance in range(parts):
        terms = []
        for head in range(heads):
            columns = pl.ds(column_of(distance, heads, head), HD)
            out_grad = out_grad_ref[:, columns].astype(jnp.float32)
            attn = attn_ref[:, columns].astype(jnp.float32)
            grad = (out_grad * gain_ref[:, columns]).astype(jnp.bfloat16)
            gain_part_ref[:, columns] = jnp.sum(out_grad * attn, axis=0, keepdims=True)
            if head:
                rests[distance][(head - 1) * rows : head * rows] = grad
            else:
                leads[distance][:rows] = grad
                leads[distance][rows : 2 * rows] = value_ref[:, columns]
            dots = jnp.sum(jnp.transpose(grad.astype(jnp.float32) * attn), axis=0, keepdims=True)
            for first in range(0, rows, LANES):
                value = dots[:, first : first + LANES]
                if value.shape[1] < LANES:
                    rest = jnp.zeros((1, LANES - value.shape[1]), jnp.float32)
                    value = jnp.concatenate([value, rest], axis=1)
                high = value.astype(jnp.bfloat16).astype(jnp.float32)
                terms += [high, value - high]
        rest = dots_depth(rows, heads) - len(terms)
        if rest:
            terms.append(jnp.zeros((rest, LANES), jnp.float32))
        leads[distance][2 * rows :] = jnp.concatenate(terms, axis=0).astype(jnp.bfloat16)


def pack_grads(out_grad, attn_out, values, out_gain, parts):
    rows, channels = out_grad.shape
    heads = channels // (parts * HD)
    lead = jax.ShapeDtypeStruct((2 * rows + dots_depth(rows, heads), HD), jnp.bfloat16)
    rest = jax.ShapeDtypeStruct(((heads - 1) * rows, HD), jnp.bfloat16)
    outs = pl.pallas_call(
        functools.partial(pack_grads_kernel, parts),
        out_shape=[lead] * parts + [rest] * parts + [jax.ShapeDtypeStruct((1, channels), jnp.float32)],
        compiler_params=params(),
        cost_estimate=COST,
    )(out_grad, attn_out, values, out_gain.reshape(1, channels))
    return outs[:parts], outs[parts : 2 * parts], outs[2 * parts]


def stacked(refs):
    return jnp.concatenate([ref[...] for ref in refs], axis=0)


def block_specs(depth, places):
    def block(index):
        return pl.BlockSpec((depth, HD), lambda step: (index, 0))

    return [block(index) for _, index in places], [array for array, _ in places]


def totals_kernel(parts, sources, heads, *refs):
    key_refs, refs = refs[: parts * heads], refs[parts * heads :]
    query_refs, refs = refs[: parts * heads * sources], refs[parts * heads * sources :]
    outs, score_ref = refs[:sources], refs[sources]
    slab = score_ref.shape[0]
    for head in range(heads):
        keys = stacked(key_refs[head * parts : (head + 1) * parts])
        for source in range(sources):
            start = (source * heads + head) * parts
            flip = jnp.transpose(stacked(query_refs[start : start + parts]))
            top = None
            for first in range(0, slab, KEY_BLOCK):
                scores = jnp.dot(keys[first : first + KEY_BLOCK], flip, preferred_element_type=jnp.float32)
                score_ref[first : first + KEY_BLOCK] = scores
                part_top = jnp.max(scores.reshape(-1, 8, slab), axis=0)
                top = part_top if top is None else jnp.maximum(top, part_top)
            top = jnp.max(top, axis=0, keepdims=True) * SCALE_LOG2
            total = None
            for first in range(0, slab, KEY_BLOCK):
                powers = jnp.exp2(score_ref[first : first + KEY_BLOCK] * SCALE_LOG2 - top)
                part_total = jnp.sum(powers.reshape(-1, 8, slab), axis=0)
                total = part_total if total is None else total + part_total
            total = jnp.sum(total, axis=0, keepdims=True)
            outs[source][head : head + 1] = top + jnp.log(total) * (1.0 / math.log(2.0))


def partial_totals(keys, queries, rows):
    heads, parts, sources = len(keys), len(keys[0]), len(queries)
    slab = parts * rows
    places = [place for head in keys for place in head]
    places += [place for source in queries for head in source for place in head]
    in_specs, operands = block_specs(rows, places)
    line = pl.BlockSpec((heads, slab), lambda step: (0, 0))
    return pl.pallas_call(
        functools.partial(totals_kernel, parts, sources, heads),
        grid=(1,),
        in_specs=in_specs,
        out_specs=[line] * sources,
        out_shape=[jax.ShapeDtypeStruct((heads, slab), jnp.float32)] * sources,
        scratch_shapes=[pltpu.VMEM((slab, slab), jnp.float32)],
        compiler_params=params(),
        cost_estimate=pl.CostEstimate(
            flops=2 * heads * sources * slab * slab * HD,
            bytes_accessed=heads * sources * slab * HD * 4,
            transcendentals=heads * sources * slab * slab,
        ),
    )(*operands)


def join_totals(values):
    top = functools.reduce(jnp.maximum, values)
    return top + jnp.log2(functools.reduce(jnp.add, [jnp.exp2(value - top) for value in values]))


def attention_kernel(parts, sources, head, rows, before, *refs):
    slab = parts * rows

    def take(count):
        nonlocal refs
        taken, refs = refs[:count], refs[count:]
        return taken

    key_refs, value_refs = take(parts), take(parts)
    query_refs, grad_refs, dots_refs = take(parts * sources), take(parts * sources), take(parts * sources)
    total_refs = take(sources)
    before_refs = take(sources) if before else ()
    piece_refs, query_grad_refs = take(parts), take(sources)
    weight_ref, score_ref = refs
    if before:
        closed = before_refs[0][...]
        for ref in before_refs[1:]:
            closed = closed + ref[...].astype(jnp.float32)
        closed = closed.astype(jnp.bfloat16)
        for part in range(parts):
            piece_refs[part][2 * rows :] = closed[part * rows : (part + 1) * rows]
    keys, values, queries, grads = stacked(key_refs), stacked(value_refs), stacked(query_refs), stacked(grad_refs)
    query_flip, grad_flip = jnp.transpose(queries), jnp.transpose(grads)
    lines = []
    for ref in dots_refs:
        terms = ref[...].astype(jnp.float32)
        for index in range(dot_groups(rows)):
            line = 2 * (head * dot_groups(rows) + index)
            count = min(LANES, rows - index * LANES)
            lines.append((terms[line : line + 1] + terms[line + 1 : line + 2])[:, :count])
    dots = jnp.concatenate(lines, axis=1)
    totals = jnp.concatenate([ref[head : head + 1] for ref in total_refs], axis=1)
    width = sources * slab
    for first in range(0, slab, KEY_BLOCK):
        stretch = slice(first, first + KEY_BLOCK)
        for start in range(0, width, QUERY_BLOCK):
            span = slice(start, start + QUERY_BLOCK)
            scores = jnp.dot(keys[stretch], query_flip[:, span], preferred_element_type=jnp.float32)
            weights = jnp.exp2(scores * SCALE_LOG2 - totals[:, span])
            grad_weights = jnp.dot(values[stretch], grad_flip[:, span], preferred_element_type=jnp.float32)
            weight_ref[stretch, span] = weights.astype(jnp.bfloat16)
            score_ref[stretch, span] = (weights * (grad_weights - dots[:, span])).astype(jnp.bfloat16)
        value_grad = jnp.dot(weight_ref[stretch], grads, preferred_element_type=jnp.float32)
        key_grad = jnp.dot(score_ref[stretch], queries, preferred_element_type=jnp.float32) * SCALE
        key_grad, value_grad = key_grad.astype(jnp.bfloat16), value_grad.astype(jnp.bfloat16)
        for part in range(parts):
            low, high = max(first, part * rows), min(first + KEY_BLOCK, (part + 1) * rows)
            if low < high:
                place = low - part * rows
                piece_refs[part][place : place + high - low] = key_grad[low - first : high - first]
                piece_refs[part][rows + place : rows + place + high - low] = value_grad[low - first : high - first]
    for source in range(sources):
        query_grad = lax.dot_general(
            score_ref[:, source * slab : (source + 1) * slab],
            keys,
            (((0,), (0,)), ((), ())),
            preferred_element_type=jnp.float32,
        )
        query_grad_refs[source][...] = (query_grad * SCALE).astype(query_grad_refs[source].dtype)


def attention(head, heads, rows, keys, values, queries, grads, dots, totals, before):
    parts = len(keys)
    sources = len(totals)
    slab = parts * rows
    in_specs, operands = block_specs(rows, keys + values + queries + grads)
    dot_specs, dot_arrays = block_specs(dots_depth(rows, heads), dots)
    before_specs, before_arrays = block_specs(slab, [(array, 0) for array in before])
    line = pl.BlockSpec((heads, slab), lambda step: (0, 0))
    depth = (3 if before else 2) * rows
    out_specs, _ = block_specs(depth, [(None, 0)] * parts)
    query_specs, _ = block_specs(slab, [(None, 0)] * sources)
    outs = pl.pallas_call(
        functools.partial(attention_kernel, parts, sources, head, rows, bool(before)),
        grid=(1,),
        in_specs=in_specs + dot_specs + [line] * sources + before_specs,
        out_specs=out_specs + query_specs,
        out_shape=[jax.ShapeDtypeStruct((depth, HD), jnp.bfloat16)] * parts
        + [jax.ShapeDtypeStruct((slab, HD), jnp.float32)]
        + [jax.ShapeDtypeStruct((slab, HD), jnp.bfloat16)] * (sources - 1),
        scratch_shapes=[pltpu.VMEM((slab, sources * slab), jnp.bfloat16)] * 2,
        compiler_params=params(),
        cost_estimate=pl.CostEstimate(
            flops=10 * slab * sources * slab * HD,
            bytes_accessed=32 * slab * HD,
            transcendentals=slab * sources * slab,
        ),
    )(*operands, *dot_arrays, *totals, *before_arrays)
    return outs[:parts], outs[parts:]


def close_kernel(parts, *refs):
    own_ref, side_refs, pieces = refs[0], refs[1:-parts], refs[-parts:]
    rows = pieces[0].shape[0]
    for part in range(parts):
        span = slice(part * rows, (part + 1) * rows)
        total = own_ref[span]
        for ref in side_refs:
            total = total + ref[span].astype(jnp.float32)
        pieces[part][...] = total.astype(jnp.bfloat16)


def close(query_grads, parts):
    rows = query_grads[0].shape[0] // parts
    return pl.pallas_call(
        functools.partial(close_kernel, parts),
        out_shape=[jax.ShapeDtypeStruct((rows, HD), jnp.bfloat16)] * parts,
        compiler_params=params(),
        cost_estimate=COST,
    )(*query_grads)


def unpack_kernel(parts, rows, heads, stages, *refs):
    count = parts * len(stages)
    pieces, outs, semaphores = refs[:count], refs[count:-1], refs[-1]
    pairs = []
    for number, blocks in enumerate(stages):
        for distance in range(parts):
            piece = pieces[number * parts + distance]
            for index, (output, head) in enumerate(blocks):
                columns = pl.ds(column_of(distance, heads, head), HD)
                pairs.append((piece.at[index * rows : (index + 1) * rows], outs[output].at[:, columns]))
    run_copies(pairs, semaphores)


def unpack(stages, pieces, rows, heads):
    parts = len(pieces[0])
    whole = pl.BlockSpec(memory_space=pl.ANY)
    channels = parts * heads * HD
    return pl.pallas_call(
        functools.partial(unpack_kernel, parts, rows, heads, stages),
        in_specs=[whole] * (parts * len(stages)),
        out_specs=[whole] * 3,
        out_shape=[jax.ShapeDtypeStruct((rows, channels), jnp.bfloat16)] * 3,
        scratch_shapes=[pltpu.SemaphoreType.DMA((3 * heads * parts,))],
        compiler_params=params(),
        cost_estimate=COST,
    )(*[piece for stage in pieces for piece in stage])


def swap(value, axis, distance):
    return lax.ppermute(value, axis, [(index, index ^ distance) for index in range(lax.axis_size(axis))])


def swap_pieces(pieces, earlier=None):
    held = [pieces[0]]
    for distance in range(1, len(pieces)):
        piece = pieces[distance]
        if earlier is not None:
            piece = after([piece], earlier[distance])[0]
        held.append(swap(piece, "ulysses", distance))
    return held


def sum_steps(axes):
    steps = []
    for axis in axes:
        size = lax.axis_size(axis)
        if size & (size - 1):
            steps.append(functools.partial(lax.psum, axis_name=axis))
            continue
        distance = 1
        while distance < size:
            steps.append(lambda value, axis=axis, distance=distance: value + swap(value, axis, distance))
            distance *= 2
    return steps


def after(values, *earlier):
    return lax.optimization_barrier((list(values), earlier))[0]


def neighbours(size):
    if size == 1:
        return []
    if size == 2:
        swapped = [(0, 1), (1, 0)]
        return [(swapped, swapped)]
    up = [(index, index + 1) for index in range(size - 1)]
    down = [(index + 1, index) for index in range(size - 1)]
    return [(up, down), (down, up)]


def exchange_totals(partial, sides):
    if not sides:
        return partial
    if len(sides) == 1:
        other = lax.ppermute(jnp.concatenate(partial), "tm", sides[0][0])
        heads = partial[0].shape[0]
        return [join_totals([partial[0], other[heads:]]), join_totals([partial[1], other[:heads]])]
    position = lax.axis_index("tm")
    present = [position < lax.axis_size("tm") - 1, position > 0]
    values = [partial[0]]
    for value, (_, back), flag in zip(partial[1:], sides, present):
        values.append(jnp.where(flag, lax.ppermute(value, "tm", back), -jnp.inf))
    own = join_totals(values)
    return [own] + [lax.ppermute(own, "tm", there) for there, _ in sides]


def local(queries, keys, values, attn_out, out_grad, out_gain):
    parts = lax.axis_size("ulysses")
    span = lax.axis_size("tm")
    rows, channels = queries.shape[1:]
    heads = channels // (parts * HD)
    rest = list(range(1, heads))
    dots = dots_depth(rows, heads)
    every = list(range(parts))
    sides = neighbours(span)

    def forward(array):
        return [lax.ppermute(array, "tm", there) for there, _ in sides]

    with jax.named_scope("keys_queries"):
        packed = pack([keys[0], queries[0]], parts, list(range(heads)))
        pairs = swap_pieces(packed)
    with jax.named_scope("grads"):
        out_grad = after([out_grad], packed[0])[0]
        sent_lead, sent_rest, gain_part = pack_grads(out_grad[0], attn_out[0], values[0], out_gain, parts)
    token_count = rows * span * parts * lax.axis_size("dp")
    gain = gain_part.reshape(-1, LANES)
    steps = sum_steps(("tm", "dp", "ulysses"))

    def advance(value, count=1):
        with jax.named_scope("gain"):
            for step in steps[:count]:
                value = step(value)
        del steps[:count]
        return value

    gain = advance(gain, max(1, len(steps) - 4))
    with jax.named_scope("halo_queries"):
        width = heads * rows
        first_side = forward(pairs[0][width:])
        late = after(pairs[1:], gain, first_side)
        late_side = forward(gather_rows(late, [(number, width, width) for number in range(parts - 1)]))
    with jax.named_scope("first_grads"):
        lead = swap_pieces(sent_lead, pairs)
    with jax.named_scope("halo_first_grads"):
        ranges = [(part, 0, rows) for part in every] + [(part, 2 * rows, dots) for part in every]
        lead_side = forward(gather_rows(lead, ranges))
    with jax.named_scope("totals"):
        key_places = [[(piece, head) for piece in pairs] for head in range(heads)]
        query_places = [[[(piece, heads + head) for piece in pairs] for head in range(heads)]]
        for first, others in zip(first_side, late_side):
            query_places.append(
                [
                    [(first, head)] + [(others, (part - 1) * heads + head) for part in every[1:]]
                    for head in range(heads)
                ]
            )
        part_totals = partial_totals(key_places, query_places, rows)
        totals = exchange_totals(part_totals, sides)
    gain = advance(after([gain], late)[0], 2)
    with jax.named_scope("rest_grads"):
        rest_grads = swap_pieces(after(sent_rest, gain), lead)
    with jax.named_scope("halo_rest_grads"):
        ranges = [(part, place * rows, rows) for place in range(heads - 1) for part in every]
        rest_side = forward(gather_rows(rest_grads, ranges))
    with jax.named_scope("rest_values"):
        rest_values = swap_pieces(after(pack([values[0]], parts, rest), part_totals), rest_grads)
    dot_places = [(piece, 2 * rows // dots) for piece in lead]
    dot_places += [(array, parts * rows // dots + part) for array in lead_side for part in every]
    stages, pieces, open_grads = [], [], []
    gate = rest_values
    for head in range(heads):
        if head == 0:
            value_places = [(piece, 1) for piece in lead]
            grad_places = [(piece, 0) for piece in lead] + [(array, part) for array in lead_side for part in every]
        else:
            value_places = [(piece, head - 1) for piece in rest_values]
            grad_places = [(piece, head - 1) for piece in rest_grads]
            grad_places += [(array, (head - 1) * parts + part) for array in rest_side for part in every]
        final = head == heads - 1
        before = open_grads if head else ()
        with jax.named_scope("attention_%d" % head):
            leaving, query_grads = attention(
                head,
                heads,
                rows,
                key_places[head],
                value_places,
                [place for source in query_places for place in source[head]],
                grad_places,
                dot_places,
                totals,
                before,
            )
        stages.append([(1, head), (2, head)] + ([(0, head - 1)] if before else []))
        query_grads = after(query_grads, gate[-1])
        with jax.named_scope("halo_query_grads_%d" % head):
            back_grads = [lax.ppermute(other, "tm", back) for other, (_, back) in zip(query_grads[1:], sides)]
            open_grads = list(query_grads[:1]) + back_grads
        with jax.named_scope("returns_%d" % head):
            pieces.append(swap_pieces(leaving, gate))
        gate = pieces[-1]
        if not final:
            gain = advance(after([gain], gate[-1])[0])
    with jax.named_scope("returns_last"):
        stages.append([(0, heads - 1)])
        pieces.append(swap_pieces(close(open_grads, parts)))
    result = unpack(stages, pieces, rows, heads)
    gain = advance(gain, len(steps)).reshape(channels) / token_count
    return tuple(grad[None] for grad in result) + (gain,)


def solution(mesh):
    split = P("dp", ("tm", "ulysses"), None)
    return jax.shard_map(
        local,
        mesh=mesh,
        in_specs=(split,) * 5 + (P(),),
        out_specs=(split,) * 3 + (P(),),
        check_vma=False,
    )
```

```python
import functools
import math

import jax
import jax.numpy as jnp
from jax import lax
from jax.experimental import pallas as pl
from jax.experimental.pallas import tpu as pltpu
from jax.sharding import PartitionSpec as P

HD = 128
LANES = 128
TILE_ROWS = 16
KEY_BLOCK = 256
QUERY_BLOCK = 256
VMEM_LIMIT = 48 * 1024 * 1024
SCALE = 1.0 / math.sqrt(HD)
SCALE_LOG2 = SCALE / math.log(2.0)
COST = pl.CostEstimate(flops=1, bytes_accessed=1, transcendentals=0)


def params():
    return pltpu.CompilerParams(vmem_limit_bytes=VMEM_LIMIT)


def partner(distance):
    return lax.axis_index("ulysses") ^ distance


def column_of(distance, heads, head):
    return pl.multiple_of((partner(distance) * heads + head) * HD, HD)


def run_copies(pairs, semaphores):
    copies = [
        pltpu.make_async_copy(source, target, semaphores.at[index]) for index, (source, target) in enumerate(pairs)
    ]
    for copy in copies:
        copy.start()
    for copy in copies:
        copy.wait()


def pack_kernel(parts, chosen, *refs):
    sources, pieces, semaphores = refs[: -parts - 1], refs[-parts - 1 : -1], refs[-1]
    rows, channels = sources[0].shape
    heads = channels // (parts * HD)
    pairs = []
    for distance in range(parts):
        for half, ref in enumerate(sources):
            for place, head in enumerate(chosen):
                columns = pl.ds(column_of(distance, heads, head), HD)
                start = (half * len(chosen) + place) * rows
                pairs.append((ref.at[:, columns], pieces[distance].at[start : start + rows]))
    run_copies(pairs, semaphores)


def pack(sources, parts, chosen):
    rows = sources[0].shape[0]
    depth = len(sources) * len(chosen) * rows
    whole = pl.BlockSpec(memory_space=pl.ANY)
    return pl.pallas_call(
        functools.partial(pack_kernel, parts, chosen),
        in_specs=[whole] * len(sources),
        out_specs=[whole] * parts,
        out_shape=[jax.ShapeDtypeStruct((depth, HD), sources[0].dtype)] * parts,
        scratch_shapes=[pltpu.SemaphoreType.DMA((len(sources) * len(chosen) * parts,))],
        compiler_params=params(),
        cost_estimate=COST,
    )(*sources)


def gather_kernel(ranges, *refs):
    arrays, out_ref, semaphores = refs[:-2], refs[-2], refs[-1]
    pairs = []
    place = 0
    for number, first, count in ranges:
        if number is not None:
            pairs.append((arrays[number].at[first : first + count], out_ref.at[place : place + count]))
        place += count
    run_copies(pairs, semaphores)


def gather_rows(arrays, ranges):
    whole = pl.BlockSpec(memory_space=pl.ANY)
    depth = sum(count for _, _, count in ranges)
    return pl.pallas_call(
        functools.partial(gather_kernel, ranges),
        in_specs=[whole] * len(arrays),
        out_specs=whole,
        out_shape=jax.ShapeDtypeStruct((depth, HD), arrays[0].dtype),
        scratch_shapes=[pltpu.SemaphoreType.DMA((len(ranges),))],
        compiler_params=params(),
        cost_estimate=COST,
    )(*arrays)


def dot_groups(rows):
    return -(-rows // LANES)


def dots_depth(rows, heads):
    return -(-2 * heads * dot_groups(rows) // TILE_ROWS) * TILE_ROWS


def pack_grads_kernel(parts, out_grad_ref, attn_ref, value_ref, gain_ref, *refs):
    leads, rests, gain_part_ref = refs[:parts], refs[parts:-1], refs[-1]
    rows, channels = out_grad_ref.shape
    heads = channels // (parts * HD)
    for distance in range(parts):
        terms = []
        for head in range(heads):
            columns = pl.ds(column_of(distance, heads, head), HD)
            out_grad = out_grad_ref[:, columns].astype(jnp.float32)
            attn = attn_ref[:, columns].astype(jnp.float32)
            grad = (out_grad * gain_ref[:, columns]).astype(jnp.bfloat16)
            gain_part_ref[:, columns] = jnp.sum(out_grad * attn, axis=0, keepdims=True)
            if head:
                rests[distance][(head - 1) * rows : head * rows] = grad
            else:
                leads[distance][:rows] = grad
                leads[distance][rows : 2 * rows] = value_ref[:, columns]
            dots = jnp.sum(jnp.transpose(grad.astype(jnp.float32) * attn), axis=0, keepdims=True)
            for first in range(0, rows, LANES):
                value = dots[:, first : first + LANES]
                if value.shape[1] < LANES:
                    rest = jnp.zeros((1, LANES - value.shape[1]), jnp.float32)
                    value = jnp.concatenate([value, rest], axis=1)
                high = value.astype(jnp.bfloat16).astype(jnp.float32)
                terms += [high, value - high]
        rest = dots_depth(rows, heads) - len(terms)
        if rest:
            terms.append(jnp.zeros((rest, LANES), jnp.float32))
        leads[distance][2 * rows :] = jnp.concatenate(terms, axis=0).astype(jnp.bfloat16)


def pack_grads(out_grad, attn_out, values, out_gain, parts):
    rows, channels = out_grad.shape
    heads = channels // (parts * HD)
    lead = jax.ShapeDtypeStruct((2 * rows + dots_depth(rows, heads), HD), jnp.bfloat16)
    rest = jax.ShapeDtypeStruct(((heads - 1) * rows, HD), jnp.bfloat16)
    outs = pl.pallas_call(
        functools.partial(pack_grads_kernel, parts),
        out_shape=[lead] * parts + [rest] * parts + [jax.ShapeDtypeStruct((1, channels), jnp.float32)],
        compiler_params=params(),
        cost_estimate=COST,
    )(out_grad, attn_out, values, out_gain.reshape(1, channels))
    return outs[:parts], outs[parts : 2 * parts], outs[2 * parts]


def stacked(refs):
    return jnp.concatenate([ref[...] for ref in refs], axis=0)


def block_specs(depth, places):
    def block(index):
        return pl.BlockSpec((depth, HD), lambda step: (index, 0))

    return [block(index) for _, index in places], [array for array, _ in places]


def totals_kernel(parts, sources, heads, *refs):
    key_refs, refs = refs[: parts * heads], refs[parts * heads :]
    query_refs, refs = refs[: parts * heads * sources], refs[parts * heads * sources :]
    outs, score_ref = refs[:sources], refs[sources]
    slab = score_ref.shape[0]
    for head in range(heads):
        keys = stacked(key_refs[head * parts : (head + 1) * parts])
        for source in range(sources):
            start = (source * heads + head) * parts
            flip = jnp.transpose(stacked(query_refs[start : start + parts]))
            top = None
            for first in range(0, slab, KEY_BLOCK):
                scores = jnp.dot(keys[first : first + KEY_BLOCK], flip, preferred_element_type=jnp.float32)
                score_ref[first : first + KEY_BLOCK] = scores
                part_top = jnp.max(scores.reshape(-1, 8, slab), axis=0)
                top = part_top if top is None else jnp.maximum(top, part_top)
            top = jnp.max(top, axis=0, keepdims=True) * SCALE_LOG2
            total = None
            for first in range(0, slab, KEY_BLOCK):
                powers = jnp.exp2(score_ref[first : first + KEY_BLOCK] * SCALE_LOG2 - top)
                part_total = jnp.sum(powers.reshape(-1, 8, slab), axis=0)
                total = part_total if total is None else total + part_total
            total = jnp.sum(total, axis=0, keepdims=True)
            outs[source][head : head + 1] = top + jnp.log(total) * (1.0 / math.log(2.0))


def partial_totals(keys, queries, rows):
    heads, parts, sources = len(keys), len(keys[0]), len(queries)
    slab = parts * rows
    places = [place for head in keys for place in head]
    places += [place for source in queries for head in source for place in head]
    in_specs, operands = block_specs(rows, places)
    line = pl.BlockSpec((heads, slab), lambda step: (0, 0))
    return pl.pallas_call(
        functools.partial(totals_kernel, parts, sources, heads),
        grid=(1,),
        in_specs=in_specs,
        out_specs=[line] * sources,
        out_shape=[jax.ShapeDtypeStruct((heads, slab), jnp.float32)] * sources,
        scratch_shapes=[pltpu.VMEM((slab, slab), jnp.float32)],
        compiler_params=params(),
        cost_estimate=pl.CostEstimate(
            flops=2 * heads * sources * slab * slab * HD,
            bytes_accessed=heads * sources * slab * HD * 4,
            transcendentals=heads * sources * slab * slab,
        ),
    )(*operands)


def join_totals(values):
    top = functools.reduce(jnp.maximum, values)
    return top + jnp.log2(functools.reduce(jnp.add, [jnp.exp2(value - top) for value in values]))


def attention_kernel(parts, sources, head, rows, before, *refs):
    slab = parts * rows

    def take(count):
        nonlocal refs
        taken, refs = refs[:count], refs[count:]
        return taken

    key_refs, value_refs = take(parts), take(parts)
    query_refs, grad_refs, dots_refs = take(parts * sources), take(parts * sources), take(parts * sources)
    total_refs = take(sources)
    before_refs = take(before)
    piece_refs, query_grad_refs = take(parts), refs[:-2]
    weight_ref, score_ref = refs[-2:]
    if before:
        closed = before_refs[0][...]
        for ref in before_refs[1:]:
            closed = closed + ref[...].astype(jnp.float32)
        closed = closed.astype(jnp.bfloat16)
        for part in range(parts):
            piece_refs[part][2 * rows :] = closed[part * rows : (part + 1) * rows]
    keys, values, queries, grads = stacked(key_refs), stacked(value_refs), stacked(query_refs), stacked(grad_refs)
    query_flip, grad_flip = jnp.transpose(queries), jnp.transpose(grads)
    lines = []
    for ref in dots_refs:
        terms = ref[...].astype(jnp.float32)
        for index in range(dot_groups(rows)):
            line = 2 * (head * dot_groups(rows) + index)
            count = min(LANES, rows - index * LANES)
            lines.append((terms[line : line + 1] + terms[line + 1 : line + 2])[:, :count])
    dots = jnp.concatenate(lines, axis=1)
    totals = jnp.concatenate([ref[head : head + 1] for ref in total_refs], axis=1)
    width = sources * slab
    for first in range(0, slab, KEY_BLOCK):
        stretch = slice(first, first + KEY_BLOCK)
        for start in range(0, width, QUERY_BLOCK):
            span = slice(start, start + QUERY_BLOCK)
            scores = jnp.dot(keys[stretch], query_flip[:, span], preferred_element_type=jnp.float32)
            weights = jnp.exp2(scores * SCALE_LOG2 - totals[:, span])
            grad_weights = jnp.dot(values[stretch], grad_flip[:, span], preferred_element_type=jnp.float32)
            weight_ref[stretch, span] = weights.astype(jnp.bfloat16)
            score_ref[stretch, span] = (weights * (grad_weights - dots[:, span])).astype(jnp.bfloat16)
        value_grad = jnp.dot(weight_ref[stretch], grads, preferred_element_type=jnp.float32)
        key_grad = jnp.dot(score_ref[stretch], queries, preferred_element_type=jnp.float32) * SCALE
        key_grad, value_grad = key_grad.astype(jnp.bfloat16), value_grad.astype(jnp.bfloat16)
        for part in range(parts):
            low, high = max(first, part * rows), min(first + KEY_BLOCK, (part + 1) * rows)
            if low < high:
                place = low - part * rows
                piece_refs[part][place : place + high - low] = key_grad[low - first : high - first]
                piece_refs[part][rows + place : rows + place + high - low] = value_grad[low - first : high - first]
    start = 0
    for ref in query_grad_refs:
        for first in range(0, ref.shape[0], slab):
            query_grad = lax.dot_general(
                score_ref[:, start : start + slab],
                keys,
                (((0,), (0,)), ((), ())),
                preferred_element_type=jnp.float32,
            )
            ref[first : first + slab] = (query_grad * SCALE).astype(ref.dtype)
            start += slab


def attention(head, heads, rows, keys, values, queries, grads, dots, totals, before, query_grads):
    parts = len(keys)
    sources = len(totals)
    slab = parts * rows
    in_specs, operands = block_specs(rows, keys + values + queries + grads)
    dot_specs, dot_arrays = block_specs(dots_depth(rows, heads), dots)
    before_specs, before_arrays = block_specs(slab, [(array, 0) for array in before])
    line = pl.BlockSpec((heads, slab), lambda step: (0, 0))
    depth = (3 if before else 2) * rows
    out_specs, _ = block_specs(depth, [(None, 0)] * parts)
    query_specs = [pl.BlockSpec((count * slab, HD), lambda step: (0, 0)) for count, _ in query_grads]
    outs = pl.pallas_call(
        functools.partial(attention_kernel, parts, sources, head, rows, len(before)),
        grid=(1,),
        in_specs=in_specs + dot_specs + [line] * sources + before_specs,
        out_specs=out_specs + query_specs,
        out_shape=[jax.ShapeDtypeStruct((depth, HD), jnp.bfloat16)] * parts
        + [jax.ShapeDtypeStruct((count * slab, HD), dtype) for count, dtype in query_grads],
        scratch_shapes=[pltpu.VMEM((slab, sources * slab), jnp.bfloat16)] * 2,
        compiler_params=params(),
        cost_estimate=pl.CostEstimate(
            flops=10 * slab * sources * slab * HD,
            bytes_accessed=32 * slab * HD,
            transcendentals=slab * sources * slab,
        ),
    )(*operands, *dot_arrays, *totals, *before_arrays)
    return outs[:parts], outs[parts:]


def close_kernel(parts, *refs):
    own_ref, side_refs, pieces = refs[0], refs[1:-parts], refs[-parts:]
    rows = pieces[0].shape[0]
    for part in range(parts):
        span = slice(part * rows, (part + 1) * rows)
        total = own_ref[span]
        for ref in side_refs:
            total = total + ref[span].astype(jnp.float32)
        pieces[part][...] = total.astype(jnp.bfloat16)


def close(query_grads, parts):
    rows = query_grads[0].shape[0] // parts
    return pl.pallas_call(
        functools.partial(close_kernel, parts),
        out_shape=[jax.ShapeDtypeStruct((rows, HD), jnp.bfloat16)] * parts,
        compiler_params=params(),
        cost_estimate=COST,
    )(*query_grads)


def unpack_kernel(parts, rows, heads, stages, *refs):
    count = parts * len(stages)
    pieces, outs, semaphores = refs[:count], refs[count:-1], refs[-1]
    pairs = []
    for number, blocks in enumerate(stages):
        for distance in range(parts):
            piece = pieces[number * parts + distance]
            for index, (output, head) in enumerate(blocks):
                columns = pl.ds(column_of(distance, heads, head), HD)
                pairs.append((piece.at[index * rows : (index + 1) * rows], outs[output].at[:, columns]))
    run_copies(pairs, semaphores)


def unpack(stages, pieces, rows, heads):
    parts = len(pieces[0])
    whole = pl.BlockSpec(memory_space=pl.ANY)
    channels = parts * heads * HD
    return pl.pallas_call(
        functools.partial(unpack_kernel, parts, rows, heads, stages),
        in_specs=[whole] * (parts * len(stages)),
        out_specs=[whole] * 3,
        out_shape=[jax.ShapeDtypeStruct((rows, channels), jnp.bfloat16)] * 3,
        scratch_shapes=[pltpu.SemaphoreType.DMA((3 * heads * parts,))],
        compiler_params=params(),
        cost_estimate=COST,
    )(*[piece for stage in pieces for piece in stage])


def swap(value, axis, distance):
    return lax.ppermute(value, axis, [(index, index ^ distance) for index in range(lax.axis_size(axis))])


def swap_pieces(pieces, earlier=None):
    held = [pieces[0]]
    for distance in range(1, len(pieces)):
        piece = pieces[distance]
        if earlier is not None:
            piece = after([piece], earlier[distance])[0]
        held.append(swap(piece, "ulysses", distance))
    return held


def sum_steps(axes):
    steps = []
    for axis in axes:
        size = lax.axis_size(axis)
        if size & (size - 1):
            steps.append(functools.partial(lax.psum, axis_name=axis))
            continue
        distance = 1
        while distance < size:
            steps.append(lambda value, axis=axis, distance=distance: value + swap(value, axis, distance))
            distance *= 2
    return steps


def after(values, *earlier):
    return lax.optimization_barrier((list(values), earlier))[0]


def neighbours(size):
    if size == 1:
        return []
    up = [(index, index + 1) for index in range(size - 1)]
    down = [(index + 1, index) for index in range(size - 1)]
    return [(up, down), (down, up)]


def exchange_totals(partial, sides):
    if not sides:
        return partial
    position = lax.axis_index("tm")
    present = [position < lax.axis_size("tm") - 1, position > 0]
    values = [partial[0]]
    for value, (_, back), flag in zip(partial[1:], sides, present):
        values.append(jnp.where(flag, lax.ppermute(value, "tm", back), -jnp.inf))
    own = join_totals(values)
    return [own] + [lax.ppermute(own, "tm", there) for there, _ in sides]


def swap_totals(partial):
    both = jnp.concatenate(partial)
    heads = partial[0].shape[0]
    joined = join_totals([both, swap(both, "tm", 1)])
    return [joined[:heads], joined[heads:]]


def local(queries, keys, values, attn_out, out_grad, out_gain):
    parts = lax.axis_size("ulysses")
    span = lax.axis_size("tm")
    rows, channels = queries.shape[1:]
    heads = channels // (parts * HD)
    rest = list(range(1, heads))
    dots = dots_depth(rows, heads)
    every = list(range(parts))
    paired = span == 2
    sides = neighbours(span)
    slabs = 2 if paired else 1

    def forward(array):
        if paired:
            return [lax.all_gather(array, "tm", axis=0, tiled=True)]
        return [lax.ppermute(array, "tm", there) for there, _ in sides]

    def forwarded(arrays, place):
        return [(array, index * (array.shape[0] // slabs) + place) for array in arrays for index in range(slabs)]

    def placed(arrays, depth, place):
        return [(array, row // depth) for array, row in forwarded(arrays, place)]

    with jax.named_scope("keys_queries"):
        packed = pack([keys[0], queries[0]], parts, list(range(heads)))
        pairs = swap_pieces(packed)
    with jax.named_scope("grads"):
        out_grad = after([out_grad], packed[0])[0]
        sent_lead, sent_rest, gain_part = pack_grads(out_grad[0], attn_out[0], values[0], out_gain, parts)
    token_count = rows * span * parts * lax.axis_size("dp")
    gain = gain_part.reshape(-1, LANES)
    steps = sum_steps(("tm", "dp", "ulysses"))

    def advance(value, count=1):
        with jax.named_scope("gain"):
            for step in steps[:count]:
                value = step(value)
        del steps[:count]
        return value

    gain = advance(gain, max(1, len(steps) - 4))
    with jax.named_scope("halo_queries"):
        width = heads * rows
        first_side = forward(pairs[0][width:])
        late = after(pairs[1:], gain, first_side)
        late_side = forward(gather_rows(late, [(number, width, width) for number in range(parts - 1)]))
    with jax.named_scope("first_grads"):
        lead = swap_pieces(sent_lead, pairs)
    with jax.named_scope("halo_first_grads"):
        ranges = [(part, 0, rows) for part in every] + [(part, 2 * rows, dots) for part in every]
        ranges.append((None, 0, -parts * dots % rows))
        lead_side = forward(gather_rows(lead, ranges))
    with jax.named_scope("totals"):
        key_places = [[(piece, head) for piece in pairs] for head in range(heads)]
        query_places = []
        if not paired:
            query_places.append([[(piece, heads + head) for piece in pairs] for head in range(heads)])
        for source in range(len(first_side) * slabs):
            query_places.append(
                [
                    [placed(first_side, rows, head * rows)[source]]
                    + [placed(late_side, rows, ((part - 1) * heads + head) * rows)[source] for part in every[1:]]
                    for head in range(heads)
                ]
            )
        part_totals = partial_totals(key_places, query_places, rows)
        totals = swap_totals(part_totals) if paired else exchange_totals(part_totals, sides)
    gain = advance(after([gain], late)[0], 2)
    with jax.named_scope("rest_grads"):
        rest_grads = swap_pieces(after(sent_rest, gain), lead)
    with jax.named_scope("halo_rest_grads"):
        ranges = [(part, place * rows, rows) for place in range(heads - 1) for part in every]
        rest_side = forward(gather_rows(rest_grads, ranges))
    with jax.named_scope("rest_values"):
        rest_values = swap_pieces(after(pack([values[0]], parts, rest), part_totals), rest_grads)
    dot_places = [] if paired else [(piece, 2 * rows // dots) for piece in lead]
    for source in range(len(lead_side) * slabs):
        dot_places += [placed(lead_side, dots, parts * rows + part * dots)[source] for part in every]
    query_grad_kinds = [(2, jnp.float32)] if paired else [(1, jnp.float32)] + [(1, jnp.bfloat16)] * len(sides)
    stages, pieces, open_grads = [], [], []
    gate = rest_values
    for head in range(heads):
        if head == 0:
            value_places = [(piece, 1) for piece in lead]
            own_grads, sent, start = lead, lead_side, 0
        else:
            value_places = [(piece, head - 1) for piece in rest_values]
            own_grads, sent, start = rest_grads, rest_side, (head - 1) * parts
        grad_places = [] if paired else [(piece, max(0, head - 1)) for piece in own_grads]
        for source in range(len(sent) * slabs):
            grad_places += [placed(sent, rows, (start + part) * rows)[source] for part in every]
        before = open_grads if head else ()
        with jax.named_scope("attention_%d" % head):
            leaving, query_grads = attention(
                head,
                heads,
                rows,
                key_places[head],
                value_places,
                [place for source in query_places for place in source[head]],
                grad_places,
                dot_places,
                totals,
                before,
                query_grad_kinds,
            )
        stages.append([(1, head), (2, head)] + ([(0, head - 1)] if before else []))
        query_grads = after(query_grads, gate[1:])
        with jax.named_scope("halo_query_grads_%d" % head):
            if paired:
                open_grads = [lax.psum_scatter(query_grads[0], "tm", scatter_dimension=0, tiled=True)]
            else:
                open_grads = [query_grads[0]]
                for other, (_, back) in zip(query_grads[1:], sides):
                    open_grads.append(lax.ppermute(other, "tm", back))
        with jax.named_scope("returns_%d" % head):
            pieces.append(swap_pieces(leaving, gate))
        gate = pieces[-1]
    with jax.named_scope("returns_last"):
        stages.append([(0, heads - 1)])
        pieces.append(swap_pieces(close(open_grads, parts)))
    result = unpack(stages, pieces, rows, heads)
    gain = advance(after([gain], pieces[-3])[0], len(steps)).reshape(channels) / token_count
    return tuple(grad[None] for grad in result) + (gain,)


def solution(mesh):
    split = P("dp", ("tm", "ulysses"), None)
    return jax.shard_map(
        local,
        mesh=mesh,
        in_specs=(split,) * 5 + (P(),),
        out_specs=(split,) * 3 + (P(),),
        check_vma=False,
    )
```

```python
import functools
import math

import jax
import jax.numpy as jnp
from jax import lax
from jax.experimental import pallas as pl
from jax.experimental.pallas import tpu as pltpu
from jax.sharding import PartitionSpec as P

HD = 128
LANES = 128
TILE_ROWS = 16
KEY_BLOCK = 256
QUERY_BLOCK = 256
VMEM_LIMIT = 48 * 1024 * 1024
SCALE = 1.0 / math.sqrt(HD)
SCALE_LOG2 = SCALE / math.log(2.0)
COST = pl.CostEstimate(flops=1, bytes_accessed=1, transcendentals=0)


def params():
    return pltpu.CompilerParams(vmem_limit_bytes=VMEM_LIMIT)


def partner(distance):
    return lax.axis_index("ulysses") ^ distance


def column_of(distance, heads, head):
    return pl.multiple_of((partner(distance) * heads + head) * HD, HD)


def run_copies(pairs, semaphores):
    copies = [
        pltpu.make_async_copy(source, target, semaphores.at[index]) for index, (source, target) in enumerate(pairs)
    ]
    for copy in copies:
        copy.start()
    for copy in copies:
        copy.wait()


def pack_kernel(parts, chosen, *refs):
    sources, pieces, semaphores = refs[: -parts - 1], refs[-parts - 1 : -1], refs[-1]
    rows, channels = sources[0].shape
    heads = channels // (parts * HD)
    pairs = []
    for distance in range(parts):
        for half, ref in enumerate(sources):
            for place, head in enumerate(chosen):
                columns = pl.ds(column_of(distance, heads, head), HD)
                start = (half * len(chosen) + place) * rows
                pairs.append((ref.at[:, columns], pieces[distance].at[start : start + rows]))
    run_copies(pairs, semaphores)


def pack(sources, parts, chosen):
    rows = sources[0].shape[0]
    depth = len(sources) * len(chosen) * rows
    whole = pl.BlockSpec(memory_space=pl.ANY)
    return pl.pallas_call(
        functools.partial(pack_kernel, parts, chosen),
        in_specs=[whole] * len(sources),
        out_specs=[whole] * parts,
        out_shape=[jax.ShapeDtypeStruct((depth, HD), sources[0].dtype)] * parts,
        scratch_shapes=[pltpu.SemaphoreType.DMA((len(sources) * len(chosen) * parts,))],
        compiler_params=params(),
        cost_estimate=COST,
    )(*sources)


def gather_kernel(ranges, *refs):
    arrays, out_ref, semaphores = refs[:-2], refs[-2], refs[-1]
    pairs = []
    place = 0
    for number, first, count in ranges:
        pairs.append((arrays[number].at[first : first + count], out_ref.at[place : place + count]))
        place += count
    run_copies(pairs, semaphores)


def gather_rows(arrays, ranges):
    whole = pl.BlockSpec(memory_space=pl.ANY)
    depth = sum(count for _, _, count in ranges)
    return pl.pallas_call(
        functools.partial(gather_kernel, ranges),
        in_specs=[whole] * len(arrays),
        out_specs=whole,
        out_shape=jax.ShapeDtypeStruct((depth, HD), arrays[0].dtype),
        scratch_shapes=[pltpu.SemaphoreType.DMA((len(ranges),))],
        compiler_params=params(),
        cost_estimate=COST,
    )(*arrays)


def dot_groups(rows):
    return -(-rows // LANES)


def dots_depth(rows, heads):
    return -(-2 * heads * dot_groups(rows) // TILE_ROWS) * TILE_ROWS


def gain_kernel(out_grad_ref, attn_ref, out_ref):
    product = out_grad_ref[...].astype(jnp.float32) * attn_ref[...].astype(jnp.float32)
    out_ref[...] = jnp.sum(product, axis=0, keepdims=True)


def gain_partial(out_grad, attn_out):
    return pl.pallas_call(
        gain_kernel,
        out_shape=jax.ShapeDtypeStruct((1, out_grad.shape[1]), jnp.float32),
        compiler_params=params(),
        cost_estimate=COST,
    )(out_grad, attn_out)


def split_terms(value, count):
    terms = []
    for _ in range(count):
        term = value.astype(jnp.bfloat16).astype(jnp.float32)
        terms.append(term)
        value = value - term
    return terms


def gain_depth(channels):
    return -(-3 * channels // LANES // TILE_ROWS) * TILE_ROWS


def pack_grads_kernel(parts, out_grad_ref, attn_ref, value_ref, gain_ref, partial_ref, *refs):
    leads, rests = refs[:parts], refs[parts:]
    rows, channels = out_grad_ref.shape
    heads = channels // (parts * HD)
    depth = 2 * rows + dots_depth(rows, heads)
    lines = partial_ref.shape[0]
    partial = jnp.concatenate(split_terms(partial_ref[...], 3), axis=0)
    spare = gain_depth(channels) - partial.shape[0]
    if spare:
        partial = jnp.concatenate([partial, jnp.zeros((spare, LANES), jnp.float32)], axis=0)
    for distance in range(parts):
        terms = []
        for head in range(heads):
            columns = pl.ds(column_of(distance, heads, head), HD)
            grad = (out_grad_ref[:, columns].astype(jnp.float32) * gain_ref[:, columns]).astype(jnp.bfloat16)
            if head:
                rests[distance][(head - 1) * rows : head * rows] = grad
            else:
                leads[distance][:rows] = grad
                leads[distance][rows : 2 * rows] = value_ref[:, columns]
            product = grad.astype(jnp.float32) * attn_ref[:, columns].astype(jnp.float32)
            dots = jnp.sum(jnp.transpose(product), axis=0, keepdims=True)
            for first in range(0, rows, LANES):
                value = dots[:, first : first + LANES]
                if value.shape[1] < LANES:
                    rest = jnp.zeros((1, LANES - value.shape[1]), jnp.float32)
                    value = jnp.concatenate([value, rest], axis=1)
                terms += split_terms(value, 2)
        rest = dots_depth(rows, heads) - len(terms)
        if rest:
            terms.append(jnp.zeros((rest, LANES), jnp.float32))
        leads[distance][2 * rows : depth] = jnp.concatenate(terms, axis=0).astype(jnp.bfloat16)
        leads[distance][depth:] = partial.astype(jnp.bfloat16)


def pack_grads(out_grad, attn_out, values, out_gain, partial, parts):
    rows, channels = out_grad.shape
    heads = channels // (parts * HD)
    depth = 2 * rows + dots_depth(rows, heads) + gain_depth(channels)
    lead = jax.ShapeDtypeStruct((depth, HD), jnp.bfloat16)
    rest = jax.ShapeDtypeStruct(((heads - 1) * rows, HD), jnp.bfloat16)
    outs = pl.pallas_call(
        functools.partial(pack_grads_kernel, parts),
        out_shape=[lead] * parts + [rest] * parts,
        compiler_params=params(),
        cost_estimate=COST,
    )(out_grad, attn_out, values, out_gain.reshape(1, channels), partial)
    return outs[:parts], outs[parts:]


def gain_total_kernel(lines, starts, scale, *refs):
    values = []
    for ref, start in zip(refs[:-1], starts):
        terms = [ref[start + index * lines : start + (index + 1) * lines].astype(jnp.float32) for index in range(3)]
        values.append(terms[0] + terms[1] + terms[2])
    refs[-1][...] = tree_sum(values) * scale


def gain_total(places, lines, scale):
    return pl.pallas_call(
        functools.partial(gain_total_kernel, lines, [start for _, start in places], scale),
        out_shape=jax.ShapeDtypeStruct((lines, LANES), jnp.float32),
        compiler_params=params(),
        cost_estimate=COST,
    )(*[array for array, _ in places])


def stacked(refs):
    return jnp.concatenate([ref[...] for ref in refs], axis=0)


def block_specs(depth, places):
    def block(index):
        return pl.BlockSpec((depth, HD), lambda step: (index, 0))

    return [block(index) for _, index in places], [array for array, _ in places]


def totals_kernel(parts, sources, heads, *refs):
    key_refs, refs = refs[: parts * heads], refs[parts * heads :]
    query_refs, refs = refs[: parts * heads * sources], refs[parts * heads * sources :]
    outs, score_ref = refs[:sources], refs[sources]
    slab = score_ref.shape[0]
    for head in range(heads):
        keys = stacked(key_refs[head * parts : (head + 1) * parts])
        for source in range(sources):
            start = (source * heads + head) * parts
            flip = jnp.transpose(stacked(query_refs[start : start + parts]))
            top = None
            for first in range(0, slab, KEY_BLOCK):
                scores = jnp.dot(keys[first : first + KEY_BLOCK], flip, preferred_element_type=jnp.float32)
                score_ref[first : first + KEY_BLOCK] = scores
                part_top = jnp.max(scores.reshape(-1, 8, slab), axis=0)
                top = part_top if top is None else jnp.maximum(top, part_top)
            top = jnp.max(top, axis=0, keepdims=True) * SCALE_LOG2
            total = None
            for first in range(0, slab, KEY_BLOCK):
                powers = jnp.exp2(score_ref[first : first + KEY_BLOCK] * SCALE_LOG2 - top)
                part_total = jnp.sum(powers.reshape(-1, 8, slab), axis=0)
                total = part_total if total is None else total + part_total
            total = jnp.sum(total, axis=0, keepdims=True)
            outs[source][head : head + 1] = top + jnp.log(total) * (1.0 / math.log(2.0))


def partial_totals(keys, queries, rows):
    heads, parts, sources = len(keys), len(keys[0]), len(queries)
    slab = parts * rows
    places = [place for head in keys for place in head]
    places += [place for source in queries for head in source for place in head]
    in_specs, operands = block_specs(rows, places)
    line = pl.BlockSpec((heads, slab), lambda step: (0, 0))
    return pl.pallas_call(
        functools.partial(totals_kernel, parts, sources, heads),
        grid=(1,),
        in_specs=in_specs,
        out_specs=[line] * sources,
        out_shape=[jax.ShapeDtypeStruct((heads, slab), jnp.float32)] * sources,
        scratch_shapes=[pltpu.VMEM((slab, slab), jnp.float32)],
        compiler_params=params(),
        cost_estimate=pl.CostEstimate(
            flops=2 * heads * sources * slab * slab * HD,
            bytes_accessed=heads * sources * slab * HD * 4,
            transcendentals=heads * sources * slab * slab,
        ),
    )(*operands)


def join_totals(values):
    top = functools.reduce(jnp.maximum, values)
    return top + jnp.log2(functools.reduce(jnp.add, [jnp.exp2(value - top) for value in values]))


def attention_kernel(parts, sources, head, rows, before, *refs):
    slab = parts * rows

    def take(count):
        nonlocal refs
        taken, refs = refs[:count], refs[count:]
        return taken

    key_refs, value_refs = take(parts), take(parts)
    query_refs, grad_refs, dots_refs = take(parts * sources), take(parts * sources), take(parts * sources)
    total_refs = take(sources)
    before_refs = take(sources) if before else ()
    piece_refs, query_grad_refs = take(parts), take(sources)
    weight_ref, score_ref = refs
    if before:
        closed = before_refs[0][...]
        for ref in before_refs[1:]:
            closed = closed + ref[...].astype(jnp.float32)
        closed = closed.astype(jnp.bfloat16)
        for part in range(parts):
            piece_refs[part][2 * rows :] = closed[part * rows : (part + 1) * rows]
    keys, values, queries, grads = stacked(key_refs), stacked(value_refs), stacked(query_refs), stacked(grad_refs)
    query_flip, grad_flip = jnp.transpose(queries), jnp.transpose(grads)
    lines = []
    for ref in dots_refs:
        terms = ref[...].astype(jnp.float32)
        for index in range(dot_groups(rows)):
            line = 2 * (head * dot_groups(rows) + index)
            count = min(LANES, rows - index * LANES)
            lines.append((terms[line : line + 1] + terms[line + 1 : line + 2])[:, :count])
    dots = jnp.concatenate(lines, axis=1)
    totals = jnp.concatenate([ref[head : head + 1] for ref in total_refs], axis=1)
    width = sources * slab
    for first in range(0, slab, KEY_BLOCK):
        stretch = slice(first, first + KEY_BLOCK)
        for start in range(0, width, QUERY_BLOCK):
            span = slice(start, start + QUERY_BLOCK)
            scores = jnp.dot(keys[stretch], query_flip[:, span], preferred_element_type=jnp.float32)
            weights = jnp.exp2(scores * SCALE_LOG2 - totals[:, span])
            grad_weights = jnp.dot(values[stretch], grad_flip[:, span], preferred_element_type=jnp.float32)
            weight_ref[stretch, span] = weights.astype(jnp.bfloat16)
            score_ref[stretch, span] = (weights * (grad_weights - dots[:, span])).astype(jnp.bfloat16)
        value_grad = jnp.dot(weight_ref[stretch], grads, preferred_element_type=jnp.float32)
        key_grad = jnp.dot(score_ref[stretch], queries, preferred_element_type=jnp.float32) * SCALE
        key_grad, value_grad = key_grad.astype(jnp.bfloat16), value_grad.astype(jnp.bfloat16)
        for part in range(parts):
            low, high = max(first, part * rows), min(first + KEY_BLOCK, (part + 1) * rows)
            if low < high:
                place = low - part * rows
                piece_refs[part][place : place + high - low] = key_grad[low - first : high - first]
                piece_refs[part][rows + place : rows + place + high - low] = value_grad[low - first : high - first]
    for source in range(sources):
        query_grad = lax.dot_general(
            score_ref[:, source * slab : (source + 1) * slab],
            keys,
            (((0,), (0,)), ((), ())),
            preferred_element_type=jnp.float32,
        )
        query_grad_refs[source][...] = (query_grad * SCALE).astype(query_grad_refs[source].dtype)


def attention(head, heads, rows, keys, values, queries, grads, dots, totals, before):
    parts = len(keys)
    sources = len(totals)
    slab = parts * rows
    in_specs, operands = block_specs(rows, keys + values + queries + grads)
    dot_specs, dot_arrays = block_specs(dots_depth(rows, heads), dots)
    before_specs, before_arrays = block_specs(slab, [(array, 0) for array in before])
    line = pl.BlockSpec((heads, slab), lambda step: (0, 0))
    depth = (3 if before else 2) * rows
    out_specs, _ = block_specs(depth, [(None, 0)] * parts)
    query_specs, _ = block_specs(slab, [(None, 0)] * sources)
    outs = pl.pallas_call(
        functools.partial(attention_kernel, parts, sources, head, rows, bool(before)),
        grid=(1,),
        in_specs=in_specs + dot_specs + [line] * sources + before_specs,
        out_specs=out_specs + query_specs,
        out_shape=[jax.ShapeDtypeStruct((depth, HD), jnp.bfloat16)] * parts
        + [jax.ShapeDtypeStruct((slab, HD), jnp.float32)]
        + [jax.ShapeDtypeStruct((slab, HD), jnp.bfloat16)] * (sources - 1),
        scratch_shapes=[pltpu.VMEM((slab, sources * slab), jnp.bfloat16)] * 2,
        compiler_params=params(),
        cost_estimate=pl.CostEstimate(
            flops=10 * slab * sources * slab * HD,
            bytes_accessed=32 * slab * HD,
            transcendentals=slab * sources * slab,
        ),
    )(*operands, *dot_arrays, *totals, *before_arrays)
    return outs[:parts], outs[parts:]


def close_kernel(parts, *refs):
    own_ref, side_refs, pieces = refs[0], refs[1:-parts], refs[-parts:]
    rows = pieces[0].shape[0]
    for part in range(parts):
        span = slice(part * rows, (part + 1) * rows)
        total = own_ref[span]
        for ref in side_refs:
            total = total + ref[span].astype(jnp.float32)
        pieces[part][...] = total.astype(jnp.bfloat16)


def close(query_grads, parts):
    rows = query_grads[0].shape[0] // parts
    return pl.pallas_call(
        functools.partial(close_kernel, parts),
        out_shape=[jax.ShapeDtypeStruct((rows, HD), jnp.bfloat16)] * parts,
        compiler_params=params(),
        cost_estimate=COST,
    )(*query_grads)


def unpack_kernel(parts, rows, heads, stages, *refs):
    count = parts * len(stages)
    pieces, outs, semaphores = refs[:count], refs[count:-1], refs[-1]
    pairs = []
    for number, blocks in enumerate(stages):
        for distance in range(parts):
            piece = pieces[number * parts + distance]
            for index, (output, head) in enumerate(blocks):
                columns = pl.ds(column_of(distance, heads, head), HD)
                pairs.append((piece.at[index * rows : (index + 1) * rows], outs[output].at[:, columns]))
    run_copies(pairs, semaphores)


def unpack(stages, pieces, rows, heads):
    parts = len(pieces[0])
    whole = pl.BlockSpec(memory_space=pl.ANY)
    channels = parts * heads * HD
    return pl.pallas_call(
        functools.partial(unpack_kernel, parts, rows, heads, stages),
        in_specs=[whole] * (parts * len(stages)),
        out_specs=[whole] * 3,
        out_shape=[jax.ShapeDtypeStruct((rows, channels), jnp.bfloat16)] * 3,
        scratch_shapes=[pltpu.SemaphoreType.DMA((3 * heads * parts,))],
        compiler_params=params(),
        cost_estimate=COST,
    )(*[piece for stage in pieces for piece in stage])


def swap(value, axis, distance):
    return lax.ppermute(value, axis, [(index, index ^ distance) for index in range(lax.axis_size(axis))])


def swap_pieces(pieces, earlier=None):
    held = [pieces[0]]
    for distance in range(1, len(pieces)):
        piece = pieces[distance]
        if earlier is not None:
            piece = after([piece], earlier[distance])[0]
        held.append(swap(piece, "ulysses", distance))
    return held


def tree_sum(values):
    while len(values) > 1:
        values = [functools.reduce(jnp.add, values[index : index + 2]) for index in range(0, len(values), 2)]
    return values[0]


def sum_over(value, axis):
    size = lax.axis_size(axis)
    if size & (size - 1):
        return lax.psum(value, axis)
    return tree_sum([value] + [swap(value, axis, distance) for distance in range(1, size)])


def after(values, *earlier):
    return lax.optimization_barrier((list(values), earlier))[0]


def neighbours(size):
    if size == 1:
        return []
    if size == 2:
        swapped = [(0, 1), (1, 0)]
        return [(swapped, swapped)]
    up = [(index, index + 1) for index in range(size - 1)]
    down = [(index + 1, index) for index in range(size - 1)]
    return [(up, down), (down, up)]


def exchange_totals(partial, sides):
    if not sides:
        return partial
    if len(sides) == 1:
        other = lax.ppermute(jnp.concatenate(partial), "tm", sides[0][0])
        heads = partial[0].shape[0]
        return [join_totals([partial[0], other[heads:]]), join_totals([partial[1], other[:heads]])]
    position = lax.axis_index("tm")
    present = [position < lax.axis_size("tm") - 1, position > 0]
    values = [partial[0]]
    for value, (_, back), flag in zip(partial[1:], sides, present):
        values.append(jnp.where(flag, lax.ppermute(value, "tm", back), -jnp.inf))
    own = join_totals(values)
    return [own] + [lax.ppermute(own, "tm", there) for there, _ in sides]


def local(queries, keys, values, attn_out, out_grad, out_gain):
    parts = lax.axis_size("ulysses")
    span = lax.axis_size("tm")
    rows, channels = queries.shape[1:]
    heads = channels // (parts * HD)
    rest = list(range(1, heads))
    dots = dots_depth(rows, heads)
    every = list(range(parts))
    sides = neighbours(span)

    def forward(array):
        return [lax.ppermute(array, "tm", there) for there, _ in sides]

    with jax.named_scope("keys_queries"):
        packed = pack([keys[0], queries[0]], parts, list(range(heads)))
        pairs = swap_pieces(packed)
    paired = span == 2
    with jax.named_scope("gain"):
        out_grad = after([out_grad], packed[0])[0]
        gain = gain_partial(out_grad[0], attn_out[0]).reshape(-1, LANES)
        gain = sum_over(gain, "dp")
        if not paired:
            gain = sum_over(gain, "tm")
    with jax.named_scope("grads"):
        sent_lead, sent_rest = pack_grads(out_grad[0], attn_out[0], values[0], out_gain, gain, parts)
    with jax.named_scope("halo_queries"):
        width = heads * rows
        first_side = forward(pairs[0][width:])
        late = after(pairs[1:], sent_lead[0], first_side)
        late_side = forward(gather_rows(late, [(number, width, width) for number in range(parts - 1)]))
    with jax.named_scope("first_grads"):
        lead = swap_pieces(sent_lead, pairs)
    with jax.named_scope("halo_first_grads"):
        extra = gain_depth(channels) if paired else 0
        ranges = [(part, 0, rows) for part in every] + [(part, 2 * rows, dots) for part in every]
        ranges += [(part, 2 * rows + dots, extra) for part in every] * paired
        lead_side = forward(gather_rows(lead, ranges))
    with jax.named_scope("totals"):
        key_places = [[(piece, head) for piece in pairs] for head in range(heads)]
        query_places = [[[(piece, heads + head) for piece in pairs] for head in range(heads)]]
        for first, others in zip(first_side, late_side):
            query_places.append(
                [
                    [(first, head)] + [(others, (part - 1) * heads + head) for part in every[1:]]
                    for head in range(heads)
                ]
            )
        part_totals = partial_totals(key_places, query_places, rows)
        totals = exchange_totals(part_totals, sides)
    with jax.named_scope("rest_grads"):
        rest_grads = swap_pieces(after(sent_rest, gain), lead)
    with jax.named_scope("halo_rest_grads"):
        ranges = [(part, place * rows, rows) for place in range(heads - 1) for part in every]
        rest_side = forward(gather_rows(rest_grads, ranges))
    with jax.named_scope("rest_values"):
        rest_values = swap_pieces(after(pack([values[0]], parts, rest), part_totals), rest_grads)
    dot_places = [(piece, 2 * rows // dots) for piece in lead]
    dot_places += [(array, parts * rows // dots + part) for array in lead_side for part in every]
    stages, pieces, open_grads = [], [], []
    gate = rest_values
    for head in range(heads):
        if head == 0:
            value_places = [(piece, 1) for piece in lead]
            grad_places = [(piece, 0) for piece in lead] + [(array, part) for array in lead_side for part in every]
        else:
            value_places = [(piece, head - 1) for piece in rest_values]
            grad_places = [(piece, head - 1) for piece in rest_grads]
            grad_places += [(array, (head - 1) * parts + part) for array in rest_side for part in every]
        before = open_grads if head else ()
        with jax.named_scope("attention_%d" % head):
            leaving, query_grads = attention(
                head,
                heads,
                rows,
                key_places[head],
                value_places,
                [place for source in query_places for place in source[head]],
                grad_places,
                dot_places,
                totals,
                before,
            )
        stages.append([(1, head), (2, head)] + ([(0, head - 1)] if before else []))
        query_grads = after(query_grads, gate[1:])
        with jax.named_scope("halo_query_grads_%d" % head):
            back_grads = [lax.ppermute(other, "tm", back) for other, (_, back) in zip(query_grads[1:], sides)]
            open_grads = list(query_grads[:1]) + back_grads
        with jax.named_scope("returns_%d" % head):
            pieces.append(swap_pieces(leaving, gate))
        gate = pieces[-1]
    with jax.named_scope("returns_last"):
        stages.append([(0, heads - 1)])
        pieces.append(swap_pieces(close(open_grads, parts)))
    result = unpack(stages, pieces, rows, heads)
    with jax.named_scope("gain"):
        places = [(piece, 2 * rows + dots) for piece in lead]
        if paired:
            places += [(lead_side[0], parts * (rows + dots) + part * extra) for part in every]
        gain = gain_total(places, channels // LANES, 1.0 / (rows * span * parts * lax.axis_size("dp")))
    return tuple(grad[None] for grad in result) + (gain.reshape(channels),)


def solution(mesh):
    split = P("dp", ("tm", "ulysses"), None)
    return jax.shard_map(
        local,
        mesh=mesh,
        in_specs=(split,) * 5 + (P(),),
        out_specs=(split,) * 3 + (P(),),
        check_vma=False,
    )
```

```python
import functools
import math

import jax
import jax.numpy as jnp
from jax import lax
from jax.experimental import pallas as pl
from jax.experimental.pallas import tpu as pltpu
from jax.sharding import PartitionSpec as P

HD = 128
LANES = 128
TILE_ROWS = 16
KEY_BLOCK = 256
QUERY_BLOCK = 256
VMEM_LIMIT = 48 * 1024 * 1024
SCALE = 1.0 / math.sqrt(HD)
SCALE_LOG2 = SCALE / math.log(2.0)
COST = pl.CostEstimate(flops=1, bytes_accessed=1, transcendentals=0)


def params():
    return pltpu.CompilerParams(vmem_limit_bytes=VMEM_LIMIT)


def distances(parts):
    return [0] + list(range(parts - 1, 0, -1))


def column_of(parts, place, heads, head):
    partner = lax.axis_index("ulysses") ^ distances(parts)[place]
    return pl.multiple_of((partner * heads + head) * HD, HD)


def run_copies(pairs, semaphores):
    copies = [
        pltpu.make_async_copy(source, target, semaphores.at[index]) for index, (source, target) in enumerate(pairs)
    ]
    for copy in copies:
        copy.start()
    for copy in copies:
        copy.wait()


def pack_kernel(parts, chosen, *refs):
    sources, pieces, semaphores = refs[: -parts - 1], refs[-parts - 1 : -1], refs[-1]
    rows, channels = sources[0].shape
    heads = channels // (parts * HD)
    pairs = []
    for distance in range(parts):
        for half, ref in enumerate(sources):
            for place, head in enumerate(chosen):
                columns = pl.ds(column_of(parts, distance, heads, head), HD)
                start = (half * len(chosen) + place) * rows
                pairs.append((ref.at[:, columns], pieces[distance].at[start : start + rows]))
    run_copies(pairs, semaphores)


def pack(sources, parts, chosen):
    rows = sources[0].shape[0]
    depth = len(sources) * len(chosen) * rows
    whole = pl.BlockSpec(memory_space=pl.ANY)
    return pl.pallas_call(
        functools.partial(pack_kernel, parts, chosen),
        in_specs=[whole] * len(sources),
        out_specs=[whole] * parts,
        out_shape=[jax.ShapeDtypeStruct((depth, HD), sources[0].dtype)] * parts,
        scratch_shapes=[pltpu.SemaphoreType.DMA((len(sources) * len(chosen) * parts,))],
        compiler_params=params(),
        cost_estimate=COST,
    )(*sources)


def gather_kernel(ranges, *refs):
    arrays, out_ref, semaphores = refs[:-2], refs[-2], refs[-1]
    pairs = []
    place = 0
    for number, first, count in ranges:
        pairs.append((arrays[number].at[first : first + count], out_ref.at[place : place + count]))
        place += count
    run_copies(pairs, semaphores)


def gather_rows(arrays, ranges):
    whole = pl.BlockSpec(memory_space=pl.ANY)
    depth = sum(count for _, _, count in ranges)
    return pl.pallas_call(
        functools.partial(gather_kernel, ranges),
        in_specs=[whole] * len(arrays),
        out_specs=whole,
        out_shape=jax.ShapeDtypeStruct((depth, HD), arrays[0].dtype),
        scratch_shapes=[pltpu.SemaphoreType.DMA((len(ranges),))],
        compiler_params=params(),
        cost_estimate=COST,
    )(*arrays)


def dot_groups(rows):
    return -(-rows // LANES)


def dots_depth(rows, heads):
    return -(-2 * heads * dot_groups(rows) // TILE_ROWS) * TILE_ROWS


def gain_kernel(out_grad_ref, attn_ref, out_ref):
    product = out_grad_ref[...].astype(jnp.float32) * attn_ref[...].astype(jnp.float32)
    out_ref[...] = jnp.sum(product, axis=0, keepdims=True)


def gain_partial(out_grad, attn_out):
    return pl.pallas_call(
        gain_kernel,
        out_shape=jax.ShapeDtypeStruct((1, out_grad.shape[1]), jnp.float32),
        compiler_params=params(),
        cost_estimate=COST,
    )(out_grad, attn_out)


def split_terms(value, count):
    terms = []
    for _ in range(count):
        term = value.astype(jnp.bfloat16).astype(jnp.float32)
        terms.append(term)
        value = value - term
    return terms


def gain_depth(channels):
    return -(-3 * channels // LANES // TILE_ROWS) * TILE_ROWS


def pack_grads_kernel(parts, out_grad_ref, attn_ref, value_ref, gain_ref, partial_ref, *refs):
    leads, rests = refs[:parts], refs[parts:]
    rows, channels = out_grad_ref.shape
    heads = channels // (parts * HD)
    depth = 2 * rows + dots_depth(rows, heads)
    lines = partial_ref.shape[0]
    partial = jnp.concatenate(split_terms(partial_ref[...], 3), axis=0)
    spare = gain_depth(channels) - partial.shape[0]
    if spare:
        partial = jnp.concatenate([partial, jnp.zeros((spare, LANES), jnp.float32)], axis=0)
    for distance in range(parts):
        terms = []
        for head in range(heads):
            columns = pl.ds(column_of(parts, distance, heads, head), HD)
            grad = (out_grad_ref[:, columns].astype(jnp.float32) * gain_ref[:, columns]).astype(jnp.bfloat16)
            if head:
                rests[distance][(head - 1) * rows : head * rows] = grad
            else:
                leads[distance][:rows] = grad
                leads[distance][rows : 2 * rows] = value_ref[:, columns]
            product = grad.astype(jnp.float32) * attn_ref[:, columns].astype(jnp.float32)
            dots = jnp.sum(jnp.transpose(product), axis=0, keepdims=True)
            for first in range(0, rows, LANES):
                value = dots[:, first : first + LANES]
                if value.shape[1] < LANES:
                    rest = jnp.zeros((1, LANES - value.shape[1]), jnp.float32)
                    value = jnp.concatenate([value, rest], axis=1)
                terms += split_terms(value, 2)
        rest = dots_depth(rows, heads) - len(terms)
        if rest:
            terms.append(jnp.zeros((rest, LANES), jnp.float32))
        leads[distance][2 * rows : depth] = jnp.concatenate(terms, axis=0).astype(jnp.bfloat16)
        leads[distance][depth:] = partial.astype(jnp.bfloat16)


def pack_grads(out_grad, attn_out, values, out_gain, partial, parts):
    rows, channels = out_grad.shape
    heads = channels // (parts * HD)
    depth = 2 * rows + dots_depth(rows, heads) + gain_depth(channels)
    lead = jax.ShapeDtypeStruct((depth, HD), jnp.bfloat16)
    rest = jax.ShapeDtypeStruct(((heads - 1) * rows, HD), jnp.bfloat16)
    outs = pl.pallas_call(
        functools.partial(pack_grads_kernel, parts),
        out_shape=[lead] * parts + [rest] * parts,
        compiler_params=params(),
        cost_estimate=COST,
    )(out_grad, attn_out, values, out_gain.reshape(1, channels), partial)
    return outs[:parts], outs[parts:]


def gain_total_kernel(lines, starts, scale, *refs):
    values = []
    for ref, start in zip(refs[:-1], starts):
        terms = [ref[start + index * lines : start + (index + 1) * lines].astype(jnp.float32) for index in range(3)]
        values.append(terms[0] + terms[1] + terms[2])
    refs[-1][...] = tree_sum(values) * scale


def gain_total(places, lines, scale):
    return pl.pallas_call(
        functools.partial(gain_total_kernel, lines, [start for _, start in places], scale),
        out_shape=jax.ShapeDtypeStruct((lines, LANES), jnp.float32),
        compiler_params=params(),
        cost_estimate=COST,
    )(*[array for array, _ in places])


def stacked(refs):
    return jnp.concatenate([ref[...] for ref in refs], axis=0)


def block_specs(depth, places):
    def block(index):
        return pl.BlockSpec((depth, HD), lambda step: (index, 0))

    return [block(index) for _, index in places], [array for array, _ in places]


def totals_kernel(parts, sources, heads, *refs):
    key_refs, refs = refs[: parts * heads], refs[parts * heads :]
    query_refs, refs = refs[: parts * heads * sources], refs[parts * heads * sources :]
    outs, score_ref = refs[:sources], refs[sources]
    slab = score_ref.shape[0]
    for head in range(heads):
        keys = stacked(key_refs[head * parts : (head + 1) * parts])
        for source in range(sources):
            start = (source * heads + head) * parts
            flip = jnp.transpose(stacked(query_refs[start : start + parts]))
            top = None
            for first in range(0, slab, KEY_BLOCK):
                scores = jnp.dot(keys[first : first + KEY_BLOCK], flip, preferred_element_type=jnp.float32)
                score_ref[first : first + KEY_BLOCK] = scores
                part_top = jnp.max(scores.reshape(-1, 8, slab), axis=0)
                top = part_top if top is None else jnp.maximum(top, part_top)
            top = jnp.max(top, axis=0, keepdims=True) * SCALE_LOG2
            total = None
            for first in range(0, slab, KEY_BLOCK):
                powers = jnp.exp2(score_ref[first : first + KEY_BLOCK] * SCALE_LOG2 - top)
                part_total = jnp.sum(powers.reshape(-1, 8, slab), axis=0)
                total = part_total if total is None else total + part_total
            total = jnp.sum(total, axis=0, keepdims=True)
            outs[source][head : head + 1] = top + jnp.log(total) * (1.0 / math.log(2.0))


def partial_totals(keys, queries, rows):
    heads, parts, sources = len(keys), len(keys[0]), len(queries)
    slab = parts * rows
    places = [place for head in keys for place in head]
    places += [place for source in queries for head in source for place in head]
    in_specs, operands = block_specs(rows, places)
    line = pl.BlockSpec((heads, slab), lambda step: (0, 0))
    return pl.pallas_call(
        functools.partial(totals_kernel, parts, sources, heads),
        grid=(1,),
        in_specs=in_specs,
        out_specs=[line] * sources,
        out_shape=[jax.ShapeDtypeStruct((heads, slab), jnp.float32)] * sources,
        scratch_shapes=[pltpu.VMEM((slab, slab), jnp.float32)],
        compiler_params=params(),
        cost_estimate=pl.CostEstimate(
            flops=2 * heads * sources * slab * slab * HD,
            bytes_accessed=heads * sources * slab * HD * 4,
            transcendentals=heads * sources * slab * slab,
        ),
    )(*operands)


def join_totals(values):
    top = functools.reduce(jnp.maximum, values)
    return top + jnp.log2(functools.reduce(jnp.add, [jnp.exp2(value - top) for value in values]))


def attention_kernel(parts, sources, head, rows, before, *refs):
    slab = parts * rows

    def take(count):
        nonlocal refs
        taken, refs = refs[:count], refs[count:]
        return taken

    key_refs, value_refs = take(parts), take(parts)
    query_refs, grad_refs, dots_refs = take(parts * sources), take(parts * sources), take(parts * sources)
    total_refs = take(sources)
    before_refs = take(sources) if before else ()
    piece_refs, query_grad_refs = take(parts), take(sources)
    weight_ref, score_ref = refs
    if before:
        closed = before_refs[0][...]
        for ref in before_refs[1:]:
            closed = closed + ref[...].astype(jnp.float32)
        closed = closed.astype(jnp.bfloat16)
        for part in range(parts):
            piece_refs[part][2 * rows :] = closed[part * rows : (part + 1) * rows]
    keys, values, queries, grads = stacked(key_refs), stacked(value_refs), stacked(query_refs), stacked(grad_refs)
    query_flip, grad_flip = jnp.transpose(queries), jnp.transpose(grads)
    lines = []
    for ref in dots_refs:
        terms = ref[...].astype(jnp.float32)
        for index in range(dot_groups(rows)):
            line = 2 * (head * dot_groups(rows) + index)
            count = min(LANES, rows - index * LANES)
            lines.append((terms[line : line + 1] + terms[line + 1 : line + 2])[:, :count])
    dots = jnp.concatenate(lines, axis=1)
    totals = jnp.concatenate([ref[head : head + 1] for ref in total_refs], axis=1)
    width = sources * slab
    for first in range(0, slab, KEY_BLOCK):
        stretch = slice(first, first + KEY_BLOCK)
        for start in range(0, width, QUERY_BLOCK):
            span = slice(start, start + QUERY_BLOCK)
            scores = jnp.dot(keys[stretch], query_flip[:, span], preferred_element_type=jnp.float32)
            weights = jnp.exp2(scores * SCALE_LOG2 - totals[:, span])
            grad_weights = jnp.dot(values[stretch], grad_flip[:, span], preferred_element_type=jnp.float32)
            weight_ref[stretch, span] = weights.astype(jnp.bfloat16)
            score_ref[stretch, span] = (weights * (grad_weights - dots[:, span])).astype(jnp.bfloat16)
        value_grad = jnp.dot(weight_ref[stretch], grads, preferred_element_type=jnp.float32)
        key_grad = jnp.dot(score_ref[stretch], queries, preferred_element_type=jnp.float32) * SCALE
        key_grad, value_grad = key_grad.astype(jnp.bfloat16), value_grad.astype(jnp.bfloat16)
        for part in range(parts):
            low, high = max(first, part * rows), min(first + KEY_BLOCK, (part + 1) * rows)
            if low < high:
                place = low - part * rows
                piece_refs[part][place : place + high - low] = key_grad[low - first : high - first]
                piece_refs[part][rows + place : rows + place + high - low] = value_grad[low - first : high - first]
    for source in range(sources):
        query_grad = lax.dot_general(
            score_ref[:, source * slab : (source + 1) * slab],
            keys,
            (((0,), (0,)), ((), ())),
            preferred_element_type=jnp.float32,
        )
        query_grad_refs[source][...] = (query_grad * SCALE).astype(query_grad_refs[source].dtype)


def attention(head, heads, rows, keys, values, queries, grads, dots, totals, before):
    parts = len(keys)
    sources = len(totals)
    slab = parts * rows
    in_specs, operands = block_specs(rows, keys + values + queries + grads)
    dot_specs, dot_arrays = block_specs(dots_depth(rows, heads), dots)
    before_specs, before_arrays = block_specs(slab, [(array, 0) for array in before])
    line = pl.BlockSpec((heads, slab), lambda step: (0, 0))
    depth = (3 if before else 2) * rows
    out_specs, _ = block_specs(depth, [(None, 0)] * parts)
    query_specs, _ = block_specs(slab, [(None, 0)] * sources)
    outs = pl.pallas_call(
        functools.partial(attention_kernel, parts, sources, head, rows, bool(before)),
        grid=(1,),
        in_specs=in_specs + dot_specs + [line] * sources + before_specs,
        out_specs=out_specs + query_specs,
        out_shape=[jax.ShapeDtypeStruct((depth, HD), jnp.bfloat16)] * parts
        + [jax.ShapeDtypeStruct((slab, HD), jnp.float32)]
        + [jax.ShapeDtypeStruct((slab, HD), jnp.bfloat16)] * (sources - 1),
        scratch_shapes=[pltpu.VMEM((slab, sources * slab), jnp.bfloat16)] * 2,
        compiler_params=params(),
        cost_estimate=pl.CostEstimate(
            flops=10 * slab * sources * slab * HD,
            bytes_accessed=32 * slab * HD,
            transcendentals=slab * sources * slab,
        ),
    )(*operands, *dot_arrays, *totals, *before_arrays)
    return outs[:parts], outs[parts:]


def close_kernel(parts, *refs):
    own_ref, side_refs, pieces = refs[0], refs[1:-parts], refs[-parts:]
    rows = pieces[0].shape[0]
    for part in range(parts):
        span = slice(part * rows, (part + 1) * rows)
        total = own_ref[span]
        for ref in side_refs:
            total = total + ref[span].astype(jnp.float32)
        pieces[part][...] = total.astype(jnp.bfloat16)


def close(query_grads, parts):
    rows = query_grads[0].shape[0] // parts
    return pl.pallas_call(
        functools.partial(close_kernel, parts),
        out_shape=[jax.ShapeDtypeStruct((rows, HD), jnp.bfloat16)] * parts,
        compiler_params=params(),
        cost_estimate=COST,
    )(*query_grads)


def unpack_kernel(parts, rows, heads, stages, *refs):
    count = parts * len(stages)
    pieces, outs, semaphores = refs[:count], refs[count:-1], refs[-1]
    pairs = []
    for number, blocks in enumerate(stages):
        for distance in range(parts):
            piece = pieces[number * parts + distance]
            for index, (output, head) in enumerate(blocks):
                columns = pl.ds(column_of(parts, distance, heads, head), HD)
                pairs.append((piece.at[index * rows : (index + 1) * rows], outs[output].at[:, columns]))
    run_copies(pairs, semaphores)


def unpack(stages, pieces, rows, heads):
    parts = len(pieces[0])
    whole = pl.BlockSpec(memory_space=pl.ANY)
    channels = parts * heads * HD
    return pl.pallas_call(
        functools.partial(unpack_kernel, parts, rows, heads, stages),
        in_specs=[whole] * (parts * len(stages)),
        out_specs=[whole] * 3,
        out_shape=[jax.ShapeDtypeStruct((rows, channels), jnp.bfloat16)] * 3,
        scratch_shapes=[pltpu.SemaphoreType.DMA((3 * heads * parts,))],
        compiler_params=params(),
        cost_estimate=COST,
    )(*[piece for stage in pieces for piece in stage])


def swap(value, axis, distance):
    return lax.ppermute(value, axis, [(index, index ^ distance) for index in range(lax.axis_size(axis))])


def swap_pieces(pieces, earlier=None):
    held = [pieces[0]]
    if earlier is not None:
        pieces = after(pieces, earlier[1:])
    for place, distance in enumerate(distances(len(pieces))):
        if distance:
            held.append(swap(pieces[place], "ulysses", distance))
    return held


def tree_sum(values):
    while len(values) > 1:
        values = [functools.reduce(jnp.add, values[index : index + 2]) for index in range(0, len(values), 2)]
    return values[0]


def sum_over(value, axis):
    size = lax.axis_size(axis)
    if size & (size - 1):
        return lax.psum(value, axis)
    return tree_sum([value] + [swap(value, axis, distance) for distance in range(1, size)])


def after(values, *earlier):
    return lax.optimization_barrier((list(values), earlier))[0]


def neighbours(size):
    if size == 1:
        return []
    if size == 2:
        swapped = [(0, 1), (1, 0)]
        return [(swapped, swapped)]
    up = [(index, index + 1) for index in range(size - 1)]
    down = [(index + 1, index) for index in range(size - 1)]
    return [(up, down), (down, up)]


def exchange_totals(partial, sides):
    if not sides:
        return partial
    if len(sides) == 1:
        other = lax.ppermute(jnp.concatenate(partial), "tm", sides[0][0])
        heads = partial[0].shape[0]
        return [join_totals([partial[0], other[heads:]]), join_totals([partial[1], other[:heads]])]
    position = lax.axis_index("tm")
    present = [position < lax.axis_size("tm") - 1, position > 0]
    values = [partial[0]]
    for value, (_, back), flag in zip(partial[1:], sides, present):
        values.append(jnp.where(flag, lax.ppermute(value, "tm", back), -jnp.inf))
    own = join_totals(values)
    return [own] + [lax.ppermute(own, "tm", there) for there, _ in sides]


def local(queries, keys, values, attn_out, out_grad, out_gain):
    parts = lax.axis_size("ulysses")
    span = lax.axis_size("tm")
    rows, channels = queries.shape[1:]
    heads = channels // (parts * HD)
    rest = list(range(1, heads))
    dots = dots_depth(rows, heads)
    every = list(range(parts))
    sides = neighbours(span)

    def forward(array):
        return [lax.ppermute(array, "tm", there) for there, _ in sides]

    with jax.named_scope("keys_queries"):
        packed = pack([keys[0], queries[0]], parts, list(range(heads)))
        pairs = swap_pieces(packed)
    paired = span == 2
    with jax.named_scope("gain"):
        out_grad = after([out_grad], packed[0])[0]
        gain = gain_partial(out_grad[0], attn_out[0]).reshape(-1, LANES)
        gain = sum_over(gain, "dp")
        if not paired:
            gain = sum_over(gain, "tm")
    with jax.named_scope("grads"):
        sent_lead, sent_rest = pack_grads(out_grad[0], attn_out[0], values[0], out_gain, gain, parts)
    with jax.named_scope("halo_queries"):
        width = heads * rows
        first_side = forward(pairs[0][width:])
    with jax.named_scope("first_grads"):
        lead = swap_pieces(sent_lead, pairs)
    with jax.named_scope("rest_grads"):
        rest_grads = swap_pieces(sent_rest, lead)
    with jax.named_scope("halo_queries"):
        late = after(pairs[1:], sent_lead[0], first_side)
        late_side = forward(gather_rows(late, [(number, width, width) for number in range(parts - 1)]))
    with jax.named_scope("halo_first_grads"):
        extra = gain_depth(channels) if paired else 0
        ranges = [(part, 0, rows) for part in every] + [(part, 2 * rows, dots) for part in every]
        ranges += [(part, 2 * rows + dots, extra) for part in every] * paired
        lead_side = forward(gather_rows(after(lead, rest_grads[-1]), ranges))
    with jax.named_scope("totals"):
        key_places = [[(piece, head) for piece in pairs] for head in range(heads)]
        query_places = [[[(piece, heads + head) for piece in pairs] for head in range(heads)]]
        for first, others in zip(first_side, late_side):
            query_places.append(
                [
                    [(first, head)] + [(others, (part - 1) * heads + head) for part in every[1:]]
                    for head in range(heads)
                ]
            )
        part_totals = partial_totals(key_places, query_places, rows)
        totals = exchange_totals(part_totals, sides)
    with jax.named_scope("rest_values"):
        rest_values = swap_pieces(after(pack([values[0]], parts, rest), part_totals), rest_grads)
    with jax.named_scope("halo_rest_grads"):
        ranges = [(part, place * rows, rows) for place in range(heads - 1) for part in every]
        rest_side = forward(gather_rows(after(rest_grads, rest_values[-1]), ranges))
    dot_places = [(piece, 2 * rows // dots) for piece in lead]
    dot_places += [(array, parts * rows // dots + part) for array in lead_side for part in every]
    stages, pieces, open_grads = [], [], []
    gate = rest_values
    for head in range(heads):
        if head == 0:
            value_places = [(piece, 1) for piece in lead]
            grad_places = [(piece, 0) for piece in lead] + [(array, part) for array in lead_side for part in every]
        else:
            value_places = [(piece, head - 1) for piece in rest_values]
            grad_places = [(piece, head - 1) for piece in rest_grads]
            grad_places += [(array, (head - 1) * parts + part) for array in rest_side for part in every]
        before = open_grads if head else ()
        with jax.named_scope("attention_%d" % head):
            leaving, query_grads = attention(
                head,
                heads,
                rows,
                key_places[head],
                value_places,
                [place for source in query_places for place in source[head]],
                grad_places,
                dot_places,
                totals,
                before,
            )
        stages.append([(1, head), (2, head)] + ([(0, head - 1)] if before else []))
        query_grads = after(query_grads, gate[1:])
        with jax.named_scope("halo_query_grads_%d" % head):
            back_grads = [lax.ppermute(other, "tm", back) for other, (_, back) in zip(query_grads[1:], sides)]
            open_grads = list(query_grads[:1]) + back_grads
        with jax.named_scope("returns_%d" % head):
            pieces.append(swap_pieces(leaving, gate))
        gate = pieces[-1]
    with jax.named_scope("returns_last"):
        stages.append([(0, heads - 1)])
        pieces.append(swap_pieces(close(open_grads, parts)))
    result = unpack(stages, pieces, rows, heads)
    with jax.named_scope("gain"):
        places = [(piece, 2 * rows + dots) for piece in lead]
        if paired:
            places += [(lead_side[0], parts * (rows + dots) + part * extra) for part in every]
        gain = gain_total(places, channels // LANES, 1.0 / (rows * span * parts * lax.axis_size("dp")))
    return tuple(grad[None] for grad in result) + (gain.reshape(channels),)


def solution(mesh):
    split = P("dp", ("tm", "ulysses"), None)
    return jax.shard_map(
        local,
        mesh=mesh,
        in_specs=(split,) * 5 + (P(),),
        out_specs=(split,) * 3 + (P(),),
        check_vma=False,
    )
```

```python
import functools
import math

import jax
import jax.numpy as jnp
from jax import lax
from jax.experimental import pallas as pl
from jax.experimental.pallas import tpu as pltpu
from jax.sharding import PartitionSpec as P

HD = 128
LANES = 128
TILE_ROWS = 16
KEY_BLOCK = 256
QUERY_BLOCK = 256
VMEM_LIMIT = 48 * 1024 * 1024
SCALE = 1.0 / math.sqrt(HD)
SCALE_LOG2 = SCALE / math.log(2.0)
COST = pl.CostEstimate(flops=1, bytes_accessed=1, transcendentals=0)


def params():
    return pltpu.CompilerParams(vmem_limit_bytes=VMEM_LIMIT)


def distances(parts):
    return [0] + list(range(parts - 1, 0, -1))


def column_of(parts, place, heads, head):
    partner = lax.axis_index("ulysses") ^ distances(parts)[place]
    return pl.multiple_of((partner * heads + head) * HD, HD)


def run_copies(pairs, semaphores):
    copies = [
        pltpu.make_async_copy(source, target, semaphores.at[index]) for index, (source, target) in enumerate(pairs)
    ]
    for copy in copies:
        copy.start()
    for copy in copies:
        copy.wait()


def pack_kernel(parts, chosen, *refs):
    sources, pieces, semaphores = refs[: -parts - 1], refs[-parts - 1 : -1], refs[-1]
    rows, channels = sources[0].shape
    heads = channels // (parts * HD)
    pairs = []
    for distance in range(parts):
        for half, ref in enumerate(sources):
            for place, head in enumerate(chosen):
                columns = pl.ds(column_of(parts, distance, heads, head), HD)
                start = (half * len(chosen) + place) * rows
                pairs.append((ref.at[:, columns], pieces[distance].at[start : start + rows]))
    run_copies(pairs, semaphores)


def pack(sources, parts, chosen):
    rows = sources[0].shape[0]
    depth = len(sources) * len(chosen) * rows
    whole = pl.BlockSpec(memory_space=pl.ANY)
    return pl.pallas_call(
        functools.partial(pack_kernel, parts, chosen),
        in_specs=[whole] * len(sources),
        out_specs=[whole] * parts,
        out_shape=[jax.ShapeDtypeStruct((depth, HD), sources[0].dtype)] * parts,
        scratch_shapes=[pltpu.SemaphoreType.DMA((len(sources) * len(chosen) * parts,))],
        compiler_params=params(),
        cost_estimate=COST,
    )(*sources)


def gather_kernel(ranges, *refs):
    arrays, out_ref, semaphores = refs[:-2], refs[-2], refs[-1]
    pairs = []
    place = 0
    for number, first, count in ranges:
        pairs.append((arrays[number].at[first : first + count], out_ref.at[place : place + count]))
        place += count
    run_copies(pairs, semaphores)


def gather_rows(arrays, ranges):
    whole = pl.BlockSpec(memory_space=pl.ANY)
    depth = sum(count for _, _, count in ranges)
    return pl.pallas_call(
        functools.partial(gather_kernel, ranges),
        in_specs=[whole] * len(arrays),
        out_specs=whole,
        out_shape=jax.ShapeDtypeStruct((depth, HD), arrays[0].dtype),
        scratch_shapes=[pltpu.SemaphoreType.DMA((len(ranges),))],
        compiler_params=params(),
        cost_estimate=COST,
    )(*arrays)


def dot_groups(rows):
    return -(-rows // LANES)


def dots_depth(rows, heads):
    return -(-2 * heads * dot_groups(rows) // TILE_ROWS) * TILE_ROWS


def gain_kernel(out_grad_ref, attn_ref, out_ref):
    product = out_grad_ref[...].astype(jnp.float32) * attn_ref[...].astype(jnp.float32)
    out_ref[...] = jnp.sum(product, axis=0, keepdims=True)


def gain_partial(out_grad, attn_out):
    return pl.pallas_call(
        gain_kernel,
        out_shape=jax.ShapeDtypeStruct((1, out_grad.shape[1]), jnp.float32),
        compiler_params=params(),
        cost_estimate=COST,
    )(out_grad, attn_out)


def split_terms(value, count):
    terms = []
    for _ in range(count):
        term = value.astype(jnp.bfloat16).astype(jnp.float32)
        terms.append(term)
        value = value - term
    return terms


def gain_depth(channels):
    return -(-3 * channels // LANES // TILE_ROWS) * TILE_ROWS


def pack_grads_kernel(parts, out_grad_ref, attn_ref, value_ref, gain_ref, partial_ref, *refs):
    rows, channels = out_grad_ref.shape
    heads = channels // (parts * HD)
    base = (heads + 1) * rows
    depth = base + dots_depth(rows, heads)
    partial = jnp.concatenate(split_terms(partial_ref[...], 3), axis=0)
    spare = gain_depth(channels) - partial.shape[0]
    if spare:
        partial = jnp.concatenate([partial, jnp.zeros((spare, LANES), jnp.float32)], axis=0)
    for distance in range(parts):
        terms = []
        for head in range(heads):
            columns = pl.ds(column_of(parts, distance, heads, head), HD)
            grad = (out_grad_ref[:, columns].astype(jnp.float32) * gain_ref[:, columns]).astype(jnp.bfloat16)
            place = head + 1 if head else 0
            refs[distance][place * rows : (place + 1) * rows] = grad
            if head == 0:
                refs[distance][rows : 2 * rows] = value_ref[:, columns]
            product = grad.astype(jnp.float32) * attn_ref[:, columns].astype(jnp.float32)
            dots = jnp.sum(jnp.transpose(product), axis=0, keepdims=True)
            for first in range(0, rows, LANES):
                value = dots[:, first : first + LANES]
                if value.shape[1] < LANES:
                    rest = jnp.zeros((1, LANES - value.shape[1]), jnp.float32)
                    value = jnp.concatenate([value, rest], axis=1)
                terms += split_terms(value, 2)
        rest = dots_depth(rows, heads) - len(terms)
        if rest:
            terms.append(jnp.zeros((rest, LANES), jnp.float32))
        refs[distance][base:depth] = jnp.concatenate(terms, axis=0).astype(jnp.bfloat16)
        refs[distance][depth:] = partial.astype(jnp.bfloat16)


def pack_grads(out_grad, attn_out, values, out_gain, partial, parts):
    rows, channels = out_grad.shape
    heads = channels // (parts * HD)
    depth = (heads + 1) * rows + dots_depth(rows, heads) + gain_depth(channels)
    return pl.pallas_call(
        functools.partial(pack_grads_kernel, parts),
        out_shape=[jax.ShapeDtypeStruct((depth, HD), jnp.bfloat16)] * parts,
        compiler_params=params(),
        cost_estimate=COST,
    )(out_grad, attn_out, values, out_gain.reshape(1, channels), partial)


def gain_total_kernel(lines, starts, scale, *refs):
    values = []
    for ref, start in zip(refs[:-1], starts):
        terms = [ref[start + index * lines : start + (index + 1) * lines].astype(jnp.float32) for index in range(3)]
        values.append(terms[0] + terms[1] + terms[2])
    refs[-1][...] = tree_sum(values) * scale


def gain_total(places, lines, scale):
    return pl.pallas_call(
        functools.partial(gain_total_kernel, lines, [start for _, start in places], scale),
        out_shape=jax.ShapeDtypeStruct((lines, LANES), jnp.float32),
        compiler_params=params(),
        cost_estimate=COST,
    )(*[array for array, _ in places])


def stacked(refs):
    return jnp.concatenate([ref[...] for ref in refs], axis=0)


def block_specs(depth, places):
    def block(index):
        return pl.BlockSpec((depth, HD), lambda step: (index, 0))

    return [block(index) for _, index in places], [array for array, _ in places]


def totals_kernel(parts, sources, heads, *refs):
    key_refs, refs = refs[: parts * heads], refs[parts * heads :]
    query_refs, refs = refs[: parts * heads * sources], refs[parts * heads * sources :]
    outs, score_ref = refs[:sources], refs[sources]
    slab = score_ref.shape[0]
    for head in range(heads):
        keys = stacked(key_refs[head * parts : (head + 1) * parts])
        for source in range(sources):
            start = (source * heads + head) * parts
            flip = jnp.transpose(stacked(query_refs[start : start + parts]))
            top = None
            for first in range(0, slab, KEY_BLOCK):
                scores = jnp.dot(keys[first : first + KEY_BLOCK], flip, preferred_element_type=jnp.float32)
                score_ref[first : first + KEY_BLOCK] = scores
                part_top = jnp.max(scores.reshape(-1, 8, slab), axis=0)
                top = part_top if top is None else jnp.maximum(top, part_top)
            top = jnp.max(top, axis=0, keepdims=True) * SCALE_LOG2
            total = None
            for first in range(0, slab, KEY_BLOCK):
                powers = jnp.exp2(score_ref[first : first + KEY_BLOCK] * SCALE_LOG2 - top)
                part_total = jnp.sum(powers.reshape(-1, 8, slab), axis=0)
                total = part_total if total is None else total + part_total
            total = jnp.sum(total, axis=0, keepdims=True)
            outs[source][head : head + 1] = top + jnp.log(total) * (1.0 / math.log(2.0))


def partial_totals(keys, queries, rows):
    heads, parts, sources = len(keys), len(keys[0]), len(queries)
    slab = parts * rows
    places = [place for head in keys for place in head]
    places += [place for source in queries for head in source for place in head]
    in_specs, operands = block_specs(rows, places)
    line = pl.BlockSpec((heads, slab), lambda step: (0, 0))
    return pl.pallas_call(
        functools.partial(totals_kernel, parts, sources, heads),
        grid=(1,),
        in_specs=in_specs,
        out_specs=[line] * sources,
        out_shape=[jax.ShapeDtypeStruct((heads, slab), jnp.float32)] * sources,
        scratch_shapes=[pltpu.VMEM((slab, slab), jnp.float32)],
        compiler_params=params(),
        cost_estimate=pl.CostEstimate(
            flops=2 * heads * sources * slab * slab * HD,
            bytes_accessed=heads * sources * slab * HD * 4,
            transcendentals=heads * sources * slab * slab,
        ),
    )(*operands)


def join_totals(values):
    top = functools.reduce(jnp.maximum, values)
    return top + jnp.log2(functools.reduce(jnp.add, [jnp.exp2(value - top) for value in values]))


def attention_kernel(parts, sources, chosen, rows, *refs):
    slab = parts * rows

    def take(count):
        nonlocal refs
        taken, refs = refs[:count], refs[count:]
        return taken

    dots_refs, total_refs = take(parts * sources), take(sources)
    inputs = [[take(parts), take(parts), take(parts * sources), take(parts * sources)] for _ in chosen]
    piece_refs, query_grad_refs = take(parts), take(sources)
    weight_ref, score_ref = refs
    for number, head in enumerate(chosen):
        keys, values, queries, grads = [stacked(held) for held in inputs[number]]
        query_flip, grad_flip = jnp.transpose(queries), jnp.transpose(grads)
        lines = []
        for ref in dots_refs:
            terms = ref[...].astype(jnp.float32)
            for index in range(dot_groups(rows)):
                line = 2 * (head * dot_groups(rows) + index)
                count = min(LANES, rows - index * LANES)
                lines.append((terms[line : line + 1] + terms[line + 1 : line + 2])[:, :count])
        dots = jnp.concatenate(lines, axis=1)
        totals = jnp.concatenate([ref[head : head + 1] for ref in total_refs], axis=1)
        base = 2 * number * rows
        for first in range(0, slab, KEY_BLOCK):
            stretch = slice(first, first + KEY_BLOCK)
            for start in range(0, sources * slab, QUERY_BLOCK):
                span = slice(start, start + QUERY_BLOCK)
                scores = jnp.dot(keys[stretch], query_flip[:, span], preferred_element_type=jnp.float32)
                weights = jnp.exp2(scores * SCALE_LOG2 - totals[:, span])
                grad_weights = jnp.dot(values[stretch], grad_flip[:, span], preferred_element_type=jnp.float32)
                weight_ref[stretch, span] = weights.astype(jnp.bfloat16)
                score_ref[stretch, span] = (weights * (grad_weights - dots[:, span])).astype(jnp.bfloat16)
            value_grad = jnp.dot(weight_ref[stretch], grads, preferred_element_type=jnp.float32)
            key_grad = jnp.dot(score_ref[stretch], queries, preferred_element_type=jnp.float32) * SCALE
            key_grad, value_grad = key_grad.astype(jnp.bfloat16), value_grad.astype(jnp.bfloat16)
            for part in range(parts):
                low, high = max(first, part * rows), min(first + KEY_BLOCK, (part + 1) * rows)
                if low < high:
                    place = base + low - part * rows
                    local_rows = slice(low - first, high - first)
                    piece_refs[part][place : place + high - low] = key_grad[local_rows]
                    piece_refs[part][place + rows : place + rows + high - low] = value_grad[local_rows]
        for source, ref in enumerate(query_grad_refs):
            query_grad = lax.dot_general(
                score_ref[:, source * slab : (source + 1) * slab],
                keys,
                (((0,), (0,)), ((), ())),
                preferred_element_type=jnp.float32,
            )
            ref[number * slab : (number + 1) * slab] = (query_grad * SCALE).astype(ref.dtype)


def attention(chosen, heads, rows, inputs, dots, totals):
    parts = len(inputs[0][0])
    sources = len(totals)
    slab = parts * rows
    dot_specs, dot_arrays = block_specs(dots_depth(rows, heads), dots)
    in_specs, operands = block_specs(rows, [place for held in inputs for places in held for place in places])
    line = pl.BlockSpec((heads, slab), lambda step: (0, 0))
    depth = 2 * len(chosen) * rows
    out_specs, _ = block_specs(depth, [(None, 0)] * parts)
    query_specs, _ = block_specs(len(chosen) * slab, [(None, 0)] * sources)
    outs = pl.pallas_call(
        functools.partial(attention_kernel, parts, sources, chosen, rows),
        grid=(1,),
        in_specs=dot_specs + [line] * sources + in_specs,
        out_specs=out_specs + query_specs,
        out_shape=[jax.ShapeDtypeStruct((depth, HD), jnp.bfloat16)] * parts
        + [jax.ShapeDtypeStruct((len(chosen) * slab, HD), jnp.float32)]
        + [jax.ShapeDtypeStruct((len(chosen) * slab, HD), jnp.bfloat16)] * (sources - 1),
        scratch_shapes=[pltpu.VMEM((slab, sources * slab), jnp.bfloat16)] * 2,
        compiler_params=params(),
        cost_estimate=pl.CostEstimate(
            flops=10 * len(chosen) * slab * sources * slab * HD,
            bytes_accessed=32 * len(chosen) * slab * HD,
            transcendentals=len(chosen) * slab * sources * slab,
        ),
    )(*dot_arrays, *totals, *operands)
    return outs[:parts], outs[parts:]


def close_kernel(parts, rows, sources, *refs):
    terms, pieces = refs[:-parts], refs[-parts:]
    place = 0
    for first in range(0, len(terms), sources):
        for start in range(0, terms[first].shape[0], parts * rows):
            for part in range(parts):
                span = slice(start + part * rows, start + (part + 1) * rows)
                total = terms[first][span]
                for ref in terms[first + 1 : first + sources]:
                    total = total + ref[span].astype(jnp.float32)
                pieces[part][place : place + rows] = total.astype(jnp.bfloat16)
            place += rows


def close(query_grads, parts, rows):
    depth = sum(terms[0].shape[0] for terms in query_grads) // parts
    return pl.pallas_call(
        functools.partial(close_kernel, parts, rows, len(query_grads[0])),
        out_shape=[jax.ShapeDtypeStruct((depth, HD), jnp.bfloat16)] * parts,
        compiler_params=params(),
        cost_estimate=COST,
    )(*[term for terms in query_grads for term in terms])


def unpack_kernel(parts, rows, heads, stages, *refs):
    count = parts * len(stages)
    pieces, outs, semaphores = refs[:count], refs[count:-1], refs[-1]
    pairs = []
    for number, blocks in enumerate(stages):
        for distance in range(parts):
            piece = pieces[number * parts + distance]
            for index, (output, head) in enumerate(blocks):
                columns = pl.ds(column_of(parts, distance, heads, head), HD)
                pairs.append((piece.at[index * rows : (index + 1) * rows], outs[output].at[:, columns]))
    run_copies(pairs, semaphores)


def unpack(stages, pieces, rows, heads):
    parts = len(pieces[0])
    whole = pl.BlockSpec(memory_space=pl.ANY)
    channels = parts * heads * HD
    return pl.pallas_call(
        functools.partial(unpack_kernel, parts, rows, heads, stages),
        in_specs=[whole] * (parts * len(stages)),
        out_specs=[whole] * 3,
        out_shape=[jax.ShapeDtypeStruct((rows, channels), jnp.bfloat16)] * 3,
        scratch_shapes=[pltpu.SemaphoreType.DMA((3 * heads * parts,))],
        compiler_params=params(),
        cost_estimate=COST,
    )(*[piece for stage in pieces for piece in stage])


def swap(value, axis, distance):
    return lax.ppermute(value, axis, [(index, index ^ distance) for index in range(lax.axis_size(axis))])


def swap_pieces(pieces, earlier=None):
    held = [pieces[0]]
    if earlier is not None:
        pieces = after(pieces, earlier[1:])
    for place, distance in enumerate(distances(len(pieces))):
        if distance:
            held.append(swap(pieces[place], "ulysses", distance))
    return held


def tree_sum(values):
    while len(values) > 1:
        values = [functools.reduce(jnp.add, values[index : index + 2]) for index in range(0, len(values), 2)]
    return values[0]


def sum_over(value, axis):
    size = lax.axis_size(axis)
    if size & (size - 1):
        return lax.psum(value, axis)
    return tree_sum([value] + [swap(value, axis, distance) for distance in range(1, size)])


def after(values, *earlier):
    return lax.optimization_barrier((list(values), earlier))[0]


def neighbours(size):
    if size == 1:
        return []
    if size == 2:
        swapped = [(0, 1), (1, 0)]
        return [(swapped, swapped)]
    up = [(index, index + 1) for index in range(size - 1)]
    down = [(index + 1, index) for index in range(size - 1)]
    return [(up, down), (down, up)]


def exchange_totals(partial, sides):
    if not sides:
        return partial
    if len(sides) == 1:
        other = lax.ppermute(jnp.concatenate(partial), "tm", sides[0][0])
        heads = partial[0].shape[0]
        return [join_totals([partial[0], other[heads:]]), join_totals([partial[1], other[:heads]])]
    position = lax.axis_index("tm")
    present = [position < lax.axis_size("tm") - 1, position > 0]
    values = [partial[0]]
    for value, (_, back), flag in zip(partial[1:], sides, present):
        values.append(jnp.where(flag, lax.ppermute(value, "tm", back), -jnp.inf))
    own = join_totals(values)
    return [own] + [lax.ppermute(own, "tm", there) for there, _ in sides]


def local(queries, keys, values, attn_out, out_grad, out_gain):
    parts = lax.axis_size("ulysses")
    span = lax.axis_size("tm")
    rows, channels = queries.shape[1:]
    heads = channels // (parts * HD)
    rest = list(range(1, heads))
    dots = dots_depth(rows, heads)
    every = list(range(parts))
    sides = neighbours(span)

    def forward(array):
        return [lax.ppermute(array, "tm", there) for there, _ in sides]

    with jax.named_scope("keys_queries"):
        packed = pack([keys[0], queries[0]], parts, list(range(heads)))
        pairs = swap_pieces(packed)
    paired = span == 2
    with jax.named_scope("gain"):
        out_grad = after([out_grad], packed[0])[0]
        gain = gain_partial(out_grad[0], attn_out[0]).reshape(-1, LANES)
        gain = sum_over(gain, "dp")
        if not paired:
            gain = sum_over(gain, "tm")
    with jax.named_scope("grads"):
        sent_lead = pack_grads(out_grad[0], attn_out[0], values[0], out_gain, gain, parts)
    with jax.named_scope("halo_own_grads"):
        own_side = forward(sent_lead[0])
    with jax.named_scope("halo_queries"):
        width = heads * rows
        first_side = forward(pairs[0][width:])
    with jax.named_scope("grads"):
        lead = swap_pieces(sent_lead, pairs)
    with jax.named_scope("halo_queries"):
        late = after(pairs[1:], first_side, sent_lead[0])
        late_side = forward(gather_rows(late, [(number, width, width) for number in range(parts - 1)]))
    base = (heads + 1) * rows
    extra = gain_depth(channels)
    with jax.named_scope("totals"):
        key_places = [[(piece, head) for piece in pairs] for head in range(heads)]
        query_places = [[[(piece, heads + head) for piece in pairs] for head in range(heads)]]
        for first, others in zip(first_side, late_side):
            query_places.append(
                [
                    [(first, head)] + [(others, (part - 1) * heads + head) for part in every[1:]]
                    for head in range(heads)
                ]
            )
        part_totals = partial_totals(key_places, query_places, rows)
        totals = exchange_totals(after(part_totals, lead[1:]), sides)
    others = range(1, parts)
    with jax.named_scope("halo_first_grads"):
        ranges = [(part, 0, rows) for part in others] + [(part, base, dots + extra) for part in others]
        lead_side = forward(gather_rows(after(lead, part_totals, own_side), ranges))
    with jax.named_scope("rest_values"):
        rest_values = swap_pieces(after(pack([values[0]], parts, rest), part_totals), lead)
    dot_places = [(piece, base // dots) for piece in lead]
    for own, array in zip(own_side, lead_side):
        dot_places.append((own, base // dots))
        step = (dots + extra) // dots
        dot_places += [(array, (parts - 1) * rows // dots + (part - 1) * step) for part in others]

    def inputs_of(head):
        queries_of = [place for source in query_places for place in source[head]]
        if head == 0:
            values_of = [(piece, 1) for piece in lead]
            grads_of = [(piece, 0) for piece in lead]
            for own, array in zip(own_side, lead_side):
                grads_of += [(own, 0)] + [(array, part - 1) for part in others]
        else:
            values_of = [(piece, head - 1) for piece in rest_values]
            grads_of = [(piece, head + 1) for piece in lead]
            for own, array in zip(own_side, rest_side):
                start = (head - 1) * (parts - 1)
                grads_of += [(own, head + 1)] + [(array, start + part - 1) for part in others]
        return [key_places[head], values_of, queries_of, grads_of]

    stages, pieces, open_grads = [], [], []
    gate = rest_values
    for number, chosen in enumerate([[0], rest]):
        if number:
            with jax.named_scope("halo_rest_grads"):
                ranges = [(part, (head + 1) * rows, rows) for head in rest for part in others]
                rest_side = forward(gather_rows(after(lead, leaving[0], rest_values[1:]), ranges))
        with jax.named_scope("attention_%d" % number):
            inputs = [inputs_of(head) for head in chosen]
            leaving, query_grads = attention(chosen, heads, rows, inputs, dot_places, totals)
            totals = after(totals, leaving[0])
        if number:
            query_grads = after(query_grads, gate[1:])
        with jax.named_scope("halo_query_grads_%d" % number):
            sent_back = [lax.ppermute(other, "tm", back) for other, (_, back) in zip(query_grads[1:], sides)]
            open_grads.append(list(query_grads[:1]) + sent_back)
        with jax.named_scope("returns_%d" % number):
            gate = swap_pieces(leaving, gate)
            pieces.append(gate)
        stages.append([(output, head) for head in chosen for output in (1, 2)])
    with jax.named_scope("returns_last"):
        pieces.append(swap_pieces(close(open_grads, parts, rows), gate))
        stages.append([(0, head) for head in range(heads)])
    result = unpack(stages, pieces, rows, heads)
    with jax.named_scope("gain"):
        places = [(piece, base + dots) for piece in lead]
        if paired:
            places.append((own_side[0], base + dots))
            start = (parts - 1) * rows + dots
            places += [(lead_side[0], start + (part - 1) * (dots + extra)) for part in others]
        gain = gain_total(places, channels // LANES, 1.0 / (rows * span * parts * lax.axis_size("dp")))
    return tuple(grad[None] for grad in result) + (gain.reshape(channels),)


def solution(mesh):
    split = P("dp", ("tm", "ulysses"), None)
    return jax.shard_map(
        local,
        mesh=mesh,
        in_specs=(split,) * 5 + (P(),),
        out_specs=(split,) * 3 + (P(),),
        check_vma=False,
    )
```

```python
import functools
import math

import jax
import jax.numpy as jnp
from jax import lax
from jax.experimental import pallas as pl
from jax.experimental.pallas import tpu as pltpu
from jax.sharding import PartitionSpec as P

HD = 128
LANES = 128
TILE_ROWS = 16
KEY_BLOCK = 256
QUERY_BLOCK = 256
VMEM_LIMIT = 48 * 1024 * 1024
VMEM_WHOLE = 62 * 1024 * 1024
SCALE = 1.0 / math.sqrt(HD)
SCALE_LOG2 = SCALE / math.log(2.0)
COST = pl.CostEstimate(flops=1, bytes_accessed=1, transcendentals=0)


def params():
    return pltpu.CompilerParams(vmem_limit_bytes=VMEM_LIMIT)


def distances(parts):
    return [0] + list(range(parts - 1, 0, -1))


def column_of(parts, place, heads, head):
    partner = lax.axis_index("ulysses") ^ distances(parts)[place]
    return pl.multiple_of((partner * heads + head) * HD, HD)


def run_copies(pairs, semaphores):
    copies = [
        pltpu.make_async_copy(source, target, semaphores.at[index]) for index, (source, target) in enumerate(pairs)
    ]
    for copy in copies:
        copy.start()
    for copy in copies:
        copy.wait()


def pack_kernel(parts, chosen, *refs):
    sources, pieces, semaphores = refs[: -parts - 1], refs[-parts - 1 : -1], refs[-1]
    rows, channels = sources[0].shape
    heads = channels // (parts * HD)
    pairs = []
    for distance in range(parts):
        for half, ref in enumerate(sources):
            for place, head in enumerate(chosen):
                columns = pl.ds(column_of(parts, distance, heads, head), HD)
                start = (half * len(chosen) + place) * rows
                pairs.append((ref.at[:, columns], pieces[distance].at[start : start + rows]))
    run_copies(pairs, semaphores)


def pack(sources, parts, chosen, limit=VMEM_LIMIT):
    rows = sources[0].shape[0]
    depth = len(sources) * len(chosen) * rows
    whole = pl.BlockSpec(memory_space=pl.ANY)
    return pl.pallas_call(
        functools.partial(pack_kernel, parts, chosen),
        in_specs=[whole] * len(sources),
        out_specs=[whole] * parts,
        out_shape=[jax.ShapeDtypeStruct((depth, HD), sources[0].dtype)] * parts,
        scratch_shapes=[pltpu.SemaphoreType.DMA((len(sources) * len(chosen) * parts,))],
        compiler_params=pltpu.CompilerParams(vmem_limit_bytes=limit),
        cost_estimate=COST,
    )(*sources)


def gather_kernel(ranges, *refs):
    arrays, out_ref, semaphores = refs[:-2], refs[-2], refs[-1]
    pairs = []
    place = 0
    for number, first, count in ranges:
        pairs.append((arrays[number].at[first : first + count], out_ref.at[place : place + count]))
        place += count
    run_copies(pairs, semaphores)


def gather_rows(arrays, ranges):
    whole = pl.BlockSpec(memory_space=pl.ANY)
    depth = sum(count for _, _, count in ranges)
    return pl.pallas_call(
        functools.partial(gather_kernel, ranges),
        in_specs=[whole] * len(arrays),
        out_specs=whole,
        out_shape=jax.ShapeDtypeStruct((depth, HD), arrays[0].dtype),
        scratch_shapes=[pltpu.SemaphoreType.DMA((len(ranges),))],
        compiler_params=params(),
        cost_estimate=COST,
    )(*arrays)


def dot_groups(rows):
    return -(-rows // LANES)


def dots_depth(rows, heads):
    return -(-2 * heads * dot_groups(rows) // TILE_ROWS) * TILE_ROWS


def gain_kernel(out_grad_ref, attn_ref, out_ref):
    product = out_grad_ref[...].astype(jnp.float32) * attn_ref[...].astype(jnp.float32)
    out_ref[...] = jnp.sum(product, axis=0, keepdims=True)


def gain_partial(out_grad, attn_out):
    return pl.pallas_call(
        gain_kernel,
        out_shape=jax.ShapeDtypeStruct((1, out_grad.shape[1]), jnp.float32),
        compiler_params=params(),
        cost_estimate=COST,
    )(out_grad, attn_out)


def split_terms(value, count):
    terms = []
    for _ in range(count):
        term = value.astype(jnp.bfloat16).astype(jnp.float32)
        terms.append(term)
        value = value - term
    return terms


def gain_depth(channels):
    return -(-3 * channels // LANES // TILE_ROWS) * TILE_ROWS


def pack_grads_kernel(parts, out_grad_ref, attn_ref, value_ref, gain_ref, partial_ref, *refs):
    rows, channels = out_grad_ref.shape
    heads = channels // (parts * HD)
    base = (heads + 1) * rows
    depth = base + dots_depth(rows, heads)
    partial = jnp.concatenate(split_terms(partial_ref[...], 3), axis=0)
    spare = gain_depth(channels) - partial.shape[0]
    if spare:
        partial = jnp.concatenate([partial, jnp.zeros((spare, LANES), jnp.float32)], axis=0)
    for distance in range(parts):
        terms = []
        for head in range(heads):
            columns = pl.ds(column_of(parts, distance, heads, head), HD)
            grad = (out_grad_ref[:, columns].astype(jnp.float32) * gain_ref[:, columns]).astype(jnp.bfloat16)
            place = head + 1 if head else 0
            refs[distance][place * rows : (place + 1) * rows] = grad
            if head == 0:
                refs[distance][rows : 2 * rows] = value_ref[:, columns]
            product = grad.astype(jnp.float32) * attn_ref[:, columns].astype(jnp.float32)
            dots = jnp.sum(jnp.transpose(product), axis=0, keepdims=True)
            for first in range(0, rows, LANES):
                value = dots[:, first : first + LANES]
                if value.shape[1] < LANES:
                    rest = jnp.zeros((1, LANES - value.shape[1]), jnp.float32)
                    value = jnp.concatenate([value, rest], axis=1)
                terms += split_terms(value, 2)
        rest = dots_depth(rows, heads) - len(terms)
        if rest:
            terms.append(jnp.zeros((rest, LANES), jnp.float32))
        refs[distance][base:depth] = jnp.concatenate(terms, axis=0).astype(jnp.bfloat16)
        refs[distance][depth:] = partial.astype(jnp.bfloat16)


def pack_grads(out_grad, attn_out, values, out_gain, partial, parts):
    rows, channels = out_grad.shape
    heads = channels // (parts * HD)
    depth = (heads + 1) * rows + dots_depth(rows, heads) + gain_depth(channels)
    return pl.pallas_call(
        functools.partial(pack_grads_kernel, parts),
        out_shape=[jax.ShapeDtypeStruct((depth, HD), jnp.bfloat16)] * parts,
        compiler_params=params(),
        cost_estimate=COST,
    )(out_grad, attn_out, values, out_gain.reshape(1, channels), partial)


def gain_total_kernel(lines, starts, scale, *refs):
    values = []
    for ref, start in zip(refs[:-1], starts):
        terms = [ref[start + index * lines : start + (index + 1) * lines].astype(jnp.float32) for index in range(3)]
        values.append(terms[0] + terms[1] + terms[2])
    refs[-1][...] = tree_sum(values) * scale


def gain_total(places, lines, scale):
    return pl.pallas_call(
        functools.partial(gain_total_kernel, lines, [start for _, start in places], scale),
        out_shape=jax.ShapeDtypeStruct((lines, LANES), jnp.float32),
        compiler_params=params(),
        cost_estimate=COST,
    )(*[array for array, _ in places])


def stacked(refs):
    return jnp.concatenate([ref[...] for ref in refs], axis=0)


def block_specs(depth, places):
    def block(index):
        return pl.BlockSpec((depth, HD), lambda step: (index, 0))

    return [block(index) for _, index in places], [array for array, _ in places]


def totals_kernel(parts, sources, heads, *refs):
    key_refs, refs = refs[: parts * heads], refs[parts * heads :]
    query_refs, refs = refs[: parts * heads * sources], refs[parts * heads * sources :]
    outs, score_ref = refs[:sources], refs[sources]
    slab = score_ref.shape[0]
    for head in range(heads):
        keys = stacked(key_refs[head * parts : (head + 1) * parts])
        for source in range(sources):
            start = (source * heads + head) * parts
            flip = jnp.transpose(stacked(query_refs[start : start + parts]))
            top = None
            for first in range(0, slab, KEY_BLOCK):
                scores = jnp.dot(keys[first : first + KEY_BLOCK], flip, preferred_element_type=jnp.float32)
                score_ref[first : first + KEY_BLOCK] = scores
                part_top = jnp.max(scores.reshape(-1, 8, slab), axis=0)
                top = part_top if top is None else jnp.maximum(top, part_top)
            top = jnp.max(top, axis=0, keepdims=True) * SCALE_LOG2
            total = None
            for first in range(0, slab, KEY_BLOCK):
                powers = jnp.exp2(score_ref[first : first + KEY_BLOCK] * SCALE_LOG2 - top)
                part_total = jnp.sum(powers.reshape(-1, 8, slab), axis=0)
                total = part_total if total is None else total + part_total
            total = jnp.sum(total, axis=0, keepdims=True)
            outs[source][head : head + 1] = top + jnp.log(total) * (1.0 / math.log(2.0))


def partial_totals(keys, queries, rows):
    heads, parts, sources = len(keys), len(keys[0]), len(queries)
    slab = parts * rows
    places = [place for head in keys for place in head]
    places += [place for source in queries for head in source for place in head]
    in_specs, operands = block_specs(rows, places)
    line = pl.BlockSpec((heads, slab), lambda step: (0, 0))
    return pl.pallas_call(
        functools.partial(totals_kernel, parts, sources, heads),
        grid=(1,),
        in_specs=in_specs,
        out_specs=[line] * sources,
        out_shape=[jax.ShapeDtypeStruct((heads, slab), jnp.float32)] * sources,
        scratch_shapes=[pltpu.VMEM((slab, slab), jnp.float32)],
        compiler_params=params(),
        cost_estimate=pl.CostEstimate(
            flops=2 * heads * sources * slab * slab * HD,
            bytes_accessed=heads * sources * slab * HD * 4,
            transcendentals=heads * sources * slab * slab,
        ),
    )(*operands)


def join_totals(values):
    top = functools.reduce(jnp.maximum, values)
    return top + jnp.log2(functools.reduce(jnp.add, [jnp.exp2(value - top) for value in values]))


def attention_kernel(parts, sources, chosen, rows, *refs):
    slab = parts * rows

    def take(count):
        nonlocal refs
        taken, refs = refs[:count], refs[count:]
        return taken

    dots_refs, total_refs = take(parts * sources), take(sources)
    inputs = [[take(parts), take(parts), take(parts * sources), take(parts * sources)] for _ in chosen]
    piece_refs, query_grad_refs = take(parts), take(sources)
    weight_ref, score_ref = refs
    for number, head in enumerate(chosen):
        keys, values, queries, grads = [stacked(held) for held in inputs[number]]
        query_flip, grad_flip = jnp.transpose(queries), jnp.transpose(grads)
        lines = []
        for ref in dots_refs:
            terms = ref[...].astype(jnp.float32)
            for index in range(dot_groups(rows)):
                line = 2 * (head * dot_groups(rows) + index)
                count = min(LANES, rows - index * LANES)
                lines.append((terms[line : line + 1] + terms[line + 1 : line + 2])[:, :count])
        dots = jnp.concatenate(lines, axis=1)
        totals = jnp.concatenate([ref[head : head + 1] for ref in total_refs], axis=1)
        base = 2 * number * rows
        for first in range(0, slab, KEY_BLOCK):
            stretch = slice(first, first + KEY_BLOCK)
            for start in range(0, sources * slab, QUERY_BLOCK):
                span = slice(start, start + QUERY_BLOCK)
                scores = jnp.dot(keys[stretch], query_flip[:, span], preferred_element_type=jnp.float32)
                weights = jnp.exp2(scores * SCALE_LOG2 - totals[:, span])
                grad_weights = jnp.dot(values[stretch], grad_flip[:, span], preferred_element_type=jnp.float32)
                weight_ref[stretch, span] = weights.astype(jnp.bfloat16)
                score_ref[stretch, span] = (weights * (grad_weights - dots[:, span])).astype(jnp.bfloat16)
            value_grad = jnp.dot(weight_ref[stretch], grads, preferred_element_type=jnp.float32)
            key_grad = jnp.dot(score_ref[stretch], queries, preferred_element_type=jnp.float32) * SCALE
            key_grad, value_grad = key_grad.astype(jnp.bfloat16), value_grad.astype(jnp.bfloat16)
            for part in range(parts):
                low, high = max(first, part * rows), min(first + KEY_BLOCK, (part + 1) * rows)
                if low < high:
                    place = base + low - part * rows
                    local_rows = slice(low - first, high - first)
                    piece_refs[part][place : place + high - low] = key_grad[local_rows]
                    piece_refs[part][place + rows : place + rows + high - low] = value_grad[local_rows]
        for source, ref in enumerate(query_grad_refs):
            query_grad = lax.dot_general(
                score_ref[:, source * slab : (source + 1) * slab],
                keys,
                (((0,), (0,)), ((), ())),
                preferred_element_type=jnp.float32,
            )
            ref[number * slab : (number + 1) * slab] = (query_grad * SCALE).astype(ref.dtype)


def attention(chosen, heads, rows, inputs, dots, totals):
    parts = len(inputs[0][0])
    sources = len(totals)
    slab = parts * rows
    dot_specs, dot_arrays = block_specs(dots_depth(rows, heads), dots)
    in_specs, operands = block_specs(rows, [place for held in inputs for places in held for place in places])
    line = pl.BlockSpec((heads, slab), lambda step: (0, 0))
    depth = 2 * len(chosen) * rows
    out_specs, _ = block_specs(depth, [(None, 0)] * parts)
    query_specs, _ = block_specs(len(chosen) * slab, [(None, 0)] * sources)
    outs = pl.pallas_call(
        functools.partial(attention_kernel, parts, sources, chosen, rows),
        grid=(1,),
        in_specs=dot_specs + [line] * sources + in_specs,
        out_specs=out_specs + query_specs,
        out_shape=[jax.ShapeDtypeStruct((depth, HD), jnp.bfloat16)] * parts
        + [jax.ShapeDtypeStruct((len(chosen) * slab, HD), jnp.float32)]
        + [jax.ShapeDtypeStruct((len(chosen) * slab, HD), jnp.bfloat16)] * (sources - 1),
        scratch_shapes=[pltpu.VMEM((slab, sources * slab), jnp.bfloat16)] * 2,
        compiler_params=params(),
        cost_estimate=pl.CostEstimate(
            flops=10 * len(chosen) * slab * sources * slab * HD,
            bytes_accessed=32 * len(chosen) * slab * HD,
            transcendentals=len(chosen) * slab * sources * slab,
        ),
    )(*dot_arrays, *totals, *operands)
    return outs[:parts], outs[parts:]


def close_kernel(parts, rows, sources, *refs):
    terms, pieces = refs[:-parts], refs[-parts:]
    place = 0
    for first in range(0, len(terms), sources):
        for start in range(0, terms[first].shape[0], parts * rows):
            for part in range(parts):
                span = slice(start + part * rows, start + (part + 1) * rows)
                total = terms[first][span]
                for ref in terms[first + 1 : first + sources]:
                    total = total + ref[span].astype(jnp.float32)
                pieces[part][place : place + rows] = total.astype(jnp.bfloat16)
            place += rows


def close(query_grads, parts, rows):
    depth = sum(terms[0].shape[0] for terms in query_grads) // parts
    return pl.pallas_call(
        functools.partial(close_kernel, parts, rows, len(query_grads[0])),
        out_shape=[jax.ShapeDtypeStruct((depth, HD), jnp.bfloat16)] * parts,
        compiler_params=params(),
        cost_estimate=COST,
    )(*[term for terms in query_grads for term in terms])


def unpack_kernel(parts, rows, heads, stages, *refs):
    count = parts * len(stages)
    pieces, outs, semaphores = refs[:count], refs[count:-1], refs[-1]
    pairs = []
    for number, blocks in enumerate(stages):
        for distance in range(parts):
            piece = pieces[number * parts + distance]
            for index, (output, head) in enumerate(blocks):
                columns = pl.ds(column_of(parts, distance, heads, head), HD)
                pairs.append((piece.at[index * rows : (index + 1) * rows], outs[output].at[:, columns]))
    run_copies(pairs, semaphores)


def unpack(stages, pieces, rows, heads, outputs):
    parts = len(pieces[0])
    whole = pl.BlockSpec(memory_space=pl.ANY)
    channels = parts * heads * HD
    return pl.pallas_call(
        functools.partial(unpack_kernel, parts, rows, heads, stages),
        in_specs=[whole] * (parts * len(stages)),
        out_specs=[whole] * outputs,
        out_shape=[jax.ShapeDtypeStruct((rows, channels), jnp.bfloat16)] * outputs,
        scratch_shapes=[pltpu.SemaphoreType.DMA((outputs * heads * parts,))],
        compiler_params=params(),
        cost_estimate=COST,
    )(*[piece for stage in pieces for piece in stage])


def swap(value, axis, distance):
    return lax.ppermute(value, axis, [(index, index ^ distance) for index in range(lax.axis_size(axis))])


def swap_pieces(pieces, earlier=None):
    held = [pieces[0]]
    for place, distance in enumerate(distances(len(pieces))):
        if distance:
            piece = pieces[place] if earlier is None else after([pieces[place]], earlier[place])[0]
            held.append(swap(piece, "ulysses", distance))
    return held


def tree_sum(values):
    while len(values) > 1:
        values = [functools.reduce(jnp.add, values[index : index + 2]) for index in range(0, len(values), 2)]
    return values[0]


def sum_over(value, axis):
    size = lax.axis_size(axis)
    if size & (size - 1):
        return lax.psum(value, axis)
    return tree_sum([value] + [swap(value, axis, distance) for distance in range(1, size)])


def after(values, *earlier):
    return lax.optimization_barrier((list(values), earlier))[0]


def neighbours(size):
    if size == 1:
        return []
    if size == 2:
        swapped = [(0, 1), (1, 0)]
        return [(swapped, swapped)]
    up = [(index, index + 1) for index in range(size - 1)]
    down = [(index + 1, index) for index in range(size - 1)]
    return [(up, down), (down, up)]


def exchange_totals(partial, sides):
    if not sides:
        return partial
    if len(sides) == 1:
        other = lax.ppermute(jnp.concatenate(partial), "tm", sides[0][0])
        heads = partial[0].shape[0]
        return [join_totals([partial[0], other[heads:]]), join_totals([partial[1], other[:heads]])]
    position = lax.axis_index("tm")
    present = [position < lax.axis_size("tm") - 1, position > 0]
    values = [partial[0]]
    for value, (_, back), flag in zip(partial[1:], sides, present):
        values.append(jnp.where(flag, lax.ppermute(value, "tm", back), -jnp.inf))
    own = join_totals(values)
    return [own] + [lax.ppermute(own, "tm", there) for there, _ in sides]


def local(queries, keys, values, attn_out, out_grad, out_gain):
    parts = lax.axis_size("ulysses")
    span = lax.axis_size("tm")
    rows, channels = queries.shape[1:]
    heads = channels // (parts * HD)
    rest = list(range(1, heads))
    dots = dots_depth(rows, heads)
    every = list(range(parts))
    sides = neighbours(span)

    def forward(array):
        return [lax.ppermute(array, "tm", there) for there, _ in sides]

    with jax.named_scope("keys_queries"):
        packed = pack([keys[0], queries[0]], parts, list(range(heads)), VMEM_WHOLE)
        pairs = swap_pieces(packed)
    paired = span == 2
    with jax.named_scope("gain"):
        out_grad = after([out_grad], packed[0])[0]
        gain = gain_partial(out_grad[0], attn_out[0]).reshape(-1, LANES)
        gain = sum_over(gain, "dp")
        if not paired:
            gain = sum_over(gain, "tm")
    with jax.named_scope("grads"):
        sent_lead = pack_grads(out_grad[0], attn_out[0], values[0], out_gain, gain, parts)
    with jax.named_scope("halo_own_grads"):
        own_side = forward(sent_lead[0])
    with jax.named_scope("halo_queries"):
        width = heads * rows
        first_side = forward(pairs[0][width:])
    with jax.named_scope("grads"):
        lead = swap_pieces(sent_lead, pairs)
    with jax.named_scope("halo_queries"):
        late = after(pairs[1:], first_side, sent_lead[0])
        late_side = forward(gather_rows(late, [(number, width, width) for number in range(parts - 1)]))
    base = (heads + 1) * rows
    extra = gain_depth(channels)
    with jax.named_scope("totals"):
        key_places = [[(piece, head) for piece in pairs] for head in range(heads)]
        query_places = [[[(piece, heads + head) for piece in pairs] for head in range(heads)]]
        for first, others in zip(first_side, late_side):
            query_places.append(
                [
                    [(first, head)] + [(others, (part - 1) * heads + head) for part in every[1:]]
                    for head in range(heads)
                ]
            )
        part_totals = partial_totals(key_places, query_places, rows)
        totals = exchange_totals(after(part_totals, lead[1:]), sides)
    others = range(1, parts)
    with jax.named_scope("halo_first_grads"):
        ranges = [(part, 0, rows) for part in others] + [(part, base, dots + extra) for part in others]
        lead_side = forward(gather_rows(after(lead, part_totals, own_side), ranges))
    with jax.named_scope("rest_values"):
        rest_values = swap_pieces(after(pack([values[0]], parts, rest), part_totals), lead)
    dot_places = [(piece, base // dots) for piece in lead]
    for own, array in zip(own_side, lead_side):
        dot_places.append((own, base // dots))
        step = (dots + extra) // dots
        dot_places += [(array, (parts - 1) * rows // dots + (part - 1) * step) for part in others]

    def inputs_of(head):
        queries_of = [place for source in query_places for place in source[head]]
        if head == 0:
            values_of = [(piece, 1) for piece in lead]
            grads_of = [(piece, 0) for piece in lead]
            for own, array in zip(own_side, lead_side):
                grads_of += [(own, 0)] + [(array, part - 1) for part in others]
        else:
            values_of = [(piece, head - 1) for piece in rest_values]
            grads_of = [(piece, head + 1) for piece in lead]
            for own, array in zip(own_side, rest_side):
                start = (head - 1) * (parts - 1)
                grads_of += [(own, head + 1)] + [(array, start + part - 1) for part in others]
        return [key_places[head], values_of, queries_of, grads_of]

    stages, pieces, open_grads = [], [], []
    gate = rest_values
    for number, chosen in enumerate([[0], rest]):
        if number:
            with jax.named_scope("halo_rest_grads"):
                ranges = [(part, (head + 1) * rows, rows) for head in rest for part in others]
                rest_side = forward(gather_rows(after(lead, leaving[0], rest_values[1:]), ranges))
        with jax.named_scope("attention_%d" % number):
            inputs = [inputs_of(head) for head in chosen]
            leaving, query_grads = attention(chosen, heads, rows, inputs, dot_places, totals)
            totals = after(totals, leaving[0])
        if number:
            query_grads = after(query_grads, gate[1:], open_grads[0][1:])
        with jax.named_scope("halo_query_grads_%d" % number):
            sent_back = [lax.ppermute(other, "tm", back) for other, (_, back) in zip(query_grads[1:], sides)]
            open_grads.append(list(query_grads[:1]) + sent_back)
        with jax.named_scope("returns_%d" % number):
            gate = swap_pieces(leaving, gate)
            pieces.append(gate)
        stages.append([(output, head) for head in chosen for output in (0, 1)])
    key_grad, value_grad = unpack(stages, pieces, rows, heads, 2)
    with jax.named_scope("returns_last"):
        last = swap_pieces(close(open_grads, parts, rows), gate)
    (query_grad,) = unpack([[(0, head) for head in range(heads)]], [last], rows, heads, 1)
    result = (query_grad, key_grad, value_grad)
    with jax.named_scope("gain"):
        places = [(piece, base + dots) for piece in lead]
        if paired:
            places.append((own_side[0], base + dots))
            start = (parts - 1) * rows + dots
            places += [(lead_side[0], start + (part - 1) * (dots + extra)) for part in others]
        gain = gain_total(places, channels // LANES, 1.0 / (rows * span * parts * lax.axis_size("dp")))
    return tuple(grad[None] for grad in result) + (gain.reshape(channels),)


def solution(mesh):
    split = P("dp", ("tm", "ulysses"), None)
    return jax.shard_map(
        local,
        mesh=mesh,
        in_specs=(split,) * 5 + (P(),),
        out_specs=(split,) * 3 + (P(),),
        check_vma=False,
    )
```

```python
import functools
import math

import jax
import jax.numpy as jnp
from jax import lax
from jax.experimental import pallas as pl
from jax.experimental.pallas import tpu as pltpu
from jax.sharding import PartitionSpec as P

HD = 128
LANES = 128
TILE_ROWS = 16
KEY_BLOCK = 256
QUERY_BLOCK = 256
VMEM_LIMIT = 48 * 1024 * 1024
SCALE = 1.0 / math.sqrt(HD)
SCALE_LOG2 = SCALE / math.log(2.0)
COST = pl.CostEstimate(flops=1, bytes_accessed=1, transcendentals=0)


def params():
    return pltpu.CompilerParams(vmem_limit_bytes=VMEM_LIMIT)


def distances(parts):
    return [0] + list(range(parts - 1, 0, -1))


def column_of(parts, place, heads, head):
    partner = lax.axis_index("ulysses") ^ distances(parts)[place]
    return pl.multiple_of((partner * heads + head) * HD, HD)


def run_copies(pairs, semaphores):
    copies = [
        pltpu.make_async_copy(source, target, semaphores.at[index]) for index, (source, target) in enumerate(pairs)
    ]
    for copy in copies:
        copy.start()
    for copy in copies:
        copy.wait()


def pack_kernel(parts, chosen, *refs):
    sources, pieces, semaphores = refs[: -parts - 1], refs[-parts - 1 : -1], refs[-1]
    rows, channels = sources[0].shape
    heads = channels // (parts * HD)
    pairs = []
    for distance in range(parts):
        for half, ref in enumerate(sources):
            for place, head in enumerate(chosen):
                columns = pl.ds(column_of(parts, distance, heads, head), HD)
                start = (half * len(chosen) + place) * rows
                pairs.append((ref.at[:, columns], pieces[distance].at[start : start + rows]))
    run_copies(pairs, semaphores)


def pack(sources, parts, chosen):
    rows = sources[0].shape[0]
    depth = len(sources) * len(chosen) * rows
    whole = pl.BlockSpec(memory_space=pl.ANY)
    return pl.pallas_call(
        functools.partial(pack_kernel, parts, chosen),
        in_specs=[whole] * len(sources),
        out_specs=[whole] * parts,
        out_shape=[jax.ShapeDtypeStruct((depth, HD), sources[0].dtype)] * parts,
        scratch_shapes=[pltpu.SemaphoreType.DMA((len(sources) * len(chosen) * parts,))],
        compiler_params=params(),
        cost_estimate=COST,
    )(*sources)


def gather_kernel(ranges, *refs):
    arrays, out_ref, semaphores = refs[:-2], refs[-2], refs[-1]
    pairs = []
    place = 0
    for number, first, count in ranges:
        pairs.append((arrays[number].at[first : first + count], out_ref.at[place : place + count]))
        place += count
    run_copies(pairs, semaphores)


def gather_rows(arrays, ranges):
    whole = pl.BlockSpec(memory_space=pl.ANY)
    depth = sum(count for _, _, count in ranges)
    return pl.pallas_call(
        functools.partial(gather_kernel, ranges),
        in_specs=[whole] * len(arrays),
        out_specs=whole,
        out_shape=jax.ShapeDtypeStruct((depth, HD), arrays[0].dtype),
        scratch_shapes=[pltpu.SemaphoreType.DMA((len(ranges),))],
        compiler_params=params(),
        cost_estimate=COST,
    )(*arrays)


def dot_groups(rows):
    return -(-rows // LANES)


def dots_depth(rows, heads):
    return -(-2 * heads * dot_groups(rows) // TILE_ROWS) * TILE_ROWS


def gain_kernel(out_grad_ref, attn_ref, out_ref):
    product = out_grad_ref[...].astype(jnp.float32) * attn_ref[...].astype(jnp.float32)
    out_ref[...] = jnp.sum(product, axis=0, keepdims=True)


def gain_partial(out_grad, attn_out):
    return pl.pallas_call(
        gain_kernel,
        out_shape=jax.ShapeDtypeStruct((1, out_grad.shape[1]), jnp.float32),
        compiler_params=params(),
        cost_estimate=COST,
    )(out_grad, attn_out)


def split_terms(value, count):
    terms = []
    for _ in range(count):
        term = value.astype(jnp.bfloat16).astype(jnp.float32)
        terms.append(term)
        value = value - term
    return terms


def gain_depth(channels):
    return -(-3 * channels // LANES // TILE_ROWS) * TILE_ROWS


def pack_grads_kernel(parts, out_grad_ref, attn_ref, value_ref, gain_ref, partial_ref, *refs):
    rows, channels = out_grad_ref.shape
    heads = channels // (parts * HD)
    base = (heads + 1) * rows
    depth = base + dots_depth(rows, heads)
    partial = jnp.concatenate(split_terms(partial_ref[...], 3), axis=0)
    spare = gain_depth(channels) - partial.shape[0]
    if spare:
        partial = jnp.concatenate([partial, jnp.zeros((spare, LANES), jnp.float32)], axis=0)
    for distance in range(parts):
        terms = []
        for head in range(heads):
            columns = pl.ds(column_of(parts, distance, heads, head), HD)
            grad = (out_grad_ref[:, columns].astype(jnp.float32) * gain_ref[:, columns]).astype(jnp.bfloat16)
            place = head + 1 if head else 0
            refs[distance][place * rows : (place + 1) * rows] = grad
            if head == 0:
                refs[distance][rows : 2 * rows] = value_ref[:, columns]
            product = grad.astype(jnp.float32) * attn_ref[:, columns].astype(jnp.float32)
            dots = jnp.sum(jnp.transpose(product), axis=0, keepdims=True)
            for first in range(0, rows, LANES):
                value = dots[:, first : first + LANES]
                if value.shape[1] < LANES:
                    rest = jnp.zeros((1, LANES - value.shape[1]), jnp.float32)
                    value = jnp.concatenate([value, rest], axis=1)
                terms += split_terms(value, 2)
        rest = dots_depth(rows, heads) - len(terms)
        if rest:
            terms.append(jnp.zeros((rest, LANES), jnp.float32))
        refs[distance][base:depth] = jnp.concatenate(terms, axis=0).astype(jnp.bfloat16)
        refs[distance][depth:] = partial.astype(jnp.bfloat16)


def pack_grads(out_grad, attn_out, values, out_gain, partial, parts):
    rows, channels = out_grad.shape
    heads = channels // (parts * HD)
    depth = (heads + 1) * rows + dots_depth(rows, heads) + gain_depth(channels)
    return pl.pallas_call(
        functools.partial(pack_grads_kernel, parts),
        out_shape=[jax.ShapeDtypeStruct((depth, HD), jnp.bfloat16)] * parts,
        compiler_params=params(),
        cost_estimate=COST,
    )(out_grad, attn_out, values, out_gain.reshape(1, channels), partial)


def gain_total_kernel(lines, starts, scale, *refs):
    values = []
    for ref, start in zip(refs[:-1], starts):
        terms = [ref[start + index * lines : start + (index + 1) * lines].astype(jnp.float32) for index in range(3)]
        values.append(terms[0] + terms[1] + terms[2])
    refs[-1][...] = tree_sum(values) * scale


def gain_total(places, lines, scale):
    return pl.pallas_call(
        functools.partial(gain_total_kernel, lines, [start for _, start in places], scale),
        out_shape=jax.ShapeDtypeStruct((lines, LANES), jnp.float32),
        compiler_params=params(),
        cost_estimate=COST,
    )(*[array for array, _ in places])


def stacked(refs):
    return jnp.concatenate([ref[...] for ref in refs], axis=0)


def block_specs(depth, places):
    def block(index):
        return pl.BlockSpec((depth, HD), lambda step: (index, 0))

    return [block(index) for _, index in places], [array for array, _ in places]


def totals_kernel(parts, sources, heads, *refs):
    key_refs, refs = refs[: parts * heads], refs[parts * heads :]
    query_refs, refs = refs[: parts * heads * sources], refs[parts * heads * sources :]
    outs, score_ref = refs[:sources], refs[sources]
    slab = score_ref.shape[0]
    for head in range(heads):
        keys = stacked(key_refs[head * parts : (head + 1) * parts])
        for source in range(sources):
            start = (source * heads + head) * parts
            flip = jnp.transpose(stacked(query_refs[start : start + parts]))
            top = None
            for first in range(0, slab, KEY_BLOCK):
                scores = jnp.dot(keys[first : first + KEY_BLOCK], flip, preferred_element_type=jnp.float32)
                score_ref[first : first + KEY_BLOCK] = scores
                part_top = jnp.max(scores.reshape(-1, 8, slab), axis=0)
                top = part_top if top is None else jnp.maximum(top, part_top)
            top = jnp.max(top, axis=0, keepdims=True) * SCALE_LOG2
            total = None
            for first in range(0, slab, KEY_BLOCK):
                powers = jnp.exp2(score_ref[first : first + KEY_BLOCK] * SCALE_LOG2 - top)
                part_total = jnp.sum(powers.reshape(-1, 8, slab), axis=0)
                total = part_total if total is None else total + part_total
            total = jnp.sum(total, axis=0, keepdims=True)
            outs[source][head : head + 1] = top + jnp.log(total) * (1.0 / math.log(2.0))


def partial_totals(keys, queries, rows):
    heads, parts, sources = len(keys), len(keys[0]), len(queries)
    slab = parts * rows
    places = [place for head in keys for place in head]
    places += [place for source in queries for head in source for place in head]
    in_specs, operands = block_specs(rows, places)
    line = pl.BlockSpec((heads, slab), lambda step: (0, 0))
    return pl.pallas_call(
        functools.partial(totals_kernel, parts, sources, heads),
        grid=(1,),
        in_specs=in_specs,
        out_specs=[line] * sources,
        out_shape=[jax.ShapeDtypeStruct((heads, slab), jnp.float32)] * sources,
        scratch_shapes=[pltpu.VMEM((slab, slab), jnp.float32)],
        compiler_params=params(),
        cost_estimate=pl.CostEstimate(
            flops=2 * heads * sources * slab * slab * HD,
            bytes_accessed=heads * sources * slab * HD * 4,
            transcendentals=heads * sources * slab * slab,
        ),
    )(*operands)


def join_totals(values):
    top = functools.reduce(jnp.maximum, values)
    return top + jnp.log2(functools.reduce(jnp.add, [jnp.exp2(value - top) for value in values]))


def attention_kernel(parts, sources, chosen, rows, *refs):
    slab = parts * rows

    def take(count):
        nonlocal refs
        taken, refs = refs[:count], refs[count:]
        return taken

    dots_refs, total_refs = take(parts * sources), take(sources)
    inputs = [[take(parts), take(parts), take(parts * sources), take(parts * sources)] for _ in chosen]
    piece_refs, query_grad_refs = take(parts), take(sources)
    weight_ref, score_ref = refs
    for number, head in enumerate(chosen):
        keys, values, queries, grads = [stacked(held) for held in inputs[number]]
        query_flip, grad_flip = jnp.transpose(queries), jnp.transpose(grads)
        lines = []
        for ref in dots_refs:
            terms = ref[...].astype(jnp.float32)
            for index in range(dot_groups(rows)):
                line = 2 * (head * dot_groups(rows) + index)
                count = min(LANES, rows - index * LANES)
                lines.append((terms[line : line + 1] + terms[line + 1 : line + 2])[:, :count])
        dots = jnp.concatenate(lines, axis=1)
        totals = jnp.concatenate([ref[head : head + 1] for ref in total_refs], axis=1)
        base = 2 * number * rows
        for first in range(0, slab, KEY_BLOCK):
            stretch = slice(first, first + KEY_BLOCK)
            for start in range(0, sources * slab, QUERY_BLOCK):
                span = slice(start, start + QUERY_BLOCK)
                scores = jnp.dot(keys[stretch], query_flip[:, span], preferred_element_type=jnp.float32)
                weights = jnp.exp2(scores * SCALE_LOG2 - totals[:, span])
                grad_weights = jnp.dot(values[stretch], grad_flip[:, span], preferred_element_type=jnp.float32)
                weight_ref[stretch, span] = weights.astype(jnp.bfloat16)
                score_ref[stretch, span] = (weights * (grad_weights - dots[:, span])).astype(jnp.bfloat16)
            value_grad = jnp.dot(weight_ref[stretch], grads, preferred_element_type=jnp.float32)
            key_grad = jnp.dot(score_ref[stretch], queries, preferred_element_type=jnp.float32) * SCALE
            key_grad, value_grad = key_grad.astype(jnp.bfloat16), value_grad.astype(jnp.bfloat16)
            for part in range(parts):
                low, high = max(first, part * rows), min(first + KEY_BLOCK, (part + 1) * rows)
                if low < high:
                    place = base + low - part * rows
                    local_rows = slice(low - first, high - first)
                    piece_refs[part][place : place + high - low] = key_grad[local_rows]
                    piece_refs[part][place + rows : place + rows + high - low] = value_grad[local_rows]
        for source, ref in enumerate(query_grad_refs):
            query_grad = lax.dot_general(
                score_ref[:, source * slab : (source + 1) * slab],
                keys,
                (((0,), (0,)), ((), ())),
                preferred_element_type=jnp.float32,
            )
            ref[number * slab : (number + 1) * slab] = (query_grad * SCALE).astype(ref.dtype)


def attention(chosen, heads, rows, inputs, dots, totals):
    parts = len(inputs[0][0])
    sources = len(totals)
    slab = parts * rows
    dot_specs, dot_arrays = block_specs(dots_depth(rows, heads), dots)
    in_specs, operands = block_specs(rows, [place for held in inputs for places in held for place in places])
    line = pl.BlockSpec((heads, slab), lambda step: (0, 0))
    depth = 2 * len(chosen) * rows
    out_specs, _ = block_specs(depth, [(None, 0)] * parts)
    query_specs, _ = block_specs(len(chosen) * slab, [(None, 0)] * sources)
    outs = pl.pallas_call(
        functools.partial(attention_kernel, parts, sources, chosen, rows),
        grid=(1,),
        in_specs=dot_specs + [line] * sources + in_specs,
        out_specs=out_specs + query_specs,
        out_shape=[jax.ShapeDtypeStruct((depth, HD), jnp.bfloat16)] * parts
        + [jax.ShapeDtypeStruct((len(chosen) * slab, HD), jnp.float32)]
        + [jax.ShapeDtypeStruct((len(chosen) * slab, HD), jnp.bfloat16)] * (sources - 1),
        scratch_shapes=[pltpu.VMEM((slab, sources * slab), jnp.bfloat16)] * 2,
        compiler_params=params(),
        cost_estimate=pl.CostEstimate(
            flops=10 * len(chosen) * slab * sources * slab * HD,
            bytes_accessed=32 * len(chosen) * slab * HD,
            transcendentals=len(chosen) * slab * sources * slab,
        ),
    )(*dot_arrays, *totals, *operands)
    return outs[:parts], outs[parts:]


def close_kernel(parts, rows, sources, *refs):
    terms, pieces = refs[:-parts], refs[-parts:]
    place = 0
    for first in range(0, len(terms), sources):
        for start in range(0, terms[first].shape[0], parts * rows):
            for part in range(parts):
                span = slice(start + part * rows, start + (part + 1) * rows)
                total = terms[first][span]
                for ref in terms[first + 1 : first + sources]:
                    total = total + ref[span].astype(jnp.float32)
                pieces[part][place : place + rows] = total.astype(jnp.bfloat16)
            place += rows


def close(query_grads, parts, rows):
    depth = sum(terms[0].shape[0] for terms in query_grads) // parts
    return pl.pallas_call(
        functools.partial(close_kernel, parts, rows, len(query_grads[0])),
        out_shape=[jax.ShapeDtypeStruct((depth, HD), jnp.bfloat16)] * parts,
        compiler_params=params(),
        cost_estimate=COST,
    )(*[term for terms in query_grads for term in terms])


def unpack_kernel(parts, rows, heads, stages, *refs):
    count = parts * len(stages)
    pieces, outs, semaphores = refs[:count], refs[count:-1], refs[-1]
    pairs = []
    for number, blocks in enumerate(stages):
        for distance in range(parts):
            piece = pieces[number * parts + distance]
            for index, (output, head) in enumerate(blocks):
                columns = pl.ds(column_of(parts, distance, heads, head), HD)
                pairs.append((piece.at[index * rows : (index + 1) * rows], outs[output].at[:, columns]))
    run_copies(pairs, semaphores)


def unpack(stages, pieces, rows, heads, outputs):
    parts = len(pieces[0])
    whole = pl.BlockSpec(memory_space=pl.ANY)
    channels = parts * heads * HD
    return pl.pallas_call(
        functools.partial(unpack_kernel, parts, rows, heads, stages),
        in_specs=[whole] * (parts * len(stages)),
        out_specs=[whole] * outputs,
        out_shape=[jax.ShapeDtypeStruct((rows, channels), jnp.bfloat16)] * outputs,
        scratch_shapes=[pltpu.SemaphoreType.DMA((outputs * heads * parts,))],
        compiler_params=params(),
        cost_estimate=COST,
    )(*[piece for stage in pieces for piece in stage])


def swap(value, axis, distance):
    return lax.ppermute(value, axis, [(index, index ^ distance) for index in range(lax.axis_size(axis))])


def swap_pieces(pieces, earlier=None):
    held = [pieces[0]]
    for place, distance in enumerate(distances(len(pieces))):
        if distance:
            piece = pieces[place] if earlier is None else after([pieces[place]], earlier[place])[0]
            held.append(swap(piece, "ulysses", distance))
    return held


def tree_sum(values):
    while len(values) > 1:
        values = [functools.reduce(jnp.add, values[index : index + 2]) for index in range(0, len(values), 2)]
    return values[0]


def sum_over(value, axis):
    size = lax.axis_size(axis)
    if size & (size - 1):
        return lax.psum(value, axis)
    return tree_sum([value] + [swap(value, axis, distance) for distance in range(1, size)])


def after(values, *earlier):
    return lax.optimization_barrier((list(values), earlier))[0]


def neighbours(size):
    if size == 1:
        return []
    if size == 2:
        swapped = [(0, 1), (1, 0)]
        return [(swapped, swapped)]
    up = [(index, index + 1) for index in range(size - 1)]
    down = [(index + 1, index) for index in range(size - 1)]
    return [(up, down), (down, up)]


def exchange_totals(partial, sides):
    if not sides:
        return partial
    if len(sides) == 1:
        other = lax.ppermute(jnp.concatenate(partial), "tm", sides[0][0])
        heads = partial[0].shape[0]
        return [join_totals([partial[0], other[heads:]]), join_totals([partial[1], other[:heads]])]
    position = lax.axis_index("tm")
    present = [position < lax.axis_size("tm") - 1, position > 0]
    values = [partial[0]]
    for value, (_, back), flag in zip(partial[1:], sides, present):
        values.append(jnp.where(flag, lax.ppermute(value, "tm", back), -jnp.inf))
    own = join_totals(values)
    return [own] + [lax.ppermute(own, "tm", there) for there, _ in sides]


def local(queries, keys, values, attn_out, out_grad, out_gain):
    parts = lax.axis_size("ulysses")
    span = lax.axis_size("tm")
    rows, channels = queries.shape[1:]
    heads = channels // (parts * HD)
    rest = list(range(1, heads))
    dots = dots_depth(rows, heads)
    every = list(range(parts))
    sides = neighbours(span)

    def forward(array):
        return [lax.ppermute(array, "tm", there) for there, _ in sides]

    with jax.named_scope("keys_queries"):
        packed = pack([keys[0], queries[0]], parts, list(range(heads)))
        pairs = swap_pieces(packed)
    paired = span == 2
    with jax.named_scope("gain"):
        out_grad = after([out_grad], packed[0])[0]
        gain = gain_partial(out_grad[0], attn_out[0]).reshape(-1, LANES)
        gain = sum_over(gain, "dp")
        if not paired:
            gain = sum_over(gain, "tm")
    with jax.named_scope("grads"):
        sent_lead = pack_grads(out_grad[0], attn_out[0], values[0], out_gain, gain, parts)
    with jax.named_scope("halo_own_grads"):
        own_side = forward(sent_lead[0])
    with jax.named_scope("halo_queries"):
        width = heads * rows
        first_side = forward(pairs[0][width:])
    with jax.named_scope("grads"):
        lead = swap_pieces(sent_lead, pairs)
    with jax.named_scope("halo_queries"):
        early_side = forward(pairs[1][width:])
        late = after(pairs[2:], first_side, early_side, sent_lead[0])
        late_side = forward(gather_rows(late, [(number, width, width) for number in range(parts - 2)]))
    base = (heads + 1) * rows
    extra = gain_depth(channels)
    with jax.named_scope("halo_own_grads"):
        own_side = forward(sent_lead[0])
    with jax.named_scope("totals"):
        key_places = [[(piece, head) for piece in pairs] for head in range(heads)]
        query_places = [[[(piece, heads + head) for piece in pairs] for head in range(heads)]]
        for first, second, array in zip(first_side, early_side, late_side):
            query_places.append(
                [
                    [(first, head), (second, head)] + [(array, part * heads + head) for part in range(parts - 2)]
                    for head in range(heads)
                ]
            )
        part_totals = partial_totals(key_places, query_places, rows)
        totals = exchange_totals(after(part_totals, lead[1:]), sides)
    others = range(1, parts)
    with jax.named_scope("halo_first_grads"):
        ranges = [(part, 0, rows) for part in others] + [(part, base, dots + extra) for part in others]
        lead_side = forward(gather_rows(after(lead, part_totals, own_side), ranges))
    with jax.named_scope("rest_values"):
        rest_values = swap_pieces(after(pack([values[0]], parts, rest), part_totals), lead)
    dot_places = [(piece, base // dots) for piece in lead]
    for own, array in zip(own_side, lead_side):
        dot_places.append((own, base // dots))
        step = (dots + extra) // dots
        dot_places += [(array, (parts - 1) * rows // dots + (part - 1) * step) for part in others]

    def inputs_of(head):
        queries_of = [place for source in query_places for place in source[head]]
        if head == 0:
            values_of = [(piece, 1) for piece in lead]
            grads_of = [(piece, 0) for piece in lead]
            for own, array in zip(own_side, lead_side):
                grads_of += [(own, 0)] + [(array, part - 1) for part in others]
        else:
            values_of = [(piece, head - 1) for piece in rest_values]
            grads_of = [(piece, head + 1) for piece in lead]
            for own, array in zip(own_side, rest_side):
                start = (head - 1) * (parts - 1)
                grads_of += [(own, head + 1)] + [(array, start + part - 1) for part in others]
        return [key_places[head], values_of, queries_of, grads_of]

    stages, pieces, open_grads = [], [], []
    gate = rest_values
    for number, chosen in enumerate([[0], rest]):
        if number:
            with jax.named_scope("halo_rest_grads"):
                ranges = [(part, (head + 1) * rows, rows) for head in rest for part in others]
                rest_side = forward(gather_rows(after(lead, leaving[0], rest_values[1:]), ranges))
        with jax.named_scope("attention_%d" % number):
            inputs = [inputs_of(head) for head in chosen]
            leaving, query_grads = attention(chosen, heads, rows, inputs, dot_places, totals)
            totals = after(totals, leaving[0])
        if number:
            query_grads = after(query_grads, gate[1:], open_grads[0][1:])
        with jax.named_scope("halo_query_grads_%d" % number):
            sent_back = [lax.ppermute(other, "tm", back) for other, (_, back) in zip(query_grads[1:], sides)]
            open_grads.append(list(query_grads[:1]) + sent_back)
        with jax.named_scope("returns_%d" % number):
            gate = swap_pieces(leaving, gate)
            pieces.append(gate)
        stages.append([(output, head) for head in chosen for output in (0, 1)])
    key_grad, value_grad = unpack(stages, pieces, rows, heads, 2)
    with jax.named_scope("returns_last"):
        last = swap_pieces(close(open_grads, parts, rows), gate)
    (query_grad,) = unpack([[(0, head) for head in range(heads)]], [last], rows, heads, 1)
    result = (query_grad, key_grad, value_grad)
    with jax.named_scope("gain"):
        places = [(piece, base + dots) for piece in lead]
        if paired:
            places.append((own_side[0], base + dots))
            start = (parts - 1) * rows + dots
            places += [(lead_side[0], start + (part - 1) * (dots + extra)) for part in others]
        gain = gain_total(places, channels // LANES, 1.0 / (rows * span * parts * lax.axis_size("dp")))
    return tuple(grad[None] for grad in result) + (gain.reshape(channels),)


def solution(mesh):
    split = P("dp", ("tm", "ulysses"), None)
    return jax.shard_map(
        local,
        mesh=mesh,
        in_specs=(split,) * 5 + (P(),),
        out_specs=(split,) * 3 + (P(),),
        check_vma=False,
    )
```

```python
import functools
import math

import jax
import jax.numpy as jnp
from jax import lax
from jax.experimental import pallas as pl
from jax.experimental.pallas import tpu as pltpu
from jax.sharding import PartitionSpec as P

HD = 128
LANES = 128
TILE_ROWS = 16
KEY_BLOCK = 256
QUERY_BLOCK = 256
VMEM_LIMIT = 48 * 1024 * 1024
SCALE = 1.0 / math.sqrt(HD)
SCALE_LOG2 = SCALE / math.log(2.0)
COST = pl.CostEstimate(flops=1, bytes_accessed=1, transcendentals=0)


def params():
    return pltpu.CompilerParams(vmem_limit_bytes=VMEM_LIMIT)


def distances(parts):
    return [0] + list(range(parts - 1, 0, -1))


def column_of(parts, place, heads, head):
    partner = lax.axis_index("ulysses") ^ distances(parts)[place]
    return pl.multiple_of((partner * heads + head) * HD, HD)


def run_copies(pairs, semaphores):
    copies = [
        pltpu.make_async_copy(source, target, semaphores.at[index]) for index, (source, target) in enumerate(pairs)
    ]
    for copy in copies:
        copy.start()
    for copy in copies:
        copy.wait()


def pack_kernel(parts, chosen, *refs):
    sources, pieces, semaphores = refs[: -parts - 1], refs[-parts - 1 : -1], refs[-1]
    rows, channels = sources[0].shape
    heads = channels // (parts * HD)
    pairs = []
    for distance in range(parts):
        for half, ref in enumerate(sources):
            for place, head in enumerate(chosen):
                columns = pl.ds(column_of(parts, distance, heads, head), HD)
                start = (half * len(chosen) + place) * rows
                pairs.append((ref.at[:, columns], pieces[distance].at[start : start + rows]))
    run_copies(pairs, semaphores)


def pack(sources, parts, chosen):
    rows = sources[0].shape[0]
    depth = len(sources) * len(chosen) * rows
    whole = pl.BlockSpec(memory_space=pl.ANY)
    return pl.pallas_call(
        functools.partial(pack_kernel, parts, chosen),
        in_specs=[whole] * len(sources),
        out_specs=[whole] * parts,
        out_shape=[jax.ShapeDtypeStruct((depth, HD), sources[0].dtype)] * parts,
        scratch_shapes=[pltpu.SemaphoreType.DMA((len(sources) * len(chosen) * parts,))],
        compiler_params=params(),
        cost_estimate=COST,
    )(*sources)


def gather_kernel(ranges, *refs):
    arrays, out_ref, semaphores = refs[:-2], refs[-2], refs[-1]
    pairs = []
    place = 0
    for number, first, count in ranges:
        pairs.append((arrays[number].at[first : first + count], out_ref.at[place : place + count]))
        place += count
    run_copies(pairs, semaphores)


def gather_rows(arrays, ranges):
    whole = pl.BlockSpec(memory_space=pl.ANY)
    depth = sum(count for _, _, count in ranges)
    return pl.pallas_call(
        functools.partial(gather_kernel, ranges),
        in_specs=[whole] * len(arrays),
        out_specs=whole,
        out_shape=jax.ShapeDtypeStruct((depth, HD), arrays[0].dtype),
        scratch_shapes=[pltpu.SemaphoreType.DMA((len(ranges),))],
        compiler_params=params(),
        cost_estimate=COST,
    )(*arrays)


def dot_groups(rows):
    return -(-rows // LANES)


def dots_depth(rows, heads):
    return -(-2 * heads * dot_groups(rows) // TILE_ROWS) * TILE_ROWS


def gain_kernel(out_grad_ref, attn_ref, out_ref):
    product = out_grad_ref[...].astype(jnp.float32) * attn_ref[...].astype(jnp.float32)
    out_ref[...] = jnp.sum(product, axis=0, keepdims=True)


def gain_partial(out_grad, attn_out):
    return pl.pallas_call(
        gain_kernel,
        out_shape=jax.ShapeDtypeStruct((1, out_grad.shape[1]), jnp.float32),
        compiler_params=params(),
        cost_estimate=COST,
    )(out_grad, attn_out)


def split_terms(value, count):
    terms = []
    for _ in range(count):
        term = value.astype(jnp.bfloat16).astype(jnp.float32)
        terms.append(term)
        value = value - term
    return terms


def gain_depth(channels):
    return -(-3 * channels // LANES // TILE_ROWS) * TILE_ROWS


def pack_grads_kernel(parts, out_grad_ref, attn_ref, value_ref, gain_ref, partial_ref, *refs):
    rows, channels = out_grad_ref.shape
    heads = channels // (parts * HD)
    base = (heads + 1) * rows
    depth = base + dots_depth(rows, heads)
    partial = jnp.concatenate(split_terms(partial_ref[...], 3), axis=0)
    spare = gain_depth(channels) - partial.shape[0]
    if spare:
        partial = jnp.concatenate([partial, jnp.zeros((spare, LANES), jnp.float32)], axis=0)
    for distance in range(parts):
        terms = []
        for head in range(heads):
            columns = pl.ds(column_of(parts, distance, heads, head), HD)
            grad = (out_grad_ref[:, columns].astype(jnp.float32) * gain_ref[:, columns]).astype(jnp.bfloat16)
            place = head + 1 if head else 0
            refs[distance][place * rows : (place + 1) * rows] = grad
            if head == 0:
                refs[distance][rows : 2 * rows] = value_ref[:, columns]
            product = grad.astype(jnp.float32) * attn_ref[:, columns].astype(jnp.float32)
            dots = jnp.sum(jnp.transpose(product), axis=0, keepdims=True)
            for first in range(0, rows, LANES):
                value = dots[:, first : first + LANES]
                if value.shape[1] < LANES:
                    rest = jnp.zeros((1, LANES - value.shape[1]), jnp.float32)
                    value = jnp.concatenate([value, rest], axis=1)
                terms += split_terms(value, 2)
        rest = dots_depth(rows, heads) - len(terms)
        if rest:
            terms.append(jnp.zeros((rest, LANES), jnp.float32))
        refs[distance][base:depth] = jnp.concatenate(terms, axis=0).astype(jnp.bfloat16)
        refs[distance][depth:] = partial.astype(jnp.bfloat16)


def pack_grads(out_grad, attn_out, values, out_gain, partial, parts):
    rows, channels = out_grad.shape
    heads = channels // (parts * HD)
    depth = (heads + 1) * rows + dots_depth(rows, heads) + gain_depth(channels)
    return pl.pallas_call(
        functools.partial(pack_grads_kernel, parts),
        out_shape=[jax.ShapeDtypeStruct((depth, HD), jnp.bfloat16)] * parts,
        compiler_params=params(),
        cost_estimate=COST,
    )(out_grad, attn_out, values, out_gain.reshape(1, channels), partial)


def gain_total_kernel(lines, starts, scale, *refs):
    values = []
    for ref, start in zip(refs[:-1], starts):
        terms = [ref[start + index * lines : start + (index + 1) * lines].astype(jnp.float32) for index in range(3)]
        values.append(terms[0] + terms[1] + terms[2])
    refs[-1][...] = tree_sum(values) * scale


def gain_total(places, lines, scale):
    return pl.pallas_call(
        functools.partial(gain_total_kernel, lines, [start for _, start in places], scale),
        out_shape=jax.ShapeDtypeStruct((lines, LANES), jnp.float32),
        compiler_params=params(),
        cost_estimate=COST,
    )(*[array for array, _ in places])


def stacked(refs):
    return jnp.concatenate([ref[...] for ref in refs], axis=0)


def block_specs(depth, places):
    def block(index):
        return pl.BlockSpec((depth, HD), lambda step: (index, 0))

    return [block(index) for _, index in places], [array for array, _ in places]


def totals_kernel(parts, sources, heads, *refs):
    key_refs, refs = refs[: parts * heads], refs[parts * heads :]
    query_refs, refs = refs[: parts * heads * sources], refs[parts * heads * sources :]
    outs, score_ref = refs[:sources], refs[sources]
    slab = score_ref.shape[0]
    for head in range(heads):
        keys = stacked(key_refs[head * parts : (head + 1) * parts])
        for source in range(sources):
            start = (source * heads + head) * parts
            flip = jnp.transpose(stacked(query_refs[start : start + parts]))
            top = None
            for first in range(0, slab, KEY_BLOCK):
                scores = jnp.dot(keys[first : first + KEY_BLOCK], flip, preferred_element_type=jnp.float32)
                score_ref[first : first + KEY_BLOCK] = scores
                part_top = jnp.max(scores.reshape(-1, 8, slab), axis=0)
                top = part_top if top is None else jnp.maximum(top, part_top)
            top = jnp.max(top, axis=0, keepdims=True) * SCALE_LOG2
            total = None
            for first in range(0, slab, KEY_BLOCK):
                powers = jnp.exp2(score_ref[first : first + KEY_BLOCK] * SCALE_LOG2 - top)
                part_total = jnp.sum(powers.reshape(-1, 8, slab), axis=0)
                total = part_total if total is None else total + part_total
            total = jnp.sum(total, axis=0, keepdims=True)
            outs[source][head : head + 1] = top + jnp.log(total) * (1.0 / math.log(2.0))


def partial_totals(keys, queries, rows):
    heads, parts, sources = len(keys), len(keys[0]), len(queries)
    slab = parts * rows
    places = [place for head in keys for place in head]
    places += [place for source in queries for head in source for place in head]
    in_specs, operands = block_specs(rows, places)
    line = pl.BlockSpec((heads, slab), lambda step: (0, 0))
    return pl.pallas_call(
        functools.partial(totals_kernel, parts, sources, heads),
        grid=(1,),
        in_specs=in_specs,
        out_specs=[line] * sources,
        out_shape=[jax.ShapeDtypeStruct((heads, slab), jnp.float32)] * sources,
        scratch_shapes=[pltpu.VMEM((slab, slab), jnp.float32)],
        compiler_params=params(),
        cost_estimate=pl.CostEstimate(
            flops=2 * heads * sources * slab * slab * HD,
            bytes_accessed=heads * sources * slab * HD * 4,
            transcendentals=heads * sources * slab * slab,
        ),
    )(*operands)


def join_totals(values):
    top = functools.reduce(jnp.maximum, values)
    return top + jnp.log2(functools.reduce(jnp.add, [jnp.exp2(value - top) for value in values]))


def attention_kernel(parts, sources, chosen, rows, *refs):
    slab = parts * rows

    def take(count):
        nonlocal refs
        taken, refs = refs[:count], refs[count:]
        return taken

    dots_refs, total_refs = take(parts * sources), take(sources)
    inputs = [[take(parts), take(parts), take(parts * sources), take(parts * sources)] for _ in chosen]
    piece_refs, query_grad_refs = take(parts), take(sources)
    weight_ref, score_ref = refs
    for number, head in enumerate(chosen):
        keys, values, queries, grads = [stacked(held) for held in inputs[number]]
        query_flip, grad_flip = jnp.transpose(queries), jnp.transpose(grads)
        lines = []
        for ref in dots_refs:
            terms = ref[...].astype(jnp.float32)
            for index in range(dot_groups(rows)):
                line = 2 * (head * dot_groups(rows) + index)
                count = min(LANES, rows - index * LANES)
                lines.append((terms[line : line + 1] + terms[line + 1 : line + 2])[:, :count])
        dots = jnp.concatenate(lines, axis=1)
        totals = jnp.concatenate([ref[head : head + 1] for ref in total_refs], axis=1)
        base = 2 * number * rows
        for first in range(0, slab, KEY_BLOCK):
            stretch = slice(first, first + KEY_BLOCK)
            for start in range(0, sources * slab, QUERY_BLOCK):
                span = slice(start, start + QUERY_BLOCK)
                scores = jnp.dot(keys[stretch], query_flip[:, span], preferred_element_type=jnp.float32)
                weights = jnp.exp2(scores * SCALE_LOG2 - totals[:, span])
                grad_weights = jnp.dot(values[stretch], grad_flip[:, span], preferred_element_type=jnp.float32)
                weight_ref[stretch, span] = weights.astype(jnp.bfloat16)
                score_ref[stretch, span] = (weights * (grad_weights - dots[:, span])).astype(jnp.bfloat16)
            value_grad = jnp.dot(weight_ref[stretch], grads, preferred_element_type=jnp.float32)
            key_grad = jnp.dot(score_ref[stretch], queries, preferred_element_type=jnp.float32) * SCALE
            key_grad, value_grad = key_grad.astype(jnp.bfloat16), value_grad.astype(jnp.bfloat16)
            for part in range(parts):
                low, high = max(first, part * rows), min(first + KEY_BLOCK, (part + 1) * rows)
                if low < high:
                    place = base + low - part * rows
                    local_rows = slice(low - first, high - first)
                    piece_refs[part][place : place + high - low] = key_grad[local_rows]
                    piece_refs[part][place + rows : place + rows + high - low] = value_grad[local_rows]
        for source, ref in enumerate(query_grad_refs):
            query_grad = lax.dot_general(
                score_ref[:, source * slab : (source + 1) * slab],
                keys,
                (((0,), (0,)), ((), ())),
                preferred_element_type=jnp.float32,
            )
            ref[number * slab : (number + 1) * slab] = (query_grad * SCALE).astype(ref.dtype)


def attention(chosen, heads, rows, inputs, dots, totals):
    parts = len(inputs[0][0])
    sources = len(totals)
    slab = parts * rows
    dot_specs, dot_arrays = block_specs(dots_depth(rows, heads), dots)
    in_specs, operands = block_specs(rows, [place for held in inputs for places in held for place in places])
    line = pl.BlockSpec((heads, slab), lambda step: (0, 0))
    depth = 2 * len(chosen) * rows
    out_specs, _ = block_specs(depth, [(None, 0)] * parts)
    query_specs, _ = block_specs(len(chosen) * slab, [(None, 0)] * sources)
    outs = pl.pallas_call(
        functools.partial(attention_kernel, parts, sources, chosen, rows),
        grid=(1,),
        in_specs=dot_specs + [line] * sources + in_specs,
        out_specs=out_specs + query_specs,
        out_shape=[jax.ShapeDtypeStruct((depth, HD), jnp.bfloat16)] * parts
        + [jax.ShapeDtypeStruct((len(chosen) * slab, HD), jnp.float32)]
        + [jax.ShapeDtypeStruct((len(chosen) * slab, HD), jnp.bfloat16)] * (sources - 1),
        scratch_shapes=[pltpu.VMEM((slab, sources * slab), jnp.bfloat16)] * 2,
        compiler_params=params(),
        cost_estimate=pl.CostEstimate(
            flops=10 * len(chosen) * slab * sources * slab * HD,
            bytes_accessed=32 * len(chosen) * slab * HD,
            transcendentals=len(chosen) * slab * sources * slab,
        ),
    )(*dot_arrays, *totals, *operands)
    return outs[:parts], outs[parts:]


def close_kernel(parts, rows, sources, *refs):
    terms, pieces = refs[:-parts], refs[-parts:]
    place = 0
    for first in range(0, len(terms), sources):
        for start in range(0, terms[first].shape[0], parts * rows):
            for part in range(parts):
                span = slice(start + part * rows, start + (part + 1) * rows)
                total = terms[first][span]
                for ref in terms[first + 1 : first + sources]:
                    total = total + ref[span].astype(jnp.float32)
                pieces[part][place : place + rows] = total.astype(jnp.bfloat16)
            place += rows


def close(query_grads, parts, rows):
    depth = sum(terms[0].shape[0] for terms in query_grads) // parts
    return pl.pallas_call(
        functools.partial(close_kernel, parts, rows, len(query_grads[0])),
        out_shape=[jax.ShapeDtypeStruct((depth, HD), jnp.bfloat16)] * parts,
        compiler_params=params(),
        cost_estimate=COST,
    )(*[term for terms in query_grads for term in terms])


def unpack_kernel(parts, rows, heads, stages, *refs):
    count = parts * len(stages)
    pieces, outs, semaphores = refs[:count], refs[count:-1], refs[-1]
    pairs = []
    for number, blocks in enumerate(stages):
        for distance in range(parts):
            piece = pieces[number * parts + distance]
            for index, (output, head) in enumerate(blocks):
                columns = pl.ds(column_of(parts, distance, heads, head), HD)
                pairs.append((piece.at[index * rows : (index + 1) * rows], outs[output].at[:, columns]))
    run_copies(pairs, semaphores)


def unpack(stages, pieces, rows, heads, outputs):
    parts = len(pieces[0])
    whole = pl.BlockSpec(memory_space=pl.ANY)
    channels = parts * heads * HD
    return pl.pallas_call(
        functools.partial(unpack_kernel, parts, rows, heads, stages),
        in_specs=[whole] * (parts * len(stages)),
        out_specs=[whole] * outputs,
        out_shape=[jax.ShapeDtypeStruct((rows, channels), jnp.bfloat16)] * outputs,
        scratch_shapes=[pltpu.SemaphoreType.DMA((outputs * heads * parts,))],
        compiler_params=params(),
        cost_estimate=COST,
    )(*[piece for stage in pieces for piece in stage])


def swap(value, axis, distance):
    return lax.ppermute(value, axis, [(index, index ^ distance) for index in range(lax.axis_size(axis))])


def swap_pieces(pieces, earlier=None):
    held = [pieces[0]]
    for place, distance in enumerate(distances(len(pieces))):
        if distance:
            piece = pieces[place] if earlier is None else after([pieces[place]], earlier[place])[0]
            held.append(swap(piece, "ulysses", distance))
    return held


def tree_sum(values):
    while len(values) > 1:
        values = [functools.reduce(jnp.add, values[index : index + 2]) for index in range(0, len(values), 2)]
    return values[0]


def sum_over(value, axis):
    size = lax.axis_size(axis)
    if size & (size - 1):
        return lax.psum(value, axis)
    return tree_sum([value] + [swap(value, axis, distance) for distance in range(1, size)])


def after(values, *earlier):
    return lax.optimization_barrier((list(values), earlier))[0]


def neighbours(size):
    if size == 1:
        return []
    if size == 2:
        swapped = [(0, 1), (1, 0)]
        return [(swapped, swapped)]
    up = [(index, index + 1) for index in range(size - 1)]
    down = [(index + 1, index) for index in range(size - 1)]
    return [(up, down), (down, up)]


def exchange_totals(partial, sides):
    if not sides:
        return partial
    if len(sides) == 1:
        other = lax.ppermute(jnp.concatenate(partial), "tm", sides[0][0])
        heads = partial[0].shape[0]
        return [join_totals([partial[0], other[heads:]]), join_totals([partial[1], other[:heads]])]
    position = lax.axis_index("tm")
    present = [position < lax.axis_size("tm") - 1, position > 0]
    values = [partial[0]]
    for value, (_, back), flag in zip(partial[1:], sides, present):
        values.append(jnp.where(flag, lax.ppermute(value, "tm", back), -jnp.inf))
    own = join_totals(values)
    return [own] + [lax.ppermute(own, "tm", there) for there, _ in sides]


def local(queries, keys, values, attn_out, out_grad, out_gain):
    parts = lax.axis_size("ulysses")
    span = lax.axis_size("tm")
    rows, channels = queries.shape[1:]
    heads = channels // (parts * HD)
    rest = list(range(1, heads))
    dots = dots_depth(rows, heads)
    every = list(range(parts))
    sides = neighbours(span)

    def forward(array):
        return [lax.ppermute(array, "tm", there) for there, _ in sides]

    with jax.named_scope("keys_queries"):
        packed = pack([keys[0], queries[0]], parts, list(range(heads)))
        pairs = [packed[0]] + after(swap_pieces(packed)[:0:-1], [])[::-1]
    paired = span == 2
    with jax.named_scope("gain"):
        out_grad = after([out_grad], packed[0])[0]
        gain = gain_partial(out_grad[0], attn_out[0]).reshape(-1, LANES)
        gain = sum_over(gain, "dp")
        if not paired:
            gain = sum_over(gain, "tm")
    with jax.named_scope("grads"):
        sent_lead = pack_grads(out_grad[0], attn_out[0], values[0], out_gain, gain, parts)
    with jax.named_scope("halo_own_grads"):
        own_side = forward(sent_lead[0])
    with jax.named_scope("halo_queries"):
        width = heads * rows
        first_side = forward(pairs[0][width:])
    with jax.named_scope("grads"):
        lead = swap_pieces(sent_lead, pairs)
    with jax.named_scope("halo_queries"):
        late = after(pairs[1:], first_side, sent_lead[0])
        late_side = forward(gather_rows(late, [(number, width, width) for number in range(parts - 1)]))
    base = (heads + 1) * rows
    extra = gain_depth(channels)
    with jax.named_scope("totals"):
        key_places = [[(piece, head) for piece in pairs] for head in range(heads)]
        query_places = [[[(piece, heads + head) for piece in pairs] for head in range(heads)]]
        for first, others in zip(first_side, late_side):
            query_places.append(
                [
                    [(first, head)] + [(others, (part - 1) * heads + head) for part in every[1:]]
                    for head in range(heads)
                ]
            )
        part_totals = partial_totals(key_places, query_places, rows)
        totals = exchange_totals(after(part_totals, lead[1:]), sides)
    others = range(1, parts)
    with jax.named_scope("halo_first_grads"):
        ranges = [(part, 0, rows) for part in others] + [(part, base, dots + extra) for part in others]
        lead_side = forward(gather_rows(after(lead, part_totals, own_side), ranges))
    with jax.named_scope("rest_values"):
        rest_values = swap_pieces(after(pack([values[0]], parts, rest), part_totals), lead)
    dot_places = [(piece, base // dots) for piece in lead]
    for own, array in zip(own_side, lead_side):
        dot_places.append((own, base // dots))
        step = (dots + extra) // dots
        dot_places += [(array, (parts - 1) * rows // dots + (part - 1) * step) for part in others]

    def inputs_of(head):
        queries_of = [place for source in query_places for place in source[head]]
        if head == 0:
            values_of = [(piece, 1) for piece in lead]
            grads_of = [(piece, 0) for piece in lead]
            for own, array in zip(own_side, lead_side):
                grads_of += [(own, 0)] + [(array, part - 1) for part in others]
        else:
            values_of = [(piece, head - 1) for piece in rest_values]
            grads_of = [(piece, head + 1) for piece in lead]
            for own, array in zip(own_side, rest_side):
                start = (head - 1) * (parts - 1)
                grads_of += [(own, head + 1)] + [(array, start + part - 1) for part in others]
        return [key_places[head], values_of, queries_of, grads_of]

    stages, pieces, open_grads = [], [], []
    gate = rest_values
    for number, chosen in enumerate([[0], rest]):
        if number:
            with jax.named_scope("halo_rest_grads"):
                ranges = [(part, (head + 1) * rows, rows) for head in rest for part in others]
                rest_side = forward(gather_rows(after(lead, lead_side), ranges))
        with jax.named_scope("attention_%d" % number):
            inputs = [inputs_of(head) for head in chosen]
            leaving, query_grads = attention(chosen, heads, rows, inputs, dot_places, totals)
            totals = after(totals, leaving[0])
        if number:
            query_grads = after(query_grads, gate[1:], open_grads[0][1:])
        with jax.named_scope("halo_query_grads_%d" % number):
            sent_back = [lax.ppermute(other, "tm", back) for other, (_, back) in zip(query_grads[1:], sides)]
            open_grads.append(list(query_grads[:1]) + sent_back)
        with jax.named_scope("returns_%d" % number):
            gate = swap_pieces(leaving, gate)
            pieces.append(gate)
        stages.append([(output, head) for head in chosen for output in (0, 1)])
    key_grad, value_grad = unpack(stages, pieces, rows, heads, 2)
    with jax.named_scope("returns_last"):
        last = swap_pieces(close(open_grads, parts, rows), gate)
    (query_grad,) = unpack([[(0, head) for head in range(heads)]], [last], rows, heads, 1)
    result = (query_grad, key_grad, value_grad)
    with jax.named_scope("gain"):
        places = [(piece, base + dots) for piece in lead]
        if paired:
            places.append((own_side[0], base + dots))
            start = (parts - 1) * rows + dots
            places += [(lead_side[0], start + (part - 1) * (dots + extra)) for part in others]
        gain = gain_total(places, channels // LANES, 1.0 / (rows * span * parts * lax.axis_size("dp")))
    return tuple(grad[None] for grad in result) + (gain.reshape(channels),)


def solution(mesh):
    split = P("dp", ("tm", "ulysses"), None)
    return jax.shard_map(
        local,
        mesh=mesh,
        in_specs=(split,) * 5 + (P(),),
        out_specs=(split,) * 3 + (P(),),
        check_vma=False,
    )
```

```python
import functools
import math

import jax
import jax.numpy as jnp
from jax import lax
from jax.experimental import pallas as pl
from jax.experimental.pallas import tpu as pltpu
from jax.sharding import PartitionSpec as P

HD = 128
LANES = 128
TILE_ROWS = 16
KEY_BLOCK = 256
QUERY_BLOCK = 256
VMEM_LIMIT = 48 * 1024 * 1024
VMEM_WHOLE = 62 * 1024 * 1024
SCALE = 1.0 / math.sqrt(HD)
SCALE_LOG2 = SCALE / math.log(2.0)
COST = pl.CostEstimate(flops=1, bytes_accessed=1, transcendentals=0)


def params():
    return pltpu.CompilerParams(vmem_limit_bytes=VMEM_LIMIT)


def distances(parts):
    return [0] + list(range(parts - 1, 0, -1))


def column_of(parts, place, heads, head):
    partner = lax.axis_index("ulysses") ^ distances(parts)[place]
    return pl.multiple_of((partner * heads + head) * HD, HD)


def run_copies(pairs, semaphores):
    copies = [
        pltpu.make_async_copy(source, target, semaphores.at[index]) for index, (source, target) in enumerate(pairs)
    ]
    for copy in copies:
        copy.start()
    for copy in copies:
        copy.wait()


def pack_kernel(parts, chosen, *refs):
    sources, pieces, semaphores = refs[: -parts - 1], refs[-parts - 1 : -1], refs[-1]
    rows, channels = sources[0].shape
    heads = channels // (parts * HD)
    pairs = []
    for distance in range(parts):
        for half, ref in enumerate(sources):
            for place, head in enumerate(chosen):
                columns = pl.ds(column_of(parts, distance, heads, head), HD)
                start = (half * len(chosen) + place) * rows
                pairs.append((ref.at[:, columns], pieces[distance].at[start : start + rows]))
    run_copies(pairs, semaphores)


def pack(sources, parts, chosen, limit=VMEM_LIMIT):
    rows = sources[0].shape[0]
    depth = len(sources) * len(chosen) * rows
    whole = pl.BlockSpec(memory_space=pl.ANY)
    return pl.pallas_call(
        functools.partial(pack_kernel, parts, chosen),
        in_specs=[whole] * len(sources),
        out_specs=[pl.BlockSpec(memory_space=pltpu.VMEM)] * parts,
        out_shape=[jax.ShapeDtypeStruct((depth, HD), sources[0].dtype)] * parts,
        scratch_shapes=[pltpu.SemaphoreType.DMA((len(sources) * len(chosen) * parts,))],
        compiler_params=pltpu.CompilerParams(vmem_limit_bytes=limit),
        cost_estimate=COST,
    )(*sources)


def gather_kernel(ranges, *refs):
    arrays, out_ref, semaphores = refs[:-2], refs[-2], refs[-1]
    pairs = []
    place = 0
    for number, first, count in ranges:
        pairs.append((arrays[number].at[first : first + count], out_ref.at[place : place + count]))
        place += count
    run_copies(pairs, semaphores)


def gather_rows(arrays, ranges):
    whole = pl.BlockSpec(memory_space=pl.ANY)
    depth = sum(count for _, _, count in ranges)
    return pl.pallas_call(
        functools.partial(gather_kernel, ranges),
        in_specs=[whole] * len(arrays),
        out_specs=whole,
        out_shape=jax.ShapeDtypeStruct((depth, HD), arrays[0].dtype),
        scratch_shapes=[pltpu.SemaphoreType.DMA((len(ranges),))],
        compiler_params=params(),
        cost_estimate=COST,
    )(*arrays)


def dot_groups(rows):
    return -(-rows // LANES)


def dots_depth(rows, heads):
    return -(-2 * heads * dot_groups(rows) // TILE_ROWS) * TILE_ROWS


def gain_kernel(out_grad_ref, attn_ref, out_ref):
    product = out_grad_ref[...].astype(jnp.float32) * attn_ref[...].astype(jnp.float32)
    out_ref[...] = jnp.sum(product, axis=0, keepdims=True)


def gain_partial(out_grad, attn_out):
    return pl.pallas_call(
        gain_kernel,
        out_shape=jax.ShapeDtypeStruct((1, out_grad.shape[1]), jnp.float32),
        compiler_params=params(),
        cost_estimate=COST,
    )(out_grad, attn_out)


def split_terms(value, count):
    terms = []
    for _ in range(count):
        term = value.astype(jnp.bfloat16).astype(jnp.float32)
        terms.append(term)
        value = value - term
    return terms


def gain_depth(channels):
    return -(-3 * channels // LANES // TILE_ROWS) * TILE_ROWS


def pack_grads_kernel(parts, out_grad_ref, attn_ref, value_ref, gain_ref, partial_ref, *refs):
    rows, channels = out_grad_ref.shape
    heads = channels // (parts * HD)
    base = (heads + 1) * rows
    depth = base + dots_depth(rows, heads)
    partial = jnp.concatenate(split_terms(partial_ref[...], 3), axis=0)
    spare = gain_depth(channels) - partial.shape[0]
    if spare:
        partial = jnp.concatenate([partial, jnp.zeros((spare, LANES), jnp.float32)], axis=0)
    for distance in range(parts):
        terms = []
        for head in range(heads):
            columns = pl.ds(column_of(parts, distance, heads, head), HD)
            grad = (out_grad_ref[:, columns].astype(jnp.float32) * gain_ref[:, columns]).astype(jnp.bfloat16)
            place = head + 1 if head else 0
            refs[distance][place * rows : (place + 1) * rows] = grad
            if head == 0:
                refs[distance][rows : 2 * rows] = value_ref[:, columns]
            product = grad.astype(jnp.float32) * attn_ref[:, columns].astype(jnp.float32)
            dots = jnp.sum(jnp.transpose(product), axis=0, keepdims=True)
            for first in range(0, rows, LANES):
                value = dots[:, first : first + LANES]
                if value.shape[1] < LANES:
                    rest = jnp.zeros((1, LANES - value.shape[1]), jnp.float32)
                    value = jnp.concatenate([value, rest], axis=1)
                terms += split_terms(value, 2)
        rest = dots_depth(rows, heads) - len(terms)
        if rest:
            terms.append(jnp.zeros((rest, LANES), jnp.float32))
        refs[distance][base:depth] = jnp.concatenate(terms, axis=0).astype(jnp.bfloat16)
        refs[distance][depth:] = partial.astype(jnp.bfloat16)


def pack_grads(out_grad, attn_out, values, out_gain, partial, parts):
    rows, channels = out_grad.shape
    heads = channels // (parts * HD)
    depth = (heads + 1) * rows + dots_depth(rows, heads) + gain_depth(channels)
    return pl.pallas_call(
        functools.partial(pack_grads_kernel, parts),
        out_shape=[jax.ShapeDtypeStruct((depth, HD), jnp.bfloat16)] * parts,
        compiler_params=params(),
        cost_estimate=COST,
    )(out_grad, attn_out, values, out_gain.reshape(1, channels), partial)


def gain_total_kernel(lines, starts, scale, *refs):
    values = []
    for ref, start in zip(refs[:-1], starts):
        terms = [ref[start + index * lines : start + (index + 1) * lines].astype(jnp.float32) for index in range(3)]
        values.append(terms[0] + terms[1] + terms[2])
    refs[-1][...] = tree_sum(values) * scale


def gain_total(places, lines, scale):
    return pl.pallas_call(
        functools.partial(gain_total_kernel, lines, [start for _, start in places], scale),
        out_shape=jax.ShapeDtypeStruct((lines, LANES), jnp.float32),
        compiler_params=params(),
        cost_estimate=COST,
    )(*[array for array, _ in places])


def stacked(refs):
    return jnp.concatenate([ref[...] for ref in refs], axis=0)


def block_specs(depth, places):
    def block(index):
        return pl.BlockSpec((depth, HD), lambda step: (index, 0))

    return [block(index) for _, index in places], [array for array, _ in places]


def totals_kernel(parts, sources, heads, *refs):
    key_refs, refs = refs[: parts * heads], refs[parts * heads :]
    query_refs, refs = refs[: parts * heads * sources], refs[parts * heads * sources :]
    outs, score_ref = refs[:sources], refs[sources]
    slab = score_ref.shape[0]
    for head in range(heads):
        keys = stacked(key_refs[head * parts : (head + 1) * parts])
        for source in range(sources):
            start = (source * heads + head) * parts
            flip = jnp.transpose(stacked(query_refs[start : start + parts]))
            top = None
            for first in range(0, slab, KEY_BLOCK):
                scores = jnp.dot(keys[first : first + KEY_BLOCK], flip, preferred_element_type=jnp.float32)
                score_ref[first : first + KEY_BLOCK] = scores
                part_top = jnp.max(scores.reshape(-1, 8, slab), axis=0)
                top = part_top if top is None else jnp.maximum(top, part_top)
            top = jnp.max(top, axis=0, keepdims=True) * SCALE_LOG2
            total = None
            for first in range(0, slab, KEY_BLOCK):
                powers = jnp.exp2(score_ref[first : first + KEY_BLOCK] * SCALE_LOG2 - top)
                part_total = jnp.sum(powers.reshape(-1, 8, slab), axis=0)
                total = part_total if total is None else total + part_total
            total = jnp.sum(total, axis=0, keepdims=True)
            outs[source][head : head + 1] = top + jnp.log(total) * (1.0 / math.log(2.0))


def partial_totals(keys, queries, rows):
    heads, parts, sources = len(keys), len(keys[0]), len(queries)
    slab = parts * rows
    places = [place for head in keys for place in head]
    places += [place for source in queries for head in source for place in head]
    in_specs, operands = block_specs(rows, places)
    line = pl.BlockSpec((heads, slab), lambda step: (0, 0))
    return pl.pallas_call(
        functools.partial(totals_kernel, parts, sources, heads),
        grid=(1,),
        in_specs=in_specs,
        out_specs=[line] * sources,
        out_shape=[jax.ShapeDtypeStruct((heads, slab), jnp.float32)] * sources,
        scratch_shapes=[pltpu.VMEM((slab, slab), jnp.float32)],
        compiler_params=params(),
        cost_estimate=pl.CostEstimate(
            flops=2 * heads * sources * slab * slab * HD,
            bytes_accessed=heads * sources * slab * HD * 4,
            transcendentals=heads * sources * slab * slab,
        ),
    )(*operands)


def join_totals(values):
    top = functools.reduce(jnp.maximum, values)
    return top + jnp.log2(functools.reduce(jnp.add, [jnp.exp2(value - top) for value in values]))


def attention_kernel(parts, sources, chosen, rows, *refs):
    slab = parts * rows

    def take(count):
        nonlocal refs
        taken, refs = refs[:count], refs[count:]
        return taken

    dots_refs, total_refs = take(parts * sources), take(sources)
    inputs = [[take(parts), take(parts), take(parts * sources), take(parts * sources)] for _ in chosen]
    piece_refs, query_grad_refs = take(parts), take(sources)
    weight_ref, score_ref = refs
    for number, head in enumerate(chosen):
        keys, values, queries, grads = [stacked(held) for held in inputs[number]]
        query_flip, grad_flip = jnp.transpose(queries), jnp.transpose(grads)
        lines = []
        for ref in dots_refs:
            terms = ref[...].astype(jnp.float32)
            for index in range(dot_groups(rows)):
                line = 2 * (head * dot_groups(rows) + index)
                count = min(LANES, rows - index * LANES)
                lines.append((terms[line : line + 1] + terms[line + 1 : line + 2])[:, :count])
        dots = jnp.concatenate(lines, axis=1)
        totals = jnp.concatenate([ref[head : head + 1] for ref in total_refs], axis=1)
        base = 2 * number * rows
        for first in range(0, slab, KEY_BLOCK):
            stretch = slice(first, first + KEY_BLOCK)
            for start in range(0, sources * slab, QUERY_BLOCK):
                span = slice(start, start + QUERY_BLOCK)
                scores = jnp.dot(keys[stretch], query_flip[:, span], preferred_element_type=jnp.float32)
                weights = jnp.exp2(scores * SCALE_LOG2 - totals[:, span])
                grad_weights = jnp.dot(values[stretch], grad_flip[:, span], preferred_element_type=jnp.float32)
                weight_ref[stretch, span] = weights.astype(jnp.bfloat16)
                score_ref[stretch, span] = (weights * (grad_weights - dots[:, span])).astype(jnp.bfloat16)
            value_grad = jnp.dot(weight_ref[stretch], grads, preferred_element_type=jnp.float32)
            key_grad = jnp.dot(score_ref[stretch], queries, preferred_element_type=jnp.float32) * SCALE
            key_grad, value_grad = key_grad.astype(jnp.bfloat16), value_grad.astype(jnp.bfloat16)
            for part in range(parts):
                low, high = max(first, part * rows), min(first + KEY_BLOCK, (part + 1) * rows)
                if low < high:
                    place = base + low - part * rows
                    local_rows = slice(low - first, high - first)
                    piece_refs[part][place : place + high - low] = key_grad[local_rows]
                    piece_refs[part][place + rows : place + rows + high - low] = value_grad[local_rows]
        for source, ref in enumerate(query_grad_refs):
            query_grad = lax.dot_general(
                score_ref[:, source * slab : (source + 1) * slab],
                keys,
                (((0,), (0,)), ((), ())),
                preferred_element_type=jnp.float32,
            )
            ref[number * slab : (number + 1) * slab] = (query_grad * SCALE).astype(ref.dtype)


def attention(chosen, heads, rows, inputs, dots, totals):
    parts = len(inputs[0][0])
    sources = len(totals)
    slab = parts * rows
    dot_specs, dot_arrays = block_specs(dots_depth(rows, heads), dots)
    in_specs, operands = block_specs(rows, [place for held in inputs for places in held for place in places])
    line = pl.BlockSpec((heads, slab), lambda step: (0, 0))
    depth = 2 * len(chosen) * rows
    out_specs, _ = block_specs(depth, [(None, 0)] * parts)
    query_specs, _ = block_specs(len(chosen) * slab, [(None, 0)] * sources)
    outs = pl.pallas_call(
        functools.partial(attention_kernel, parts, sources, chosen, rows),
        grid=(1,),
        in_specs=dot_specs + [line] * sources + in_specs,
        out_specs=out_specs + query_specs,
        out_shape=[jax.ShapeDtypeStruct((depth, HD), jnp.bfloat16)] * parts
        + [jax.ShapeDtypeStruct((len(chosen) * slab, HD), jnp.float32)]
        + [jax.ShapeDtypeStruct((len(chosen) * slab, HD), jnp.bfloat16)] * (sources - 1),
        scratch_shapes=[pltpu.VMEM((slab, sources * slab), jnp.bfloat16)] * 2,
        compiler_params=params(),
        cost_estimate=pl.CostEstimate(
            flops=10 * len(chosen) * slab * sources * slab * HD,
            bytes_accessed=32 * len(chosen) * slab * HD,
            transcendentals=len(chosen) * slab * sources * slab,
        ),
    )(*dot_arrays, *totals, *operands)
    return outs[:parts], outs[parts:]


def close_kernel(parts, rows, sources, *refs):
    terms, pieces = refs[:-parts], refs[-parts:]
    place = 0
    for first in range(0, len(terms), sources):
        for start in range(0, terms[first].shape[0], parts * rows):
            for part in range(parts):
                span = slice(start + part * rows, start + (part + 1) * rows)
                total = terms[first][span]
                for ref in terms[first + 1 : first + sources]:
                    total = total + ref[span].astype(jnp.float32)
                pieces[part][place : place + rows] = total.astype(jnp.bfloat16)
            place += rows


def close(query_grads, parts, rows):
    depth = sum(terms[0].shape[0] for terms in query_grads) // parts
    return pl.pallas_call(
        functools.partial(close_kernel, parts, rows, len(query_grads[0])),
        out_shape=[jax.ShapeDtypeStruct((depth, HD), jnp.bfloat16)] * parts,
        compiler_params=params(),
        cost_estimate=COST,
    )(*[term for terms in query_grads for term in terms])


def unpack_kernel(parts, rows, heads, stages, *refs):
    count = parts * len(stages)
    pieces, outs, semaphores = refs[:count], refs[count:-1], refs[-1]
    pairs = []
    for number, blocks in enumerate(stages):
        for distance in range(parts):
            piece = pieces[number * parts + distance]
            for index, (output, head) in enumerate(blocks):
                columns = pl.ds(column_of(parts, distance, heads, head), HD)
                pairs.append((piece.at[index * rows : (index + 1) * rows], outs[output].at[:, columns]))
    run_copies(pairs, semaphores)


def unpack(stages, pieces, rows, heads, outputs):
    parts = len(pieces[0])
    whole = pl.BlockSpec(memory_space=pl.ANY)
    channels = parts * heads * HD
    return pl.pallas_call(
        functools.partial(unpack_kernel, parts, rows, heads, stages),
        in_specs=[whole] * (parts * len(stages)),
        out_specs=[whole] * outputs,
        out_shape=[jax.ShapeDtypeStruct((rows, channels), jnp.bfloat16)] * outputs,
        scratch_shapes=[pltpu.SemaphoreType.DMA((outputs * heads * parts,))],
        compiler_params=params(),
        cost_estimate=COST,
    )(*[piece for stage in pieces for piece in stage])


def swap(value, axis, distance):
    return lax.ppermute(value, axis, [(index, index ^ distance) for index in range(lax.axis_size(axis))])


def swap_pieces(pieces, earlier=None):
    held = [pieces[0]]
    for place, distance in enumerate(distances(len(pieces))):
        if distance:
            piece = pieces[place] if earlier is None else after([pieces[place]], earlier[place])[0]
            held.append(swap(piece, "ulysses", distance))
    return held


def tree_sum(values):
    while len(values) > 1:
        values = [functools.reduce(jnp.add, values[index : index + 2]) for index in range(0, len(values), 2)]
    return values[0]


def sum_over(value, axis):
    size = lax.axis_size(axis)
    if size & (size - 1):
        return lax.psum(value, axis)
    return tree_sum([value] + [swap(value, axis, distance) for distance in range(1, size)])


def after(values, *earlier):
    return lax.optimization_barrier((list(values), earlier))[0]


def neighbours(size):
    if size == 1:
        return []
    if size == 2:
        swapped = [(0, 1), (1, 0)]
        return [(swapped, swapped)]
    up = [(index, index + 1) for index in range(size - 1)]
    down = [(index + 1, index) for index in range(size - 1)]
    return [(up, down), (down, up)]


def exchange_totals(partial, sides):
    if not sides:
        return partial
    if len(sides) == 1:
        other = lax.ppermute(jnp.concatenate(partial), "tm", sides[0][0])
        heads = partial[0].shape[0]
        return [join_totals([partial[0], other[heads:]]), join_totals([partial[1], other[:heads]])]
    position = lax.axis_index("tm")
    present = [position < lax.axis_size("tm") - 1, position > 0]
    values = [partial[0]]
    for value, (_, back), flag in zip(partial[1:], sides, present):
        values.append(jnp.where(flag, lax.ppermute(value, "tm", back), -jnp.inf))
    own = join_totals(values)
    return [own] + [lax.ppermute(own, "tm", there) for there, _ in sides]


def local(queries, keys, values, attn_out, out_grad, out_gain):
    parts = lax.axis_size("ulysses")
    span = lax.axis_size("tm")
    rows, channels = queries.shape[1:]
    heads = channels // (parts * HD)
    rest = list(range(1, heads))
    dots = dots_depth(rows, heads)
    every = list(range(parts))
    sides = neighbours(span)

    def forward(array):
        return [lax.ppermute(array, "tm", there) for there, _ in sides]

    with jax.named_scope("keys_queries"):
        packed = pack([keys[0], queries[0]], parts, list(range(heads)), VMEM_WHOLE)
        pairs = [packed[0]] + after(swap_pieces(packed)[:0:-1], [])[::-1]
    paired = span == 2
    with jax.named_scope("gain"):
        out_grad = after([out_grad], packed[0])[0]
        gain = gain_partial(out_grad[0], attn_out[0]).reshape(-1, LANES)
        gain = sum_over(gain, "dp")
        if not paired:
            gain = sum_over(gain, "tm")
    with jax.named_scope("grads"):
        sent_lead = pack_grads(out_grad[0], attn_out[0], values[0], out_gain, gain, parts)
    with jax.named_scope("halo_queries"):
        width = heads * rows
        first_side = forward(pairs[0][width:])
    with jax.named_scope("grads"):
        lead = swap_pieces(sent_lead, pairs)
    with jax.named_scope("halo_queries"):
        late = after(pairs[1:], first_side, sent_lead[0])
        late_side = forward(gather_rows(late, [(number, width, width) for number in range(parts - 1)]))
    base = (heads + 1) * rows
    extra = gain_depth(channels)
    with jax.named_scope("halo_own_grads"):
        own_side = forward(after(sent_lead[:1], late_side)[0])
    with jax.named_scope("totals"):
        key_places = [[(piece, head) for piece in pairs] for head in range(heads)]
        query_places = [[[(piece, heads + head) for piece in pairs] for head in range(heads)]]
        for first, others in zip(first_side, late_side):
            query_places.append(
                [
                    [(first, head)] + [(others, (part - 1) * heads + head) for part in every[1:]]
                    for head in range(heads)
                ]
            )
        part_totals = partial_totals(key_places, query_places, rows)
        totals = exchange_totals(after(part_totals, lead[1:]), sides)
    others = range(1, parts)
    with jax.named_scope("halo_first_grads"):
        ranges = [(part, 0, rows) for part in others] + [(part, base, dots + extra) for part in others]
        lead_side = forward(gather_rows(after(lead, part_totals, own_side), ranges))
    with jax.named_scope("rest_values"):
        rest_values = swap_pieces(after(pack([values[0]], parts, rest), part_totals), lead)
    dot_places = [(piece, base // dots) for piece in lead]
    for own, array in zip(own_side, lead_side):
        dot_places.append((own, base // dots))
        step = (dots + extra) // dots
        dot_places += [(array, (parts - 1) * rows // dots + (part - 1) * step) for part in others]

    def inputs_of(head):
        queries_of = [place for source in query_places for place in source[head]]
        if head == 0:
            values_of = [(piece, 1) for piece in lead]
            grads_of = [(piece, 0) for piece in lead]
            for own, array in zip(own_side, lead_side):
                grads_of += [(own, 0)] + [(array, part - 1) for part in others]
        else:
            values_of = [(piece, head - 1) for piece in rest_values]
            grads_of = [(piece, head + 1) for piece in lead]
            for own, array in zip(own_side, rest_side):
                start = (head - 1) * (parts - 1)
                grads_of += [(own, head + 1)] + [(array, start + part - 1) for part in others]
        return [key_places[head], values_of, queries_of, grads_of]

    stages, pieces, open_grads = [], [], []
    gate = rest_values
    for number, chosen in enumerate([[0], rest]):
        if number:
            with jax.named_scope("halo_rest_grads"):
                ranges = [(part, (head + 1) * rows, rows) for head in rest for part in others]
                rest_side = forward(gather_rows(after(lead, lead_side), ranges))
        with jax.named_scope("attention_%d" % number):
            inputs = [inputs_of(head) for head in chosen]
            leaving, query_grads = attention(chosen, heads, rows, inputs, dot_places, totals)
            totals = after(totals, leaving[0])
        if number:
            query_grads = after(query_grads, gate[1:], open_grads[0][1:])
        with jax.named_scope("halo_query_grads_%d" % number):
            sent_back = [lax.ppermute(other, "tm", back) for other, (_, back) in zip(query_grads[1:], sides)]
            open_grads.append(list(query_grads[:1]) + sent_back)
        with jax.named_scope("returns_%d" % number):
            gate = swap_pieces(leaving, gate)
            pieces.append(gate)
        stages.append([(output, head) for head in chosen for output in (0, 1)])
    key_grad, value_grad = unpack(stages, pieces, rows, heads, 2)
    with jax.named_scope("returns_last"):
        last = swap_pieces(close(open_grads, parts, rows), gate)
    (query_grad,) = unpack([[(0, head) for head in range(heads)]], [last], rows, heads, 1)
    result = (query_grad, key_grad, value_grad)
    with jax.named_scope("gain"):
        places = [(piece, base + dots) for piece in lead]
        if paired:
            places.append((own_side[0], base + dots))
            start = (parts - 1) * rows + dots
            places += [(lead_side[0], start + (part - 1) * (dots + extra)) for part in others]
        gain = gain_total(places, channels // LANES, 1.0 / (rows * span * parts * lax.axis_size("dp")))
    return tuple(grad[None] for grad in result) + (gain.reshape(channels),)


def solution(mesh):
    split = P("dp", ("tm", "ulysses"), None)
    return jax.shard_map(
        local,
        mesh=mesh,
        in_specs=(split,) * 5 + (P(),),
        out_specs=(split,) * 3 + (P(),),
        check_vma=False,
    )
```

```python
import functools
import math

import jax
import jax.numpy as jnp
from jax import lax
from jax.experimental import pallas as pl
from jax.experimental.pallas import tpu as pltpu
from jax.sharding import PartitionSpec as P

HD = 128
LANES = 128
TILE_ROWS = 16
KEY_BLOCK = 768
QUERY_BLOCK = 256
VMEM_LIMIT = 48 * 1024 * 1024
VMEM_WHOLE = 62 * 1024 * 1024
SCALE = 1.0 / math.sqrt(HD)
SCALE_LOG2 = SCALE / math.log(2.0)
COST = pl.CostEstimate(flops=1, bytes_accessed=1, transcendentals=0)


def params():
    return pltpu.CompilerParams(vmem_limit_bytes=VMEM_LIMIT)


def distances(parts):
    return [0] + list(range(parts - 1, 0, -1))


def column_of(parts, place, heads, head):
    partner = lax.axis_index("ulysses") ^ distances(parts)[place]
    return pl.multiple_of((partner * heads + head) * HD, HD)


def run_copies(pairs, semaphores):
    copies = [
        pltpu.make_async_copy(source, target, semaphores.at[index]) for index, (source, target) in enumerate(pairs)
    ]
    for copy in copies:
        copy.start()
    for copy in copies:
        copy.wait()


def pack_kernel(parts, chosen, *refs):
    sources, pieces, semaphores = refs[: -parts - 1], refs[-parts - 1 : -1], refs[-1]
    rows, channels = sources[0].shape
    heads = channels // (parts * HD)
    pairs = []
    for distance in range(parts):
        for half, ref in enumerate(sources):
            for place, head in enumerate(chosen):
                columns = pl.ds(column_of(parts, distance, heads, head), HD)
                start = (half * len(chosen) + place) * rows
                pairs.append((ref.at[:, columns], pieces[distance].at[start : start + rows]))
    run_copies(pairs, semaphores)


def pack(sources, parts, chosen, limit=VMEM_LIMIT):
    rows = sources[0].shape[0]
    depth = len(sources) * len(chosen) * rows
    whole = pl.BlockSpec(memory_space=pl.ANY)
    return pl.pallas_call(
        functools.partial(pack_kernel, parts, chosen),
        in_specs=[whole] * len(sources),
        out_specs=[pl.BlockSpec(memory_space=pltpu.VMEM)] * parts,
        out_shape=[jax.ShapeDtypeStruct((depth, HD), sources[0].dtype)] * parts,
        scratch_shapes=[pltpu.SemaphoreType.DMA((len(sources) * len(chosen) * parts,))],
        compiler_params=pltpu.CompilerParams(vmem_limit_bytes=limit),
        cost_estimate=COST,
    )(*sources)


def gather_kernel(ranges, *refs):
    arrays, out_ref, semaphores = refs[:-2], refs[-2], refs[-1]
    pairs = []
    place = 0
    for number, first, count in ranges:
        pairs.append((arrays[number].at[first : first + count], out_ref.at[place : place + count]))
        place += count
    run_copies(pairs, semaphores)


def gather_rows(arrays, ranges):
    whole = pl.BlockSpec(memory_space=pl.ANY)
    depth = sum(count for _, _, count in ranges)
    return pl.pallas_call(
        functools.partial(gather_kernel, ranges),
        in_specs=[whole] * len(arrays),
        out_specs=whole,
        out_shape=jax.ShapeDtypeStruct((depth, HD), arrays[0].dtype),
        scratch_shapes=[pltpu.SemaphoreType.DMA((len(ranges),))],
        compiler_params=params(),
        cost_estimate=COST,
    )(*arrays)


def dot_groups(rows):
    return -(-rows // LANES)


def dots_depth(rows, heads):
    return -(-2 * heads * dot_groups(rows) // TILE_ROWS) * TILE_ROWS


def gain_kernel(out_grad_ref, attn_ref, out_ref):
    product = out_grad_ref[...].astype(jnp.float32) * attn_ref[...].astype(jnp.float32)
    out_ref[...] = jnp.sum(product, axis=0, keepdims=True)


def gain_partial(out_grad, attn_out):
    return pl.pallas_call(
        gain_kernel,
        out_shape=jax.ShapeDtypeStruct((1, out_grad.shape[1]), jnp.float32),
        compiler_params=params(),
        cost_estimate=COST,
    )(out_grad, attn_out)


def split_terms(value, count):
    terms = []
    for _ in range(count):
        term = value.astype(jnp.bfloat16).astype(jnp.float32)
        terms.append(term)
        value = value - term
    return terms


def gain_depth(channels):
    return -(-3 * channels // LANES // TILE_ROWS) * TILE_ROWS


def pack_grads_kernel(parts, out_grad_ref, attn_ref, value_ref, gain_ref, partial_ref, *refs):
    rows, channels = out_grad_ref.shape
    heads = channels // (parts * HD)
    base = (heads + 1) * rows
    depth = base + dots_depth(rows, heads)
    partial = jnp.concatenate(split_terms(partial_ref[...], 3), axis=0)
    spare = gain_depth(channels) - partial.shape[0]
    if spare:
        partial = jnp.concatenate([partial, jnp.zeros((spare, LANES), jnp.float32)], axis=0)
    for distance in range(parts):
        terms = []
        for head in range(heads):
            columns = pl.ds(column_of(parts, distance, heads, head), HD)
            grad = (out_grad_ref[:, columns].astype(jnp.float32) * gain_ref[:, columns]).astype(jnp.bfloat16)
            place = head + 1 if head else 0
            refs[distance][place * rows : (place + 1) * rows] = grad
            if head == 0:
                refs[distance][rows : 2 * rows] = value_ref[:, columns]
            product = grad.astype(jnp.float32) * attn_ref[:, columns].astype(jnp.float32)
            dots = jnp.sum(jnp.transpose(product), axis=0, keepdims=True)
            for first in range(0, rows, LANES):
                value = dots[:, first : first + LANES]
                if value.shape[1] < LANES:
                    rest = jnp.zeros((1, LANES - value.shape[1]), jnp.float32)
                    value = jnp.concatenate([value, rest], axis=1)
                terms += split_terms(value, 2)
        rest = dots_depth(rows, heads) - len(terms)
        if rest:
            terms.append(jnp.zeros((rest, LANES), jnp.float32))
        refs[distance][base:depth] = jnp.concatenate(terms, axis=0).astype(jnp.bfloat16)
        refs[distance][depth:] = partial.astype(jnp.bfloat16)


def pack_grads(out_grad, attn_out, values, out_gain, partial, parts):
    rows, channels = out_grad.shape
    heads = channels // (parts * HD)
    depth = (heads + 1) * rows + dots_depth(rows, heads) + gain_depth(channels)
    return pl.pallas_call(
        functools.partial(pack_grads_kernel, parts),
        out_shape=[jax.ShapeDtypeStruct((depth, HD), jnp.bfloat16)] * parts,
        compiler_params=params(),
        cost_estimate=COST,
    )(out_grad, attn_out, values, out_gain.reshape(1, channels), partial)


def gain_total_kernel(lines, starts, scale, *refs):
    values = []
    for ref, start in zip(refs[:-1], starts):
        terms = [ref[start + index * lines : start + (index + 1) * lines].astype(jnp.float32) for index in range(3)]
        values.append(terms[0] + terms[1] + terms[2])
    refs[-1][...] = tree_sum(values) * scale


def gain_total(places, lines, scale):
    return pl.pallas_call(
        functools.partial(gain_total_kernel, lines, [start for _, start in places], scale),
        out_shape=jax.ShapeDtypeStruct((lines, LANES), jnp.float32),
        compiler_params=params(),
        cost_estimate=COST,
    )(*[array for array, _ in places])


def stacked(refs):
    return jnp.concatenate([ref[...] for ref in refs], axis=0)


def block_specs(depth, places):
    def block(index):
        return pl.BlockSpec((depth, HD), lambda step: (index, 0))

    return [block(index) for _, index in places], [array for array, _ in places]


def totals_kernel(parts, sources, heads, *refs):
    key_refs, refs = refs[: parts * heads], refs[parts * heads :]
    query_refs, refs = refs[: parts * heads * sources], refs[parts * heads * sources :]
    outs, score_ref = refs[:sources], refs[sources]
    slab = score_ref.shape[0]
    for head in range(heads):
        keys = stacked(key_refs[head * parts : (head + 1) * parts])
        for source in range(sources):
            start = (source * heads + head) * parts
            flip = jnp.transpose(stacked(query_refs[start : start + parts]))
            top = None
            for first in range(0, slab, KEY_BLOCK):
                scores = jnp.dot(keys[first : first + KEY_BLOCK], flip, preferred_element_type=jnp.float32)
                score_ref[first : first + KEY_BLOCK] = scores
                part_top = jnp.max(scores.reshape(-1, 8, slab), axis=0)
                top = part_top if top is None else jnp.maximum(top, part_top)
            top = jnp.max(top, axis=0, keepdims=True) * SCALE_LOG2
            total = None
            for first in range(0, slab, KEY_BLOCK):
                powers = jnp.exp2(score_ref[first : first + KEY_BLOCK] * SCALE_LOG2 - top)
                part_total = jnp.sum(powers.reshape(-1, 8, slab), axis=0)
                total = part_total if total is None else total + part_total
            total = jnp.sum(total, axis=0, keepdims=True)
            outs[source][head : head + 1] = top + jnp.log(total) * (1.0 / math.log(2.0))


def partial_totals(keys, queries, rows):
    heads, parts, sources = len(keys), len(keys[0]), len(queries)
    slab = parts * rows
    places = [place for head in keys for place in head]
    places += [place for source in queries for head in source for place in head]
    in_specs, operands = block_specs(rows, places)
    line = pl.BlockSpec((heads, slab), lambda step: (0, 0))
    return pl.pallas_call(
        functools.partial(totals_kernel, parts, sources, heads),
        grid=(1,),
        in_specs=in_specs,
        out_specs=[line] * sources,
        out_shape=[jax.ShapeDtypeStruct((heads, slab), jnp.float32)] * sources,
        scratch_shapes=[pltpu.VMEM((slab, slab), jnp.float32)],
        compiler_params=params(),
        cost_estimate=pl.CostEstimate(
            flops=2 * heads * sources * slab * slab * HD,
            bytes_accessed=heads * sources * slab * HD * 4,
            transcendentals=heads * sources * slab * slab,
        ),
    )(*operands)


def join_totals(values):
    top = functools.reduce(jnp.maximum, values)
    return top + jnp.log2(functools.reduce(jnp.add, [jnp.exp2(value - top) for value in values]))


def attention_kernel(parts, sources, chosen, rows, *refs):
    slab = parts * rows

    def take(count):
        nonlocal refs
        taken, refs = refs[:count], refs[count:]
        return taken

    dots_refs, total_refs = take(parts * sources), take(sources)
    inputs = [[take(parts), take(parts), take(parts * sources), take(parts * sources)] for _ in chosen]
    piece_refs, query_grad_refs = take(parts), take(sources)
    weight_ref, score_ref = refs
    for number, head in enumerate(chosen):
        keys, values, queries, grads = [stacked(held) for held in inputs[number]]
        query_flip, grad_flip = jnp.transpose(queries), jnp.transpose(grads)
        lines = []
        for ref in dots_refs:
            terms = ref[...].astype(jnp.float32)
            for index in range(dot_groups(rows)):
                line = 2 * (head * dot_groups(rows) + index)
                count = min(LANES, rows - index * LANES)
                lines.append((terms[line : line + 1] + terms[line + 1 : line + 2])[:, :count])
        dots = jnp.concatenate(lines, axis=1)
        totals = jnp.concatenate([ref[head : head + 1] for ref in total_refs], axis=1)
        base = 2 * number * rows
        for first in range(0, slab, KEY_BLOCK):
            stretch = slice(first, first + KEY_BLOCK)
            for start in range(0, sources * slab, QUERY_BLOCK):
                span = slice(start, start + QUERY_BLOCK)
                scores = jnp.dot(keys[stretch], query_flip[:, span], preferred_element_type=jnp.float32)
                weights = jnp.exp2(scores * SCALE_LOG2 - totals[:, span])
                grad_weights = jnp.dot(values[stretch], grad_flip[:, span], preferred_element_type=jnp.float32)
                weight_ref[stretch, span] = weights.astype(jnp.bfloat16)
                score_ref[stretch, span] = (weights * (grad_weights - dots[:, span])).astype(jnp.bfloat16)
            value_grad = jnp.dot(weight_ref[stretch], grads, preferred_element_type=jnp.float32)
            key_grad = jnp.dot(score_ref[stretch], queries, preferred_element_type=jnp.float32) * SCALE
            key_grad, value_grad = key_grad.astype(jnp.bfloat16), value_grad.astype(jnp.bfloat16)
            for part in range(parts):
                low, high = max(first, part * rows), min(first + KEY_BLOCK, (part + 1) * rows)
                if low < high:
                    place = base + low - part * rows
                    local_rows = slice(low - first, high - first)
                    piece_refs[part][place : place + high - low] = key_grad[local_rows]
                    piece_refs[part][place + rows : place + rows + high - low] = value_grad[local_rows]
        for source, ref in enumerate(query_grad_refs):
            query_grad = lax.dot_general(
                score_ref[:, source * slab : (source + 1) * slab],
                keys,
                (((0,), (0,)), ((), ())),
                preferred_element_type=jnp.float32,
            )
            ref[number * slab : (number + 1) * slab] = (query_grad * SCALE).astype(ref.dtype)


def attention(chosen, heads, rows, inputs, dots, totals):
    parts = len(inputs[0][0])
    sources = len(totals)
    slab = parts * rows
    dot_specs, dot_arrays = block_specs(dots_depth(rows, heads), dots)
    in_specs, operands = block_specs(rows, [place for held in inputs for places in held for place in places])
    line = pl.BlockSpec((heads, slab), lambda step: (0, 0))
    depth = 2 * len(chosen) * rows
    out_specs, _ = block_specs(depth, [(None, 0)] * parts)
    query_specs, _ = block_specs(len(chosen) * slab, [(None, 0)] * sources)
    outs = pl.pallas_call(
        functools.partial(attention_kernel, parts, sources, chosen, rows),
        grid=(1,),
        in_specs=dot_specs + [line] * sources + in_specs,
        out_specs=out_specs + query_specs,
        out_shape=[jax.ShapeDtypeStruct((depth, HD), jnp.bfloat16)] * parts
        + [jax.ShapeDtypeStruct((len(chosen) * slab, HD), jnp.float32)]
        + [jax.ShapeDtypeStruct((len(chosen) * slab, HD), jnp.bfloat16)] * (sources - 1),
        scratch_shapes=[pltpu.VMEM((slab, sources * slab), jnp.bfloat16)] * 2,
        compiler_params=params(),
        cost_estimate=pl.CostEstimate(
            flops=10 * len(chosen) * slab * sources * slab * HD,
            bytes_accessed=32 * len(chosen) * slab * HD,
            transcendentals=len(chosen) * slab * sources * slab,
        ),
    )(*dot_arrays, *totals, *operands)
    return outs[:parts], outs[parts:]


def close_kernel(parts, rows, sources, *refs):
    terms, pieces = refs[:-parts], refs[-parts:]
    place = 0
    for first in range(0, len(terms), sources):
        for start in range(0, terms[first].shape[0], parts * rows):
            for part in range(parts):
                span = slice(start + part * rows, start + (part + 1) * rows)
                total = terms[first][span]
                for ref in terms[first + 1 : first + sources]:
                    total = total + ref[span].astype(jnp.float32)
                pieces[part][place : place + rows] = total.astype(jnp.bfloat16)
            place += rows


def close(query_grads, parts, rows):
    depth = sum(terms[0].shape[0] for terms in query_grads) // parts
    return pl.pallas_call(
        functools.partial(close_kernel, parts, rows, len(query_grads[0])),
        out_shape=[jax.ShapeDtypeStruct((depth, HD), jnp.bfloat16)] * parts,
        compiler_params=params(),
        cost_estimate=COST,
    )(*[term for terms in query_grads for term in terms])


def unpack_kernel(parts, rows, heads, stages, *refs):
    count = parts * len(stages)
    pieces, outs, semaphores = refs[:count], refs[count:-1], refs[-1]
    pairs = []
    for number, blocks in enumerate(stages):
        for distance in range(parts):
            piece = pieces[number * parts + distance]
            for index, (output, head) in enumerate(blocks):
                columns = pl.ds(column_of(parts, distance, heads, head), HD)
                pairs.append((piece.at[index * rows : (index + 1) * rows], outs[output].at[:, columns]))
    run_copies(pairs, semaphores)


def unpack(stages, pieces, rows, heads, outputs):
    parts = len(pieces[0])
    whole = pl.BlockSpec(memory_space=pl.ANY)
    channels = parts * heads * HD
    return pl.pallas_call(
        functools.partial(unpack_kernel, parts, rows, heads, stages),
        in_specs=[whole] * (parts * len(stages)),
        out_specs=[whole] * outputs,
        out_shape=[jax.ShapeDtypeStruct((rows, channels), jnp.bfloat16)] * outputs,
        scratch_shapes=[pltpu.SemaphoreType.DMA((outputs * heads * parts,))],
        compiler_params=params(),
        cost_estimate=COST,
    )(*[piece for stage in pieces for piece in stage])


def swap(value, axis, distance):
    return lax.ppermute(value, axis, [(index, index ^ distance) for index in range(lax.axis_size(axis))])


def swap_pieces(pieces, earlier=None):
    held = [pieces[0]]
    for place, distance in enumerate(distances(len(pieces))):
        if distance:
            piece = pieces[place] if earlier is None else after([pieces[place]], earlier[place])[0]
            held.append(swap(piece, "ulysses", distance))
    return held


def tree_sum(values):
    while len(values) > 1:
        values = [functools.reduce(jnp.add, values[index : index + 2]) for index in range(0, len(values), 2)]
    return values[0]


def sum_over(value, axis):
    size = lax.axis_size(axis)
    if size & (size - 1):
        return lax.psum(value, axis)
    return tree_sum([value] + [swap(value, axis, distance) for distance in range(1, size)])


def after(values, *earlier):
    return lax.optimization_barrier((list(values), earlier))[0]


def neighbours(size):
    if size == 1:
        return []
    if size == 2:
        swapped = [(0, 1), (1, 0)]
        return [(swapped, swapped)]
    up = [(index, index + 1) for index in range(size - 1)]
    down = [(index + 1, index) for index in range(size - 1)]
    return [(up, down), (down, up)]


def exchange_totals(partial, sides):
    if not sides:
        return partial
    if len(sides) == 1:
        other = lax.ppermute(jnp.concatenate(partial), "tm", sides[0][0])
        heads = partial[0].shape[0]
        return [join_totals([partial[0], other[heads:]]), join_totals([partial[1], other[:heads]])]
    position = lax.axis_index("tm")
    present = [position < lax.axis_size("tm") - 1, position > 0]
    values = [partial[0]]
    for value, (_, back), flag in zip(partial[1:], sides, present):
        values.append(jnp.where(flag, lax.ppermute(value, "tm", back), -jnp.inf))
    own = join_totals(values)
    return [own] + [lax.ppermute(own, "tm", there) for there, _ in sides]


def local(queries, keys, values, attn_out, out_grad, out_gain):
    parts = lax.axis_size("ulysses")
    span = lax.axis_size("tm")
    rows, channels = queries.shape[1:]
    heads = channels // (parts * HD)
    rest = list(range(1, heads))
    dots = dots_depth(rows, heads)
    every = list(range(parts))
    sides = neighbours(span)

    def forward(array):
        return [lax.ppermute(array, "tm", there) for there, _ in sides]

    with jax.named_scope("keys_queries"):
        packed = pack([keys[0], queries[0]], parts, list(range(heads)), VMEM_WHOLE)
        pairs = [packed[0]] + after(swap_pieces(packed)[:0:-1], [])[::-1]
    paired = span == 2
    with jax.named_scope("gain"):
        out_grad = after([out_grad], packed[0])[0]
        gain = gain_partial(out_grad[0], attn_out[0]).reshape(-1, LANES)
        gain = sum_over(gain, "dp")
        if not paired:
            gain = sum_over(gain, "tm")
    with jax.named_scope("grads"):
        sent_lead = pack_grads(out_grad[0], attn_out[0], values[0], out_gain, gain, parts)
    with jax.named_scope("halo_own_grads"):
        own_side = forward(sent_lead[0])
    with jax.named_scope("halo_queries"):
        width = heads * rows
        first_side = forward(pairs[0][width:])
    with jax.named_scope("grads"):
        lead = swap_pieces(sent_lead, pairs)
    with jax.named_scope("halo_queries"):
        late = after(pairs[1:], first_side, sent_lead[0])
        late_side = forward(gather_rows(late, [(number, width, width) for number in range(parts - 1)]))
    base = (heads + 1) * rows
    extra = gain_depth(channels)
    with jax.named_scope("totals"):
        key_places = [[(piece, head) for piece in pairs] for head in range(heads)]
        query_places = [[[(piece, heads + head) for piece in pairs] for head in range(heads)]]
        for first, others in zip(first_side, late_side):
            query_places.append(
                [
                    [(first, head)] + [(others, (part - 1) * heads + head) for part in every[1:]]
                    for head in range(heads)
                ]
            )
        part_totals = partial_totals(key_places, query_places, rows)
        totals = exchange_totals(after(part_totals, lead[1:]), sides)
    others = range(1, parts)
    with jax.named_scope("halo_first_grads"):
        ranges = [(part, 0, rows) for part in others] + [(part, base, dots + extra) for part in others]
        lead_side = forward(gather_rows(after(lead, part_totals, own_side), ranges))
    with jax.named_scope("rest_values"):
        rest_values = swap_pieces(after(pack([values[0]], parts, rest), part_totals), lead)
    dot_places = [(piece, base // dots) for piece in lead]
    for own, array in zip(own_side, lead_side):
        dot_places.append((own, base // dots))
        step = (dots + extra) // dots
        dot_places += [(array, (parts - 1) * rows // dots + (part - 1) * step) for part in others]

    def inputs_of(head):
        queries_of = [place for source in query_places for place in source[head]]
        if head == 0:
            values_of = [(piece, 1) for piece in lead]
            grads_of = [(piece, 0) for piece in lead]
            for own, array in zip(own_side, lead_side):
                grads_of += [(own, 0)] + [(array, part - 1) for part in others]
        else:
            values_of = [(piece, head - 1) for piece in rest_values]
            grads_of = [(piece, head + 1) for piece in lead]
            for own, array in zip(own_side, rest_side):
                start = (head - 1) * (parts - 1)
                grads_of += [(own, head + 1)] + [(array, start + part - 1) for part in others]
        return [key_places[head], values_of, queries_of, grads_of]

    stages, pieces, open_grads = [], [], []
    gate = rest_values
    for number, chosen in enumerate([[0], rest]):
        if number:
            with jax.named_scope("halo_rest_grads"):
                ranges = [(part, (head + 1) * rows, rows) for head in rest for part in others]
                rest_side = forward(gather_rows(after(lead, lead_side), ranges))
        with jax.named_scope("attention_%d" % number):
            inputs = [inputs_of(head) for head in chosen]
            leaving, query_grads = attention(chosen, heads, rows, inputs, dot_places, totals)
            totals = after(totals, leaving[0])
        if number:
            query_grads = after(query_grads, gate[1:], open_grads[0][1:])
        with jax.named_scope("halo_query_grads_%d" % number):
            sent_back = [lax.ppermute(other, "tm", back) for other, (_, back) in zip(query_grads[1:], sides)]
            open_grads.append(list(query_grads[:1]) + sent_back)
        with jax.named_scope("returns_%d" % number):
            gate = swap_pieces(leaving, gate)
            pieces.append(gate)
        stages.append([(output, head) for head in chosen for output in (0, 1)])
    key_grad, value_grad = unpack(stages, pieces, rows, heads, 2)
    with jax.named_scope("returns_last"):
        last = swap_pieces(close(open_grads, parts, rows), gate)
    (query_grad,) = unpack([[(0, head) for head in range(heads)]], [last], rows, heads, 1)
    result = (query_grad, key_grad, value_grad)
    with jax.named_scope("gain"):
        places = [(piece, base + dots) for piece in lead]
        if paired:
            places.append((own_side[0], base + dots))
            start = (parts - 1) * rows + dots
            places += [(lead_side[0], start + (part - 1) * (dots + extra)) for part in others]
        gain = gain_total(places, channels // LANES, 1.0 / (rows * span * parts * lax.axis_size("dp")))
    return tuple(grad[None] for grad in result) + (gain.reshape(channels),)


def solution(mesh):
    split = P("dp", ("tm", "ulysses"), None)
    return jax.shard_map(
        local,
        mesh=mesh,
        in_specs=(split,) * 5 + (P(),),
        out_specs=(split,) * 3 + (P(),),
        check_vma=False,
    )
```

```python
import functools
import math

import jax
import jax.numpy as jnp
from jax import lax
from jax.experimental import pallas as pl
from jax.experimental.pallas import tpu as pltpu
from jax.sharding import PartitionSpec as P

HD = 128
LANES = 128
TILE_ROWS = 16
KEY_BLOCK = 768
QUERY_BLOCK = 256
VMEM_LIMIT = 48 * 1024 * 1024
VMEM_WHOLE = 62 * 1024 * 1024
SCALE = 1.0 / math.sqrt(HD)
SCALE_LOG2 = SCALE / math.log(2.0)
COST = pl.CostEstimate(flops=1, bytes_accessed=1, transcendentals=0)


def params():
    return pltpu.CompilerParams(vmem_limit_bytes=VMEM_LIMIT)


def distances(parts):
    return [0] + list(range(parts - 1, 0, -1))


def column_of(parts, place, heads, head):
    partner = lax.axis_index("ulysses") ^ distances(parts)[place]
    return pl.multiple_of((partner * heads + head) * HD, HD)


def run_copies(pairs, semaphores):
    copies = [
        pltpu.make_async_copy(source, target, semaphores.at[index]) for index, (source, target) in enumerate(pairs)
    ]
    for copy in copies:
        copy.start()
    for copy in copies:
        copy.wait()


def pack_kernel(parts, chosen, *refs):
    sources, pieces, semaphores = refs[: -parts - 1], refs[-parts - 1 : -1], refs[-1]
    rows, channels = sources[0].shape
    heads = channels // (parts * HD)
    pairs = []
    for distance in range(parts):
        for half, ref in enumerate(sources):
            for place, head in enumerate(chosen):
                columns = pl.ds(column_of(parts, distance, heads, head), HD)
                start = (half * len(chosen) + place) * rows
                pairs.append((ref.at[:, columns], pieces[distance].at[start : start + rows]))
    run_copies(pairs, semaphores)


def pack(sources, parts, chosen, limit=VMEM_LIMIT):
    rows = sources[0].shape[0]
    depth = len(sources) * len(chosen) * rows
    whole = pl.BlockSpec(memory_space=pl.ANY)
    return pl.pallas_call(
        functools.partial(pack_kernel, parts, chosen),
        in_specs=[whole] * len(sources),
        out_specs=[pl.BlockSpec(memory_space=pltpu.VMEM)] * parts,
        out_shape=[jax.ShapeDtypeStruct((depth, HD), sources[0].dtype)] * parts,
        scratch_shapes=[pltpu.SemaphoreType.DMA((len(sources) * len(chosen) * parts,))],
        compiler_params=pltpu.CompilerParams(vmem_limit_bytes=limit),
        cost_estimate=COST,
    )(*sources)


def gather_kernel(ranges, *refs):
    arrays, out_ref, semaphores = refs[:-2], refs[-2], refs[-1]
    pairs = []
    place = 0
    for number, first, count in ranges:
        pairs.append((arrays[number].at[first : first + count], out_ref.at[place : place + count]))
        place += count
    run_copies(pairs, semaphores)


def gather_rows(arrays, ranges):
    whole = pl.BlockSpec(memory_space=pl.ANY)
    depth = sum(count for _, _, count in ranges)
    return pl.pallas_call(
        functools.partial(gather_kernel, ranges),
        in_specs=[whole] * len(arrays),
        out_specs=whole,
        out_shape=jax.ShapeDtypeStruct((depth, HD), arrays[0].dtype),
        scratch_shapes=[pltpu.SemaphoreType.DMA((len(ranges),))],
        compiler_params=params(),
        cost_estimate=COST,
    )(*arrays)


def dot_groups(rows):
    return -(-rows // LANES)


def dots_depth(rows, heads):
    return -(-2 * heads * dot_groups(rows) // TILE_ROWS) * TILE_ROWS


def gain_kernel(out_grad_ref, attn_ref, out_ref):
    product = out_grad_ref[...].astype(jnp.float32) * attn_ref[...].astype(jnp.float32)
    out_ref[...] = jnp.sum(product, axis=0, keepdims=True)


def gain_partial(out_grad, attn_out):
    return pl.pallas_call(
        gain_kernel,
        out_shape=jax.ShapeDtypeStruct((1, out_grad.shape[1]), jnp.float32),
        compiler_params=params(),
        cost_estimate=COST,
    )(out_grad, attn_out)


def split_terms(value, count):
    terms = []
    for _ in range(count):
        term = value.astype(jnp.bfloat16).astype(jnp.float32)
        terms.append(term)
        value = value - term
    return terms


def gain_depth(channels):
    return -(-3 * channels // LANES // TILE_ROWS) * TILE_ROWS


def pack_grads_kernel(parts, out_grad_ref, attn_ref, value_ref, gain_ref, partial_ref, *refs):
    rows, channels = out_grad_ref.shape
    heads = channels // (parts * HD)
    base = (heads + 1) * rows
    depth = base + dots_depth(rows, heads)
    partial = jnp.concatenate(split_terms(partial_ref[...], 3), axis=0)
    spare = gain_depth(channels) - partial.shape[0]
    if spare:
        partial = jnp.concatenate([partial, jnp.zeros((spare, LANES), jnp.float32)], axis=0)
    for distance in range(parts):
        terms = []
        for head in range(heads):
            columns = pl.ds(column_of(parts, distance, heads, head), HD)
            grad = (out_grad_ref[:, columns].astype(jnp.float32) * gain_ref[:, columns]).astype(jnp.bfloat16)
            place = head + 1 if head else 0
            refs[distance][place * rows : (place + 1) * rows] = grad
            if head == 0:
                refs[distance][rows : 2 * rows] = value_ref[:, columns]
            product = grad.astype(jnp.float32) * attn_ref[:, columns].astype(jnp.float32)
            dots = jnp.sum(jnp.transpose(product), axis=0, keepdims=True)
            for first in range(0, rows, LANES):
                value = dots[:, first : first + LANES]
                if value.shape[1] < LANES:
                    rest = jnp.zeros((1, LANES - value.shape[1]), jnp.float32)
                    value = jnp.concatenate([value, rest], axis=1)
                terms += split_terms(value, 2)
        rest = dots_depth(rows, heads) - len(terms)
        if rest:
            terms.append(jnp.zeros((rest, LANES), jnp.float32))
        refs[distance][base:depth] = jnp.concatenate(terms, axis=0).astype(jnp.bfloat16)
        refs[distance][depth:] = partial.astype(jnp.bfloat16)


def pack_grads(out_grad, attn_out, values, out_gain, partial, parts):
    rows, channels = out_grad.shape
    heads = channels // (parts * HD)
    depth = (heads + 1) * rows + dots_depth(rows, heads) + gain_depth(channels)
    return pl.pallas_call(
        functools.partial(pack_grads_kernel, parts),
        out_shape=[jax.ShapeDtypeStruct((depth, HD), jnp.bfloat16)] * parts,
        compiler_params=params(),
        cost_estimate=COST,
    )(out_grad, attn_out, values, out_gain.reshape(1, channels), partial)


def gain_total_kernel(lines, starts, scale, *refs):
    values = []
    for ref, start in zip(refs[:-1], starts):
        terms = [ref[start + index * lines : start + (index + 1) * lines].astype(jnp.float32) for index in range(3)]
        values.append(terms[0] + terms[1] + terms[2])
    refs[-1][...] = tree_sum(values) * scale


def gain_total(places, lines, scale):
    return pl.pallas_call(
        functools.partial(gain_total_kernel, lines, [start for _, start in places], scale),
        out_shape=jax.ShapeDtypeStruct((lines, LANES), jnp.float32),
        compiler_params=params(),
        cost_estimate=COST,
    )(*[array for array, _ in places])


def stacked(refs):
    return jnp.concatenate([ref[...] for ref in refs], axis=0)


def block_specs(depth, places):
    def block(index):
        return pl.BlockSpec((depth, HD), lambda step: (index, 0))

    return [block(index) for _, index in places], [array for array, _ in places]


def totals_kernel(parts, sources, heads, *refs):
    key_refs, refs = refs[: parts * heads], refs[parts * heads :]
    query_refs, refs = refs[: parts * heads * sources], refs[parts * heads * sources :]
    outs, score_ref = refs[:sources], refs[sources]
    slab = score_ref.shape[0]
    for head in range(heads):
        keys = stacked(key_refs[head * parts : (head + 1) * parts])
        for source in range(sources):
            start = (source * heads + head) * parts
            flip = jnp.transpose(stacked(query_refs[start : start + parts]))
            top = None
            for first in range(0, slab, KEY_BLOCK):
                scores = jnp.dot(keys[first : first + KEY_BLOCK], flip, preferred_element_type=jnp.float32)
                score_ref[first : first + KEY_BLOCK] = scores
                part_top = jnp.max(scores.reshape(-1, 8, slab), axis=0)
                top = part_top if top is None else jnp.maximum(top, part_top)
            top = jnp.max(top, axis=0, keepdims=True) * SCALE_LOG2
            total = None
            for first in range(0, slab, KEY_BLOCK):
                powers = jnp.exp2(score_ref[first : first + KEY_BLOCK] * SCALE_LOG2 - top)
                part_total = jnp.sum(powers.reshape(-1, 8, slab), axis=0)
                total = part_total if total is None else total + part_total
            total = jnp.sum(total, axis=0, keepdims=True)
            outs[source][head : head + 1] = top + jnp.log(total) * (1.0 / math.log(2.0))


def partial_totals(keys, queries, rows):
    heads, parts, sources = len(keys), len(keys[0]), len(queries)
    slab = parts * rows
    places = [place for head in keys for place in head]
    places += [place for source in queries for head in source for place in head]
    in_specs, operands = block_specs(rows, places)
    line = pl.BlockSpec((heads, slab), lambda step: (0, 0))
    return pl.pallas_call(
        functools.partial(totals_kernel, parts, sources, heads),
        grid=(1,),
        in_specs=in_specs,
        out_specs=[line] * sources,
        out_shape=[jax.ShapeDtypeStruct((heads, slab), jnp.float32)] * sources,
        scratch_shapes=[pltpu.VMEM((slab, slab), jnp.float32)],
        compiler_params=params(),
        cost_estimate=pl.CostEstimate(
            flops=2 * heads * sources * slab * slab * HD,
            bytes_accessed=heads * sources * slab * HD * 4,
            transcendentals=heads * sources * slab * slab,
        ),
    )(*operands)


def join_totals(values):
    top = functools.reduce(jnp.maximum, values)
    return top + jnp.log2(functools.reduce(jnp.add, [jnp.exp2(value - top) for value in values]))


def attention_kernel(parts, sources, chosen, rows, *refs):
    slab = parts * rows

    def take(count):
        nonlocal refs
        taken, refs = refs[:count], refs[count:]
        return taken

    dots_refs, total_refs = take(parts * sources), take(sources)
    inputs = [[take(parts), take(parts), take(parts * sources), take(parts * sources)] for _ in chosen]
    piece_refs, query_grad_refs = take(parts), take(sources)
    weight_ref, score_ref = refs
    for number, head in enumerate(chosen):
        keys, values, queries, grads = [stacked(held) for held in inputs[number]]
        query_flip, grad_flip = jnp.transpose(queries), jnp.transpose(grads)
        lines = []
        for ref in dots_refs:
            terms = ref[...].astype(jnp.float32)
            for index in range(dot_groups(rows)):
                line = 2 * (head * dot_groups(rows) + index)
                count = min(LANES, rows - index * LANES)
                lines.append((terms[line : line + 1] + terms[line + 1 : line + 2])[:, :count])
        dots = jnp.concatenate(lines, axis=1)
        totals = jnp.concatenate([ref[head : head + 1] for ref in total_refs], axis=1)
        base = 2 * number * rows
        for first in range(0, slab, KEY_BLOCK):
            stretch = slice(first, first + KEY_BLOCK)
            for start in range(0, sources * slab, QUERY_BLOCK):
                span = slice(start, start + QUERY_BLOCK)
                scores = jnp.dot(keys[stretch], query_flip[:, span], preferred_element_type=jnp.float32)
                weights = jnp.exp2(scores * SCALE_LOG2 - totals[:, span])
                grad_weights = jnp.dot(values[stretch], grad_flip[:, span], preferred_element_type=jnp.float32)
                weight_ref[stretch, span] = weights.astype(jnp.bfloat16)
                score_ref[stretch, span] = (weights * (grad_weights - dots[:, span])).astype(jnp.bfloat16)
            value_grad = jnp.dot(weight_ref[stretch], grads, preferred_element_type=jnp.float32)
            key_grad = jnp.dot(score_ref[stretch], queries, preferred_element_type=jnp.float32) * SCALE
            key_grad, value_grad = key_grad.astype(jnp.bfloat16), value_grad.astype(jnp.bfloat16)
            for part in range(parts):
                low, high = max(first, part * rows), min(first + KEY_BLOCK, (part + 1) * rows)
                if low < high:
                    place = base + low - part * rows
                    local_rows = slice(low - first, high - first)
                    piece_refs[part][place : place + high - low] = key_grad[local_rows]
                    piece_refs[part][place + rows : place + rows + high - low] = value_grad[local_rows]
        for source, ref in enumerate(query_grad_refs):
            query_grad = lax.dot_general(
                score_ref[:, source * slab : (source + 1) * slab],
                keys,
                (((0,), (0,)), ((), ())),
                preferred_element_type=jnp.float32,
            )
            ref[number * slab : (number + 1) * slab] = (query_grad * SCALE).astype(ref.dtype)


def attention(chosen, heads, rows, inputs, dots, totals):
    parts = len(inputs[0][0])
    sources = len(totals)
    slab = parts * rows
    dot_specs, dot_arrays = block_specs(dots_depth(rows, heads), dots)
    in_specs, operands = block_specs(rows, [place for held in inputs for places in held for place in places])
    line = pl.BlockSpec((heads, slab), lambda step: (0, 0))
    depth = 2 * len(chosen) * rows
    out_specs, _ = block_specs(depth, [(None, 0)] * parts)
    query_specs, _ = block_specs(len(chosen) * slab, [(None, 0)] * sources)
    outs = pl.pallas_call(
        functools.partial(attention_kernel, parts, sources, chosen, rows),
        grid=(1,),
        in_specs=dot_specs + [line] * sources + in_specs,
        out_specs=out_specs + query_specs,
        out_shape=[jax.ShapeDtypeStruct((depth, HD), jnp.bfloat16)] * parts
        + [jax.ShapeDtypeStruct((len(chosen) * slab, HD), jnp.float32)]
        + [jax.ShapeDtypeStruct((len(chosen) * slab, HD), jnp.bfloat16)] * (sources - 1),
        scratch_shapes=[pltpu.VMEM((slab, sources * slab), jnp.bfloat16)] * 2,
        compiler_params=params(),
        cost_estimate=pl.CostEstimate(
            flops=10 * len(chosen) * slab * sources * slab * HD,
            bytes_accessed=32 * len(chosen) * slab * HD,
            transcendentals=len(chosen) * slab * sources * slab,
        ),
    )(*dot_arrays, *totals, *operands)
    return outs[:parts], outs[parts:]


def close_kernel(parts, rows, sources, *refs):
    terms, pieces = refs[:-parts], refs[-parts:]
    place = 0
    for first in range(0, len(terms), sources):
        for start in range(0, terms[first].shape[0], parts * rows):
            for part in range(parts):
                span = slice(start + part * rows, start + (part + 1) * rows)
                total = terms[first][span]
                for ref in terms[first + 1 : first + sources]:
                    total = total + ref[span].astype(jnp.float32)
                pieces[part][place : place + rows] = total.astype(jnp.bfloat16)
            place += rows


def close(query_grads, parts, rows):
    depth = sum(terms[0].shape[0] for terms in query_grads) // parts
    return pl.pallas_call(
        functools.partial(close_kernel, parts, rows, len(query_grads[0])),
        out_shape=[jax.ShapeDtypeStruct((depth, HD), jnp.bfloat16)] * parts,
        compiler_params=params(),
        cost_estimate=COST,
    )(*[term for terms in query_grads for term in terms])


def unpack_kernel(parts, rows, heads, stages, *refs):
    count = parts * len(stages)
    pieces, outs, semaphores = refs[:count], refs[count:-1], refs[-1]
    pairs = []
    for number, blocks in enumerate(stages):
        for distance in range(parts):
            piece = pieces[number * parts + distance]
            for index, (output, head) in enumerate(blocks):
                columns = pl.ds(column_of(parts, distance, heads, head), HD)
                pairs.append((piece.at[index * rows : (index + 1) * rows], outs[output].at[:, columns]))
    run_copies(pairs, semaphores)


def unpack(stages, pieces, rows, heads, outputs):
    parts = len(pieces[0])
    whole = pl.BlockSpec(memory_space=pl.ANY)
    channels = parts * heads * HD
    return pl.pallas_call(
        functools.partial(unpack_kernel, parts, rows, heads, stages),
        in_specs=[whole] * (parts * len(stages)),
        out_specs=[whole] * outputs,
        out_shape=[jax.ShapeDtypeStruct((rows, channels), jnp.bfloat16)] * outputs,
        scratch_shapes=[pltpu.SemaphoreType.DMA((outputs * heads * parts,))],
        compiler_params=params(),
        cost_estimate=COST,
    )(*[piece for stage in pieces for piece in stage])


def swap(value, axis, distance):
    return lax.ppermute(value, axis, [(index, index ^ distance) for index in range(lax.axis_size(axis))])


def swap_pieces(pieces, earlier=None):
    held = [pieces[0]]
    for place, distance in enumerate(distances(len(pieces))):
        if distance:
            piece = pieces[place] if earlier is None else after([pieces[place]], earlier[place])[0]
            held.append(swap(piece, "ulysses", distance))
    return held


def tree_sum(values):
    while len(values) > 1:
        values = [functools.reduce(jnp.add, values[index : index + 2]) for index in range(0, len(values), 2)]
    return values[0]


def sum_over(value, axis):
    size = lax.axis_size(axis)
    if size & (size - 1):
        return lax.psum(value, axis)
    return tree_sum([value] + [swap(value, axis, distance) for distance in range(1, size)])


def after(values, *earlier):
    return lax.optimization_barrier((list(values), earlier))[0]


def neighbours(size):
    if size == 1:
        return []
    if size == 2:
        swapped = [(0, 1), (1, 0)]
        return [(swapped, swapped)]
    up = [(index, index + 1) for index in range(size - 1)]
    down = [(index + 1, index) for index in range(size - 1)]
    return [(up, down), (down, up)]


def exchange_totals(partial, sides):
    if not sides:
        return partial
    if len(sides) == 1:
        other = lax.ppermute(jnp.concatenate(partial), "tm", sides[0][0])
        heads = partial[0].shape[0]
        return [join_totals([partial[0], other[heads:]]), join_totals([partial[1], other[:heads]])]
    position = lax.axis_index("tm")
    present = [position < lax.axis_size("tm") - 1, position > 0]
    values = [partial[0]]
    for value, (_, back), flag in zip(partial[1:], sides, present):
        values.append(jnp.where(flag, lax.ppermute(value, "tm", back), -jnp.inf))
    own = join_totals(values)
    return [own] + [lax.ppermute(own, "tm", there) for there, _ in sides]


def local(queries, keys, values, attn_out, out_grad, out_gain):
    parts = lax.axis_size("ulysses")
    span = lax.axis_size("tm")
    rows, channels = queries.shape[1:]
    heads = channels // (parts * HD)
    rest = list(range(1, heads))
    dots = dots_depth(rows, heads)
    every = list(range(parts))
    sides = neighbours(span)

    def forward(array):
        return [lax.ppermute(array, "tm", there) for there, _ in sides]

    with jax.named_scope("keys_queries"):
        packed = pack([keys[0], queries[0]], parts, list(range(heads)), VMEM_WHOLE)
        pairs = [packed[0]] + after(swap_pieces(packed)[:0:-1], [])[::-1]
    paired = span == 2
    with jax.named_scope("gain"):
        out_grad = after([out_grad], packed[0])[0]
        gain = gain_partial(out_grad[0], attn_out[0]).reshape(-1, LANES)
        gain = sum_over(gain, "dp")
        if not paired:
            gain = sum_over(gain, "tm")
    with jax.named_scope("grads"):
        sent_lead = pack_grads(out_grad[0], attn_out[0], values[0], out_gain, gain, parts)
    with jax.named_scope("halo_own_grads"):
        own_side = forward(sent_lead[0])
    with jax.named_scope("halo_queries"):
        width = heads * rows
        first_side = forward(pairs[0][width:])
    with jax.named_scope("grads"):
        lead = swap_pieces(sent_lead, pairs)
    with jax.named_scope("halo_queries"):
        late = after(pairs[1:], first_side, sent_lead[0])
        late_side = forward(gather_rows(late, [(number, width, width) for number in range(parts - 1)]))
    base = (heads + 1) * rows
    extra = gain_depth(channels)
    with jax.named_scope("totals"):
        key_places = [[(piece, head) for piece in pairs] for head in range(heads)]
        query_places = [[[(piece, heads + head) for piece in pairs] for head in range(heads)]]
        for first, others in zip(first_side, late_side):
            query_places.append(
                [
                    [(first, head)] + [(others, (part - 1) * heads + head) for part in every[1:]]
                    for head in range(heads)
                ]
            )
        part_totals = partial_totals(key_places, query_places, rows)
        totals = exchange_totals(after(part_totals, lead[1:]), sides)
    others = range(1, parts)
    with jax.named_scope("halo_first_grads"):
        ranges = [(part, 0, rows) for part in others] + [(part, base, dots + extra) for part in others]
        lead_side = forward(gather_rows(after(lead, part_totals, own_side), ranges))
    with jax.named_scope("rest_values"):
        rest_values = swap_pieces(after(pack([values[0]], parts, rest), part_totals), lead)
    dot_places = [(piece, base // dots) for piece in lead]
    for own, array in zip(own_side, lead_side):
        dot_places.append((own, base // dots))
        step = (dots + extra) // dots
        dot_places += [(array, (parts - 1) * rows // dots + (part - 1) * step) for part in others]

    def inputs_of(head):
        queries_of = [place for source in query_places for place in source[head]]
        if head == 0:
            values_of = [(piece, 1) for piece in lead]
            grads_of = [(piece, 0) for piece in lead]
            for own, array in zip(own_side, lead_side):
                grads_of += [(own, 0)] + [(array, part - 1) for part in others]
        else:
            values_of = [(piece, head - 1) for piece in rest_values]
            grads_of = [(piece, head + 1) for piece in lead]
            for own, array in zip(own_side, rest_side):
                start = (head - 1) * (parts - 1)
                grads_of += [(own, head + 1)] + [(array, start + part - 1) for part in others]
        return [key_places[head], values_of, queries_of, grads_of]

    stages, pieces, open_grads = [], [], []
    gate = rest_values
    for number, chosen in enumerate([[0], rest]):
        if number:
            with jax.named_scope("halo_rest_grads"):
                ranges = [(part, (head + 1) * rows, rows) for head in rest for part in others]
                rest_side = forward(gather_rows(after(lead, lead_side), ranges))
        with jax.named_scope("attention_%d" % number):
            inputs = [inputs_of(head) for head in chosen]
            leaving, query_grads = attention(chosen, heads, rows, inputs, dot_places, totals)
            totals = after(totals, leaving[0])
        if number:
            query_grads = after(query_grads, gate[1:], open_grads[0][1:])
        with jax.named_scope("halo_query_grads_%d" % number):
            sent_back = [lax.ppermute(other, "tm", back) for other, (_, back) in zip(query_grads[1:], sides)]
            open_grads.append(list(query_grads[:1]) + sent_back)
        with jax.named_scope("returns_%d" % number):
            gate = swap_pieces(leaving, gate)
            pieces.append(gate)
        stages.append([(output, head) for head in chosen for output in (0, 1)])
    key_grad, value_grad = unpack(stages, pieces, rows, heads, 2)
    with jax.named_scope("returns_last"):
        last = swap_pieces(close(open_grads, parts, rows), gate[:2] + gate[:1:-1])
    (query_grad,) = unpack([[(0, head) for head in range(heads)]], [last], rows, heads, 1)
    result = (query_grad, key_grad, value_grad)
    with jax.named_scope("gain"):
        places = [(piece, base + dots) for piece in lead]
        if paired:
            places.append((own_side[0], base + dots))
            start = (parts - 1) * rows + dots
            places += [(lead_side[0], start + (part - 1) * (dots + extra)) for part in others]
        gain = gain_total(places, channels // LANES, 1.0 / (rows * span * parts * lax.axis_size("dp")))
    return tuple(grad[None] for grad in result) + (gain.reshape(channels),)


def solution(mesh):
    split = P("dp", ("tm", "ulysses"), None)
    return jax.shard_map(
        local,
        mesh=mesh,
        in_specs=(split,) * 5 + (P(),),
        out_specs=(split,) * 3 + (P(),),
        check_vma=False,
    )
```

```python
import functools
import math

import jax
import jax.numpy as jnp
from jax import lax
from jax.experimental import pallas as pl
from jax.experimental.pallas import tpu as pltpu
from jax.sharding import PartitionSpec as P

HD = 128
LANES = 128
TILE_ROWS = 16
KEY_BLOCK = 768
TOTAL_BLOCK = 256
QUERY_BLOCK = 256
VMEM_LIMIT = 48 * 1024 * 1024
VMEM_WHOLE = 62 * 1024 * 1024
SCALE = 1.0 / math.sqrt(HD)
SCALE_LOG2 = SCALE / math.log(2.0)
COST = pl.CostEstimate(flops=1, bytes_accessed=1, transcendentals=0)


def params():
    return pltpu.CompilerParams(vmem_limit_bytes=VMEM_LIMIT)


def distances(parts):
    return [0] + list(range(parts - 1, 0, -1))


def column_of(parts, place, heads, head):
    partner = lax.axis_index("ulysses") ^ distances(parts)[place]
    return pl.multiple_of((partner * heads + head) * HD, HD)


def run_copies(pairs, semaphores):
    copies = [
        pltpu.make_async_copy(source, target, semaphores.at[index]) for index, (source, target) in enumerate(pairs)
    ]
    for copy in copies:
        copy.start()
    for copy in copies:
        copy.wait()


def pack_kernel(parts, chosen, *refs):
    sources, pieces, semaphores = refs[: -parts - 1], refs[-parts - 1 : -1], refs[-1]
    rows, channels = sources[0].shape
    heads = channels // (parts * HD)
    pairs = []
    for distance in range(parts):
        for half, ref in enumerate(sources):
            for place, head in enumerate(chosen):
                columns = pl.ds(column_of(parts, distance, heads, head), HD)
                start = (half * len(chosen) + place) * rows
                pairs.append((ref.at[:, columns], pieces[distance].at[start : start + rows]))
    run_copies(pairs, semaphores)


def pack(sources, parts, chosen, limit=VMEM_LIMIT):
    rows = sources[0].shape[0]
    depth = len(sources) * len(chosen) * rows
    whole = pl.BlockSpec(memory_space=pl.ANY)
    return pl.pallas_call(
        functools.partial(pack_kernel, parts, chosen),
        in_specs=[whole] * len(sources),
        out_specs=[pl.BlockSpec(memory_space=pltpu.VMEM)] * parts,
        out_shape=[jax.ShapeDtypeStruct((depth, HD), sources[0].dtype)] * parts,
        scratch_shapes=[pltpu.SemaphoreType.DMA((len(sources) * len(chosen) * parts,))],
        compiler_params=pltpu.CompilerParams(vmem_limit_bytes=limit),
        cost_estimate=COST,
    )(*sources)


def gather_kernel(ranges, *refs):
    arrays, out_ref, semaphores = refs[:-2], refs[-2], refs[-1]
    pairs = []
    place = 0
    for number, first, count in ranges:
        pairs.append((arrays[number].at[first : first + count], out_ref.at[place : place + count]))
        place += count
    run_copies(pairs, semaphores)


def gather_rows(arrays, ranges):
    whole = pl.BlockSpec(memory_space=pl.ANY)
    depth = sum(count for _, _, count in ranges)
    return pl.pallas_call(
        functools.partial(gather_kernel, ranges),
        in_specs=[whole] * len(arrays),
        out_specs=whole,
        out_shape=jax.ShapeDtypeStruct((depth, HD), arrays[0].dtype),
        scratch_shapes=[pltpu.SemaphoreType.DMA((len(ranges),))],
        compiler_params=params(),
        cost_estimate=COST,
    )(*arrays)


def dot_groups(rows):
    return -(-rows // LANES)


def dots_depth(rows, heads):
    return -(-2 * heads * dot_groups(rows) // TILE_ROWS) * TILE_ROWS


def gain_kernel(out_grad_ref, attn_ref, out_ref):
    product = out_grad_ref[...].astype(jnp.float32) * attn_ref[...].astype(jnp.float32)
    out_ref[...] = jnp.sum(product, axis=0, keepdims=True)


def gain_partial(out_grad, attn_out):
    return pl.pallas_call(
        gain_kernel,
        out_shape=jax.ShapeDtypeStruct((1, out_grad.shape[1]), jnp.float32),
        compiler_params=params(),
        cost_estimate=COST,
    )(out_grad, attn_out)


def split_terms(value, count):
    terms = []
    for _ in range(count):
        term = value.astype(jnp.bfloat16).astype(jnp.float32)
        terms.append(term)
        value = value - term
    return terms


def gain_depth(channels):
    return -(-3 * channels // LANES // TILE_ROWS) * TILE_ROWS


def pack_grads_kernel(parts, out_grad_ref, attn_ref, value_ref, gain_ref, partial_ref, *refs):
    rows, channels = out_grad_ref.shape
    heads = channels // (parts * HD)
    base = (heads + 1) * rows
    depth = base + dots_depth(rows, heads)
    partial = jnp.concatenate(split_terms(partial_ref[...], 3), axis=0)
    spare = gain_depth(channels) - partial.shape[0]
    if spare:
        partial = jnp.concatenate([partial, jnp.zeros((spare, LANES), jnp.float32)], axis=0)
    for distance in range(parts):
        terms = []
        for head in range(heads):
            columns = pl.ds(column_of(parts, distance, heads, head), HD)
            grad = (out_grad_ref[:, columns].astype(jnp.float32) * gain_ref[:, columns]).astype(jnp.bfloat16)
            place = head + 1 if head else 0
            refs[distance][place * rows : (place + 1) * rows] = grad
            if head == 0:
                refs[distance][rows : 2 * rows] = value_ref[:, columns]
            product = grad.astype(jnp.float32) * attn_ref[:, columns].astype(jnp.float32)
            dots = jnp.sum(jnp.transpose(product), axis=0, keepdims=True)
            for first in range(0, rows, LANES):
                value = dots[:, first : first + LANES]
                if value.shape[1] < LANES:
                    rest = jnp.zeros((1, LANES - value.shape[1]), jnp.float32)
                    value = jnp.concatenate([value, rest], axis=1)
                terms += split_terms(value, 2)
        rest = dots_depth(rows, heads) - len(terms)
        if rest:
            terms.append(jnp.zeros((rest, LANES), jnp.float32))
        refs[distance][base:depth] = jnp.concatenate(terms, axis=0).astype(jnp.bfloat16)
        refs[distance][depth:] = partial.astype(jnp.bfloat16)


def pack_grads(out_grad, attn_out, values, out_gain, partial, parts):
    rows, channels = out_grad.shape
    heads = channels // (parts * HD)
    depth = (heads + 1) * rows + dots_depth(rows, heads) + gain_depth(channels)
    return pl.pallas_call(
        functools.partial(pack_grads_kernel, parts),
        out_shape=[jax.ShapeDtypeStruct((depth, HD), jnp.bfloat16)] * parts,
        compiler_params=params(),
        cost_estimate=COST,
    )(out_grad, attn_out, values, out_gain.reshape(1, channels), partial)


def gain_total_kernel(lines, starts, scale, *refs):
    values = []
    for ref, start in zip(refs[:-1], starts):
        terms = [ref[start + index * lines : start + (index + 1) * lines].astype(jnp.float32) for index in range(3)]
        values.append(terms[0] + terms[1] + terms[2])
    refs[-1][...] = tree_sum(values) * scale


def gain_total(places, lines, scale):
    return pl.pallas_call(
        functools.partial(gain_total_kernel, lines, [start for _, start in places], scale),
        out_shape=jax.ShapeDtypeStruct((lines, LANES), jnp.float32),
        compiler_params=params(),
        cost_estimate=COST,
    )(*[array for array, _ in places])


def stacked(refs):
    return jnp.concatenate([ref[...] for ref in refs], axis=0)


def block_specs(depth, places):
    def block(index):
        return pl.BlockSpec((depth, HD), lambda step: (index, 0))

    return [block(index) for _, index in places], [array for array, _ in places]


def totals_kernel(parts, sources, heads, *refs):
    key_refs, refs = refs[: parts * heads], refs[parts * heads :]
    query_refs, refs = refs[: parts * heads * sources], refs[parts * heads * sources :]
    outs, score_ref = refs[:sources], refs[sources]
    slab = score_ref.shape[0]
    for head in range(heads):
        keys = stacked(key_refs[head * parts : (head + 1) * parts])
        for source in range(sources):
            start = (source * heads + head) * parts
            flip = jnp.transpose(stacked(query_refs[start : start + parts]))
            top = None
            for first in range(0, slab, TOTAL_BLOCK):
                scores = jnp.dot(keys[first : first + TOTAL_BLOCK], flip, preferred_element_type=jnp.float32)
                score_ref[first : first + TOTAL_BLOCK] = scores
                part_top = jnp.max(scores.reshape(-1, 8, slab), axis=0)
                top = part_top if top is None else jnp.maximum(top, part_top)
            top = jnp.max(top, axis=0, keepdims=True) * SCALE_LOG2
            total = None
            for first in range(0, slab, TOTAL_BLOCK):
                powers = jnp.exp2(score_ref[first : first + TOTAL_BLOCK] * SCALE_LOG2 - top)
                part_total = jnp.sum(powers.reshape(-1, 8, slab), axis=0)
                total = part_total if total is None else total + part_total
            total = jnp.sum(total, axis=0, keepdims=True)
            outs[source][head : head + 1] = top + jnp.log(total) * (1.0 / math.log(2.0))


def partial_totals(keys, queries, rows):
    heads, parts, sources = len(keys), len(keys[0]), len(queries)
    slab = parts * rows
    places = [place for head in keys for place in head]
    places += [place for source in queries for head in source for place in head]
    in_specs, operands = block_specs(rows, places)
    line = pl.BlockSpec((heads, slab), lambda step: (0, 0))
    return pl.pallas_call(
        functools.partial(totals_kernel, parts, sources, heads),
        grid=(1,),
        in_specs=in_specs,
        out_specs=[line] * sources,
        out_shape=[jax.ShapeDtypeStruct((heads, slab), jnp.float32)] * sources,
        scratch_shapes=[pltpu.VMEM((slab, slab), jnp.float32)],
        compiler_params=params(),
        cost_estimate=pl.CostEstimate(
            flops=2 * heads * sources * slab * slab * HD,
            bytes_accessed=heads * sources * slab * HD * 4,
            transcendentals=heads * sources * slab * slab,
        ),
    )(*operands)


def join_totals(values):
    top = functools.reduce(jnp.maximum, values)
    return top + jnp.log2(functools.reduce(jnp.add, [jnp.exp2(value - top) for value in values]))


def attention_kernel(parts, sources, chosen, rows, *refs):
    slab = parts * rows

    def take(count):
        nonlocal refs
        taken, refs = refs[:count], refs[count:]
        return taken

    dots_refs, total_refs = take(parts * sources), take(sources)
    inputs = [[take(parts), take(parts), take(parts * sources), take(parts * sources)] for _ in chosen]
    piece_refs, query_grad_refs = take(parts), take(sources)
    weight_ref, score_ref = refs
    for number, head in enumerate(chosen):
        keys, values, queries, grads = [stacked(held) for held in inputs[number]]
        query_flip, grad_flip = jnp.transpose(queries), jnp.transpose(grads)
        lines = []
        for ref in dots_refs:
            terms = ref[...].astype(jnp.float32)
            for index in range(dot_groups(rows)):
                line = 2 * (head * dot_groups(rows) + index)
                count = min(LANES, rows - index * LANES)
                lines.append((terms[line : line + 1] + terms[line + 1 : line + 2])[:, :count])
        dots = jnp.concatenate(lines, axis=1)
        totals = jnp.concatenate([ref[head : head + 1] for ref in total_refs], axis=1)
        base = 2 * number * rows
        for first in range(0, slab, KEY_BLOCK):
            stretch = slice(first, first + KEY_BLOCK)
            for start in range(0, sources * slab, QUERY_BLOCK):
                span = slice(start, start + QUERY_BLOCK)
                scores = jnp.dot(keys[stretch], query_flip[:, span], preferred_element_type=jnp.float32)
                weights = jnp.exp2(scores * SCALE_LOG2 - totals[:, span])
                grad_weights = jnp.dot(values[stretch], grad_flip[:, span], preferred_element_type=jnp.float32)
                weight_ref[stretch, span] = weights.astype(jnp.bfloat16)
                score_ref[stretch, span] = (weights * (grad_weights - dots[:, span])).astype(jnp.bfloat16)
            value_grad = jnp.dot(weight_ref[stretch], grads, preferred_element_type=jnp.float32)
            key_grad = jnp.dot(score_ref[stretch], queries, preferred_element_type=jnp.float32) * SCALE
            key_grad, value_grad = key_grad.astype(jnp.bfloat16), value_grad.astype(jnp.bfloat16)
            for part in range(parts):
                low, high = max(first, part * rows), min(first + KEY_BLOCK, (part + 1) * rows)
                if low < high:
                    place = base + low - part * rows
                    local_rows = slice(low - first, high - first)
                    piece_refs[part][place : place + high - low] = key_grad[local_rows]
                    piece_refs[part][place + rows : place + rows + high - low] = value_grad[local_rows]
        key_flip = jnp.transpose(keys)
        for source, ref in enumerate(query_grad_refs):
            for start in range(0, slab, QUERY_BLOCK):
                span = slice(source * slab + start, source * slab + start + QUERY_BLOCK)
                flat = jnp.dot(key_flip, score_ref[:, span], preferred_element_type=jnp.float32)
                place = number * slab + start
                ref[place : place + QUERY_BLOCK] = (jnp.transpose(flat) * SCALE).astype(ref.dtype)


def attention(chosen, heads, rows, inputs, dots, totals):
    parts = len(inputs[0][0])
    sources = len(totals)
    slab = parts * rows
    dot_specs, dot_arrays = block_specs(dots_depth(rows, heads), dots)
    in_specs, operands = block_specs(rows, [place for held in inputs for places in held for place in places])
    line = pl.BlockSpec((heads, slab), lambda step: (0, 0))
    depth = 2 * len(chosen) * rows
    out_specs, _ = block_specs(depth, [(None, 0)] * parts)
    query_specs, _ = block_specs(len(chosen) * slab, [(None, 0)] * sources)
    outs = pl.pallas_call(
        functools.partial(attention_kernel, parts, sources, chosen, rows),
        grid=(1,),
        in_specs=dot_specs + [line] * sources + in_specs,
        out_specs=out_specs + query_specs,
        out_shape=[jax.ShapeDtypeStruct((depth, HD), jnp.bfloat16)] * parts
        + [jax.ShapeDtypeStruct((len(chosen) * slab, HD), jnp.float32)]
        + [jax.ShapeDtypeStruct((len(chosen) * slab, HD), jnp.bfloat16)] * (sources - 1),
        scratch_shapes=[pltpu.VMEM((slab, sources * slab), jnp.bfloat16)] * 2,
        compiler_params=params(),
        cost_estimate=pl.CostEstimate(
            flops=10 * len(chosen) * slab * sources * slab * HD,
            bytes_accessed=32 * len(chosen) * slab * HD,
            transcendentals=len(chosen) * slab * sources * slab,
        ),
    )(*dot_arrays, *totals, *operands)
    return outs[:parts], outs[parts:]


def close_kernel(parts, rows, sources, *refs):
    terms, pieces = refs[:-parts], refs[-parts:]
    place = 0
    for first in range(0, len(terms), sources):
        for start in range(0, terms[first].shape[0], parts * rows):
            for part in range(parts):
                span = slice(start + part * rows, start + (part + 1) * rows)
                total = terms[first][span]
                for ref in terms[first + 1 : first + sources]:
                    total = total + ref[span].astype(jnp.float32)
                pieces[part][place : place + rows] = total.astype(jnp.bfloat16)
            place += rows


def close(query_grads, parts, rows):
    depth = sum(terms[0].shape[0] for terms in query_grads) // parts
    return pl.pallas_call(
        functools.partial(close_kernel, parts, rows, len(query_grads[0])),
        out_shape=[jax.ShapeDtypeStruct((depth, HD), jnp.bfloat16)] * parts,
        compiler_params=params(),
        cost_estimate=COST,
    )(*[term for terms in query_grads for term in terms])


def unpack_kernel(parts, rows, heads, stages, *refs):
    count = parts * len(stages)
    pieces, outs, semaphores = refs[:count], refs[count:-1], refs[-1]
    pairs = []
    for number, blocks in enumerate(stages):
        for distance in range(parts):
            piece = pieces[number * parts + distance]
            for index, (output, head) in enumerate(blocks):
                columns = pl.ds(column_of(parts, distance, heads, head), HD)
                pairs.append((piece.at[index * rows : (index + 1) * rows], outs[output].at[:, columns]))
    run_copies(pairs, semaphores)


def unpack(stages, pieces, rows, heads, outputs):
    parts = len(pieces[0])
    whole = pl.BlockSpec(memory_space=pl.ANY)
    channels = parts * heads * HD
    return pl.pallas_call(
        functools.partial(unpack_kernel, parts, rows, heads, stages),
        in_specs=[whole] * (parts * len(stages)),
        out_specs=[whole] * outputs,
        out_shape=[jax.ShapeDtypeStruct((rows, channels), jnp.bfloat16)] * outputs,
        scratch_shapes=[pltpu.SemaphoreType.DMA((outputs * heads * parts,))],
        compiler_params=params(),
        cost_estimate=COST,
    )(*[piece for stage in pieces for piece in stage])


def swap(value, axis, distance):
    return lax.ppermute(value, axis, [(index, index ^ distance) for index in range(lax.axis_size(axis))])


def swap_pieces(pieces, earlier=None):
    held = [pieces[0]]
    for place, distance in enumerate(distances(len(pieces))):
        if distance:
            piece = pieces[place] if earlier is None else after([pieces[place]], earlier[place])[0]
            held.append(swap(piece, "ulysses", distance))
    return held


def tree_sum(values):
    while len(values) > 1:
        values = [functools.reduce(jnp.add, values[index : index + 2]) for index in range(0, len(values), 2)]
    return values[0]


def sum_over(value, axis):
    size = lax.axis_size(axis)
    if size & (size - 1):
        return lax.psum(value, axis)
    return tree_sum([value] + [swap(value, axis, distance) for distance in range(1, size)])


def after(values, *earlier):
    return lax.optimization_barrier((list(values), earlier))[0]


def neighbours(size):
    if size == 1:
        return []
    if size == 2:
        swapped = [(0, 1), (1, 0)]
        return [(swapped, swapped)]
    up = [(index, index + 1) for index in range(size - 1)]
    down = [(index + 1, index) for index in range(size - 1)]
    return [(up, down), (down, up)]


def exchange_totals(partial, sides):
    if not sides:
        return partial
    if len(sides) == 1:
        other = lax.ppermute(jnp.concatenate(partial), "tm", sides[0][0])
        heads = partial[0].shape[0]
        return [join_totals([partial[0], other[heads:]]), join_totals([partial[1], other[:heads]])]
    position = lax.axis_index("tm")
    present = [position < lax.axis_size("tm") - 1, position > 0]
    values = [partial[0]]
    for value, (_, back), flag in zip(partial[1:], sides, present):
        values.append(jnp.where(flag, lax.ppermute(value, "tm", back), -jnp.inf))
    own = join_totals(values)
    return [own] + [lax.ppermute(own, "tm", there) for there, _ in sides]


def local(queries, keys, values, attn_out, out_grad, out_gain):
    parts = lax.axis_size("ulysses")
    span = lax.axis_size("tm")
    rows, channels = queries.shape[1:]
    heads = channels // (parts * HD)
    rest = list(range(1, heads))
    dots = dots_depth(rows, heads)
    every = list(range(parts))
    sides = neighbours(span)

    def forward(array):
        return [lax.ppermute(array, "tm", there) for there, _ in sides]

    with jax.named_scope("keys_queries"):
        packed = pack([keys[0], queries[0]], parts, list(range(heads)), VMEM_WHOLE)
        pairs = [packed[0]] + after(swap_pieces(packed)[:0:-1], [])[::-1]
    paired = span == 2
    with jax.named_scope("gain"):
        out_grad = after([out_grad], packed[0])[0]
        gain = gain_partial(out_grad[0], attn_out[0]).reshape(-1, LANES)
        gain = sum_over(gain, "dp")
        if not paired:
            gain = sum_over(gain, "tm")
    with jax.named_scope("grads"):
        sent_lead = pack_grads(out_grad[0], attn_out[0], values[0], out_gain, gain, parts)
    with jax.named_scope("halo_own_grads"):
        own_side = forward(sent_lead[0])
    with jax.named_scope("halo_queries"):
        width = heads * rows
        first_side = forward(pairs[0][width:])
    with jax.named_scope("grads"):
        lead = swap_pieces(sent_lead, pairs)
    with jax.named_scope("halo_queries"):
        late = after(pairs[1:], first_side, sent_lead[0])
        late_side = forward(gather_rows(late, [(number, width, width) for number in range(parts - 1)]))
    base = (heads + 1) * rows
    extra = gain_depth(channels)
    with jax.named_scope("totals"):
        key_places = [[(piece, head) for piece in pairs] for head in range(heads)]
        query_places = [[[(piece, heads + head) for piece in pairs] for head in range(heads)]]
        for first, others in zip(first_side, late_side):
            query_places.append(
                [
                    [(first, head)] + [(others, (part - 1) * heads + head) for part in every[1:]]
                    for head in range(heads)
                ]
            )
        part_totals = partial_totals(key_places, query_places, rows)
        totals = exchange_totals(after(part_totals, lead[1:]), sides)
    others = range(1, parts)
    with jax.named_scope("halo_first_grads"):
        ranges = [(part, 0, rows) for part in others] + [(part, base, dots + extra) for part in others]
        lead_side = forward(gather_rows(after(lead, part_totals, own_side), ranges))
    with jax.named_scope("rest_values"):
        rest_values = swap_pieces(after(pack([values[0]], parts, rest), part_totals), lead)
    dot_places = [(piece, base // dots) for piece in lead]
    for own, array in zip(own_side, lead_side):
        dot_places.append((own, base // dots))
        step = (dots + extra) // dots
        dot_places += [(array, (parts - 1) * rows // dots + (part - 1) * step) for part in others]

    def inputs_of(head):
        queries_of = [place for source in query_places for place in source[head]]
        if head == 0:
            values_of = [(piece, 1) for piece in lead]
            grads_of = [(piece, 0) for piece in lead]
            for own, array in zip(own_side, lead_side):
                grads_of += [(own, 0)] + [(array, part - 1) for part in others]
        else:
            values_of = [(piece, head - 1) for piece in rest_values]
            grads_of = [(piece, head + 1) for piece in lead]
            for own, array in zip(own_side, rest_side):
                start = (head - 1) * (parts - 1)
                grads_of += [(own, head + 1)] + [(array, start + part - 1) for part in others]
        return [key_places[head], values_of, queries_of, grads_of]

    stages, pieces, open_grads = [], [], []
    gate = rest_values
    for number, chosen in enumerate([[0], rest]):
        if number:
            with jax.named_scope("halo_rest_grads"):
                ranges = [(part, (head + 1) * rows, rows) for head in rest for part in others]
                rest_side = forward(gather_rows(after(lead, lead_side), ranges))
        with jax.named_scope("attention_%d" % number):
            inputs = [inputs_of(head) for head in chosen]
            leaving, query_grads = attention(chosen, heads, rows, inputs, dot_places, totals)
            totals = after(totals, leaving[0])
        if number:
            query_grads = after(query_grads, gate[1:], open_grads[0][1:])
        with jax.named_scope("halo_query_grads_%d" % number):
            sent_back = [lax.ppermute(other, "tm", back) for other, (_, back) in zip(query_grads[1:], sides)]
            open_grads.append(list(query_grads[:1]) + sent_back)
        with jax.named_scope("returns_%d" % number):
            gate = swap_pieces(leaving, gate)
            pieces.append(gate)
        stages.append([(output, head) for head in chosen for output in (0, 1)])
    key_grad, value_grad = unpack(stages, pieces, rows, heads, 2)
    with jax.named_scope("returns_last"):
        last = swap_pieces(close(open_grads, parts, rows), gate)
    (query_grad,) = unpack([[(0, head) for head in range(heads)]], [last], rows, heads, 1)
    result = (query_grad, key_grad, value_grad)
    with jax.named_scope("gain"):
        places = [(piece, base + dots) for piece in lead]
        if paired:
            places.append((own_side[0], base + dots))
            start = (parts - 1) * rows + dots
            places += [(lead_side[0], start + (part - 1) * (dots + extra)) for part in others]
        gain = gain_total(places, channels // LANES, 1.0 / (rows * span * parts * lax.axis_size("dp")))
    return tuple(grad[None] for grad in result) + (gain.reshape(channels),)


def solution(mesh):
    split = P("dp", ("tm", "ulysses"), None)
    return jax.shard_map(
        local,
        mesh=mesh,
        in_specs=(split,) * 5 + (P(),),
        out_specs=(split,) * 3 + (P(),),
        check_vma=False,
    )
```
